32 devices in a mesh: fsdp: 4 (over z), ctx: 4 (over y, x), tp: 2 (over core).
Axes of the slice: x: 2, y: 2, z: 4, core: 2. Of those that a mesh axis runs over, the one named last changes fastest.
Arguments:
- layer_input: bfloat16 [4, 1024, 896], P('fsdp', 'ctx'), may hold values from -6 to 6
- segments: int32 [4, 1024], P('fsdp', 'ctx'), may hold values from 0 to 2, as said below
- positions: int32 [4, 1024], P('fsdp', 'ctx'), may hold values from 0 to 2046, as said below
- attn_gain: float32 [896], replicated, may hold values from 0.5 to 1.5
- w_q: bfloat16 [896, 896], P(('fsdp', 'ctx'), 'tp'), may hold values from -0.1875 to 0.1875
- b_q: float32 [896], P('tp'), may hold values from -3 to 3
- w_k: bfloat16 [896, 128], P(('fsdp', 'ctx'), 'tp'), may hold values from -0.1875 to 0.1875
- b_k: float32 [128], P('tp'), may hold values from -3 to 3
- w_v: bfloat16 [896, 128], P(('fsdp', 'ctx'), 'tp'), may hold values from -0.1875 to 0.1875
- b_v: float32 [128], P('tp'), may hold values from -3 to 3
- w_o: bfloat16 [896, 896], P('tp', ('fsdp', 'ctx')), may hold values from -6 to 6
- mlp_gain: float32 [896], replicated, may hold values from 0.5 to 1.5
- w_gate: bfloat16 [896, 4864], P(('fsdp', 'ctx'), 'tp'), may hold values from -0.1875 to 0.1875
- w_up: bfloat16 [896, 4864], P(('fsdp', 'ctx'), 'tp'), may hold values from -0.1875 to 0.1875
- w_down: bfloat16 [4864, 896], P('tp', ('fsdp', 'ctx')), may hold values from -0.078125 to 0.078125
- cotangent: bfloat16 [4, 1024, 896], P('fsdp', 'ctx'), may hold values from -6 to 6
Outputs:
- result: bfloat16 [4, 1024, 896], P('fsdp', 'ctx')
- grad_input: bfloat16 [4, 1024, 896], P('fsdp', 'ctx')
- grad_attn_gain: float32 [896], replicated
- grad_w_q: float32 [896, 896], P(('fsdp', 'ctx'), 'tp')
- grad_b_q: float32 [896], P('tp')
- grad_w_k: float32 [896, 128], P(('fsdp', 'ctx'), 'tp')
- grad_b_k: float32 [128], P('tp')
- grad_w_v: float32 [896, 128], P(('fsdp', 'ctx'), 'tp')
- grad_b_v: float32 [128], P('tp')
- grad_w_o: float32 [896, 896], P('tp', ('fsdp', 'ctx'))
- grad_mlp_gain: float32 [896], replicated
- grad_w_gate: float32 [896, 4864], P(('fsdp', 'ctx'), 'tp')
- grad_w_up: float32 [896, 4864], P(('fsdp', 'ctx'), 'tp')
- grad_w_down: float32 [4864, 896], P('tp', ('fsdp', 'ctx'))
The draws below stay inside these ranges and needn't reach their ends.
Inputs may be any that keep to these rules, and one draw needn't show every extreme that they name: `segments`: in each row the segment numbers are 0, then 1, then 2, never falling; segment 1 begins within the first 256 positions and ends within the last 256 positions. `positions`: A token's place within its segment plus an offset of that segment.
All inputs are finite; a program needn't handle non-finite values.
Results may differ from the reference program's by a relative error of at most 0.04.
Values may be sent and summed in bfloat16 or wider, within the bound.
No kernel may reach another device: no remote copies, remote signals or barrier semaphores. Data moves between devices by JAX's collectives and lax.ppermute only.
A program may use at most 128 MiB of HBM per device.

```python
import math
from functools import partial
import jax
import jax.numpy as jnp
from jax import lax

D = 896
HEADS = 14
KV_HEADS = 2
HEAD_DIM = 64
FF = 4864
CTX_TOK = 256
ROWS = 4
ROW_LEN = 1024


def layout(key):
    first_key = jax.random.fold_in(key, 101)
    second_key = jax.random.fold_in(key, 202)
    third_key = jax.random.fold_in(key, 303)
    lower = jax.random.randint(first_key, (ROWS, 1), 1, CTX_TOK)
    upper = jax.random.randint(second_key, (ROWS, 1), ROW_LEN - CTX_TOK + 1, ROW_LEN)
    places = jnp.arange(ROW_LEN, dtype=jnp.int32)[None, :]
    numbers = (places >= lower).astype(jnp.int32) + (places >= upper).astype(jnp.int32)
    begins = jnp.where(numbers == 0, 0, jnp.where(numbers == 1, lower, upper))
    middle_offset = jax.random.randint(third_key, (ROWS, 1), 0, 1024)
    offsets = jnp.concatenate([jnp.zeros((ROWS, 1), jnp.int32), middle_offset.astype(jnp.int32), (upper + 1023).astype(jnp.int32)], axis=1)
    shifted = jnp.take_along_axis(offsets, numbers, axis=1)
    return (numbers, (places - begins + shifted).astype(jnp.int32))


def draw_segments(key, part):
    numbers, places = layout(key)
    return numbers


def draw_positions(key, part):
    numbers, places = layout(key)
    return places


def strengthened(entries, rng, source, target, parts, factor):
    def block_of(position):
        return (jnp.arange(entries.shape[position]) // (entries.shape[position] // parts)).reshape((-1,) + (1,) * (entries.ndim - 1 - position))

    first = jax.random.permutation(rng, parts)[block_of(target)]
    far = (block_of(target) + parts // 2) % parts
    return jnp.where((block_of(source) == first) | (block_of(source) == far), factor * entries, entries)


def level_of(stream_key, dims, split, low, top_value):
    def one(dim, blocks):
        heights = jax.random.uniform(jax.random.fold_in(jax.random.fold_in(stream_key, 6), dim), (blocks,), jnp.float32, low / len(split), top_value / len(split))
        return jnp.repeat(jnp.exp(heights), dims[dim] // blocks).reshape((-1,) + (1,) * (len(dims) - dim - 1))

    level = one(*split[0])
    for cut in split[1:]:
        level = level * one(*cut)
    return level


def bell_draw(stream_key, shape, spread, bound, shards=(), kind=jnp.bfloat16):
    values = jax.random.normal(stream_key, shape, jnp.float32) * spread
    if len(shards) > 0:
        values = level_of(stream_key, shape, shards, -0.22, 0.18) * values
    return jnp.clip(values, min=-bound, max=bound).astype(kind)


def noise_with(stream_key, extent, deviation, reach, split, heavy, held_as=jnp.bfloat16):
    values = deviation * jax.random.normal(stream_key, extent, jnp.float32)
    if split:
        values = values * level_of(stream_key, extent, split, -0.22, 0.18)
    return jnp.clip(strengthened(values, jax.random.fold_in(stream_key, 3), *heavy), -reach, reach).astype(held_as)


def setup_inputs(seed: int = 0) -> dict:
    key_of = jax.random.split(jax.random.key(seed), 17)
    return {
        "layer_input": bell_draw(key_of[0], (ROWS, ROW_LEN, D), 1.0, 6.0, ((0, 4), (1, 4))),
        "segments": draw_segments(jax.random.fold_in(key_of[16], 71), 0),
        "positions": draw_positions(jax.random.fold_in(key_of[16], 71), 0),
        "attn_gain": jnp.clip(1.0 + 0.1 * jax.random.normal(key_of[3], (D,), jnp.float32), 0.5, 1.5),
        "w_q": bell_draw(key_of[4], (D, HEADS * HEAD_DIM), D ** -0.5, 0.1875, ((0, 16), (1, 2))),
        "b_q": bell_draw(key_of[5], (HEADS * HEAD_DIM,), 0.5, 3.0, ((0, 2),), jnp.float32),
        "w_k": bell_draw(key_of[6], (D, KV_HEADS * HEAD_DIM), D ** -0.5, 0.1875, ((0, 16), (1, 2))),
        "b_k": bell_draw(key_of[7], (KV_HEADS * HEAD_DIM,), 0.5, 3.0, ((0, 2),), jnp.float32),
        "w_v": bell_draw(key_of[8], (D, KV_HEADS * HEAD_DIM), D ** -0.5, 0.1875, ((0, 16), (1, 2))),
        "b_v": bell_draw(key_of[9], (KV_HEADS * HEAD_DIM,), 0.5, 3.0, ((0, 2),), jnp.float32),
        "w_o": bell_draw(key_of[10], (HEADS * HEAD_DIM, D), ((ROW_LEN / (4 * HEADS * HEAD_DIM)) ** 0.5), 6.0, ((0, 2), (1, 16))),
        "mlp_gain": jnp.clip(1.0 + 0.1 * jax.random.normal(key_of[11], (D,), jnp.float32), 0.5, 1.5),
        "w_gate": bell_draw(key_of[12], (D, FF), D ** -0.5, 0.1875, ((0, 16), (1, 2))),
        "w_up": bell_draw(key_of[13], (D, FF), D ** -0.5, 0.1875, ((0, 16), (1, 2))),
        "w_down": bell_draw(key_of[14], (FF, D), FF ** -0.5, 0.078125, ((0, 2), (1, 16))),
        "cotangent": noise_with(key_of[15], (ROWS, ROW_LEN, D), 1.0, 6.0, ((0, 4), (1, 4)), (1, 2, 4, 2.0)),
    }


EPS = 1e-06
THETA = 1000000.0
NEG = -1e+30
BEST = lax.Precision.HIGHEST

@jax.custom_vjp
def low(v):
    return lax.optimization_barrier(v.astype(jnp.bfloat16)).astype(jnp.float32)

@jax.custom_vjp
def low_back(v):
    return v

def low_keep(v):
    return (low(v), None)

def low_pass(kept, grad):
    return (grad,)

def back_keep(v):
    return (v, None)

def back_low(kept, grad):
    return (low(grad),)
low.defvjp(low_keep, low_pass)
low_back.defvjp(back_keep, back_low)

def norm_rows(values, gain):
    return values * lax.rsqrt(lax.optimization_barrier(jnp.mean(values * values, -1, keepdims=True)) + EPS) * gain

def rotate(values, cosines, sines):
    halfway = values.shape[-1] // 2
    turned = jnp.concatenate([-values[..., halfway:], values[..., :halfway]], axis=-1)
    return values * cosines + turned * sines

def angles(positions):
    even_steps = jnp.arange(0, HEAD_DIM, 2).astype(jnp.float32)
    inverse = jnp.exp(-math.log(THETA) * even_steps / HEAD_DIM)
    phases = positions.astype(jnp.float32)[..., None] * inverse
    phases = jnp.concatenate([phases, phases], axis=-1)
    return (jnp.cos(phases)[..., None, :], jnp.sin(phases)[..., None, :])

def project(values, weight):
    return jnp.einsum('rld,de->rle', values, weight, precision=BEST)

def attention(query_rot, key_rot, value_rows, segments):
    group_size = HEADS // KV_HEADS
    query_width = min(512, ROW_LEN)
    blocks = ROW_LEN // query_width
    score_scale = HEAD_DIM ** (-0.5)
    query_blocks = query_rot.reshape(ROWS * blocks, query_width, KV_HEADS, group_size, HEAD_DIM)
    seg_blocks = segments.reshape(ROWS * blocks, query_width)
    row_ids = jnp.arange(ROWS * blocks, dtype=jnp.int32) // blocks
    starts = jnp.arange(ROWS * blocks, dtype=jnp.int32) % blocks * query_width
    key_index = jnp.arange(ROW_LEN, dtype=jnp.int32)

    def one_block(packed):
        queries, seg_query, row_id, start_at = packed
        keys_row = lax.dynamic_index_in_dim(key_rot, row_id, 0, keepdims=False)
        values_row = lax.dynamic_index_in_dim(value_rows, row_id, 0, keepdims=False)
        seg_keys = lax.dynamic_index_in_dim(segments, row_id, 0, keepdims=False)
        logits = low_back(jnp.einsum('qgjd,kgd->gjqk', queries, keys_row, precision=BEST) * score_scale)
        query_index = start_at + jnp.arange(query_width, dtype=jnp.int32)
        allowed = (seg_keys[None, :] == seg_query[:, None]) & (key_index[None, :] <= query_index[:, None])
        masked = jnp.where(allowed, logits, NEG)
        row_peak = lax.optimization_barrier(jnp.max(masked, -1, keepdims=True))
        raised = jnp.exp(masked - row_peak)
        probabilities = low(raised / lax.optimization_barrier(jnp.sum(raised, -1, keepdims=True)))
        mixed = jnp.einsum('gjqk,kgd->qgjd', probabilities, values_row, precision=BEST)
        return mixed.reshape(query_width, HEADS * HEAD_DIM)
    outputs = lax.map(jax.checkpoint(one_block), (query_blocks, seg_blocks, row_ids, starts))
    return outputs.reshape(ROWS, ROW_LEN, HEADS * HEAD_DIM)

def layer(segments, cosines, sines, inputs, attn_gain, w_q, b_q, w_k, b_k, w_v, b_v, w_o, mlp_gain, w_gate, w_up, w_down):
    normed = low(norm_rows(inputs, attn_gain))
    queries = low_back(project(normed, w_q) + b_q)
    keyproj = low_back(project(normed, w_k) + b_k)
    valproj = low(low_back(project(normed, w_v) + b_v))
    query_rot = low(rotate(queries.reshape(ROWS, ROW_LEN, HEADS, HEAD_DIM), cosines, sines))
    key_rot = low(rotate(keyproj.reshape(ROWS, ROW_LEN, KV_HEADS, HEAD_DIM), cosines, sines))
    value_rows = valproj.reshape(ROWS, ROW_LEN, KV_HEADS, HEAD_DIM)
    attended = low(low_back(attention(query_rot, key_rot, value_rows, segments)))
    middle = inputs + low_back(project(attended, w_o))
    normed_two = low(norm_rows(middle, mlp_gain))
    gate_values = low_back(project(normed_two, w_gate))
    upward = low_back(project(normed_two, w_up))
    hidden = low(jax.nn.silu(gate_values) * upward)
    return middle + low_back(project(hidden, w_down))

def reference(layer_input, segments, positions, attn_gain, w_q, b_q, w_k, b_k, w_v, b_v, w_o, mlp_gain, w_gate, w_up, w_down, cotangent):
    cosines, sines = angles(positions)
    floats = tuple((member.astype(jnp.float32) for member in (layer_input, attn_gain, w_q, b_q, w_k, b_k, w_v, b_v, w_o, mlp_gain, w_gate, w_up, w_down)))
    result, pullback = jax.vjp(partial(layer, segments, cosines, sines), *floats)
    grads = pullback(cotangent.astype(jnp.float32))
    return (result.astype(jnp.bfloat16), grads[0].astype(jnp.bfloat16), grads[1], grads[2], grads[3], grads[4], grads[5], grads[6], grads[7], grads[8], grads[9], grads[10], grads[11], grads[12])
```

```python
import math

import jax
import jax.numpy as jnp
from jax import lax
from jax.sharding import PartitionSpec as P

HEAD_DIM = 64


EPS = 1e-06
THETA = 1000000.0
NEG = -1e30


def rotate(values, cosines, sines):
    halfway = values.shape[-1] // 2
    turned = jnp.concatenate([-values[..., halfway:], values[..., :halfway]], axis=-1)
    return values * cosines + turned * sines


def angles(positions, head_dim):
    even_steps = jnp.arange(0, head_dim, 2).astype(jnp.float32)
    inverse = jnp.exp(-math.log(THETA) * even_steps / head_dim)
    phases = positions.astype(jnp.float32)[..., None] * inverse
    phases = jnp.concatenate([phases, phases], axis=-1)
    return (jnp.cos(phases)[..., None, :], jnp.sin(phases)[..., None, :])


LANES = 128


def flips(size, step):
    return [(index, index ^ step) for index in range(size)]


def swap_cores(values):
    return lax.ppermute(values, "tp", flips(lax.axis_size("tp"), 1))


def few():
    return lax.axis_size("ctx") <= 8


def peers():
    size = lax.axis_size("ctx")
    if few():
        return [lax.axis_index("ctx") ^ step for step in range(size)]
    return list(range(size))


def spread(values):
    size = lax.axis_size("ctx")
    if not few():
        return list(lax.all_gather(values, "ctx"))
    return [values] + [lax.ppermute(values, "ctx", flips(size, step)) for step in range(1, size)]


def trade(parts):
    size = lax.axis_size("ctx")
    if not few():
        return list(lax.all_to_all(jnp.stack(parts), "ctx", 0, 0))
    return [parts[0]] + [
        lax.ppermute(parts[step], "ctx", flips(size, step)) for step in range(1, size)
    ]


def untangle(parts):
    if not few():
        return jnp.stack(parts)
    own = lax.axis_index("ctx")
    whole = jnp.stack(parts)
    return jnp.stack(
        [lax.dynamic_index_in_dim(whole, own ^ place, 0, keepdims=False) for place in range(len(parts))]
    )


def choose(whole):
    if not few():
        return list(whole)
    return [lax.dynamic_index_in_dim(whole, peer, 0, keepdims=False) for peer in peers()]


def chain_gather(values):
    size = lax.axis_size("fsdp")
    ups = [(index, index + 1) for index in range(size - 1)]
    downs = [(index + 1, index) for index in range(size - 1)]
    below, above = [], []
    rising = falling = values
    for step in range(size - 1):
        rising = lax.ppermute(rising, "fsdp", ups[step:])
        falling = lax.ppermute(falling, "fsdp", downs[: size - 1 - step])
        below.insert(0, rising)
        above.append(falling)
    line = jnp.stack(below + [values] + above)
    return lax.dynamic_slice_in_dim(line, size - 1 - lax.axis_index("fsdp"), size, 0)


def chain_scatter(whole):
    size = lax.axis_size("fsdp")
    own = lax.axis_index("fsdp")
    ups = [(index, index + 1) for index in range(size - 1)]
    downs = [(index + 1, index) for index in range(size - 1)]

    def pick(place):
        return lax.dynamic_index_in_dim(whole, place, 0, keepdims=False)

    rising = falling = None
    for step in range(1, size):
        up_piece, down_piece = pick(own + size - step), pick(own - size + step)
        if rising is not None:
            up_piece, down_piece = up_piece + rising, down_piece + falling
        rising = lax.ppermute(up_piece, "fsdp", ups[:step])
        falling = lax.ppermute(down_piece, "fsdp", downs[size - 1 - step :])
    return (
        pick(own).astype(jnp.float32) + rising.astype(jnp.float32) + falling.astype(jnp.float32)
    )


def gather_tokens(values):
    half = values.shape[0] // 2
    own = lax.dynamic_slice_in_dim(values, lax.axis_index("tp") * half, half, 0)
    mine = jnp.concatenate(spread(own))
    return jnp.concatenate([mine, swap_cores(mine)])


def scatter_tokens(partial):
    middle = partial.shape[0] // 2
    size = lax.axis_size("ctx")
    summed = (
        partial[:middle].astype(jnp.float32) + swap_cores(partial[middle:]).astype(jnp.float32)
    ).astype(jnp.bfloat16)
    own = sum(part.astype(jnp.float32) for part in trade(jnp.split(summed, size)))
    own = own.astype(jnp.bfloat16)
    other = swap_cores(own)
    first = lax.axis_index("tp") == 0
    return jnp.where(
        first, jnp.concatenate([own, other]), jnp.concatenate([other, own])
    ).astype(jnp.float32)


def total_small(values):
    for axis in ("ctx", "fsdp"):
        size = lax.axis_size(axis)
        step = 1
        while step < size:
            values = values + lax.ppermute(values, axis, flips(size, step))
            step *= 2
    return values


def score_block(query_groups, key_rows, seg_keys, key_index, seg_own, query_index):
    head_dim = query_groups.shape[-1]
    logits = jnp.einsum(
        "qgjd,kgd->gjqk", query_groups, key_rows, preferred_element_type=jnp.float32
    ) * head_dim ** (-0.5)
    allowed = (seg_keys[None, :] == seg_own[:, None]) & (key_index[None, :] <= query_index[:, None])
    return jnp.where(allowed, logits, NEG)


def key_window(keyval_all, seg_all, index_all, number, key_block, key_heads):
    window = lax.dynamic_slice_in_dim(keyval_all, number * key_block, key_block, 0)
    width = window.shape[1] // 2
    key_rows = window[:, :width].reshape(key_block, key_heads, width // key_heads)
    value_rows = window[:, width:].reshape(key_block, key_heads, width // key_heads)
    seg_keys = lax.dynamic_slice_in_dim(seg_all, number * key_block, key_block, 0)
    key_index = lax.dynamic_slice_in_dim(index_all, number * key_block, key_block, 0)
    return key_rows, value_rows, seg_keys, key_index


def repeat(count, step, state):
    if count == 1:
        return step(0, state)
    return lax.fori_loop(0, count, step, state)


def attend(query_rot, keyval_all, seg_all, index_all, seg_own, query_index, key_heads):
    tokens, head_count, head_dim = query_rot.shape
    group_size = head_count // key_heads
    key_block = min(keyval_all.shape[0], 1024)
    query_groups = query_rot.reshape(tokens, key_heads, group_size, head_dim)
    block_count = keyval_all.shape[0] // key_block

    def measure(number, state_pair):
        running_peak, running_total = state_pair
        key_rows, value_rows, seg_keys, key_index = key_window(
            keyval_all, seg_all, index_all, number, key_block, key_heads
        )
        masked = score_block(query_groups, key_rows, seg_keys, key_index, seg_own, query_index)
        fresh = jnp.maximum(running_peak, jnp.max(masked, -1))
        running_total = running_total * jnp.exp(running_peak - fresh) + jnp.sum(
            jnp.exp(masked - fresh[..., None]), -1
        )
        return (fresh, running_total)

    start_state = (
        jnp.full((key_heads, group_size, tokens), NEG, jnp.float32),
        jnp.zeros((key_heads, group_size, tokens), jnp.float32),
    )
    running_peak, running_total = repeat(block_count, measure, start_state)
    log_total = running_peak + jnp.log(running_total)

    def collect(number, summed):
        key_rows, value_rows, seg_keys, key_index = key_window(
            keyval_all, seg_all, index_all, number, key_block, key_heads
        )
        masked = score_block(query_groups, key_rows, seg_keys, key_index, seg_own, query_index)
        chances = jnp.exp(masked - log_total[..., None]).astype(jnp.bfloat16)
        return summed + jnp.einsum(
            "gjqk,kgd->gjqd", chances, value_rows, preferred_element_type=jnp.float32
        )

    summed = repeat(
        block_count, collect, jnp.zeros((key_heads, group_size, tokens, head_dim), jnp.float32)
    )
    return (summed.transpose(2, 0, 1, 3).reshape(tokens, head_count * head_dim), log_total)


def attend_back(
    query_rot,
    keyval_all,
    seg_all,
    index_all,
    seg_own,
    query_index,
    key_heads,
    log_total,
    attended,
    grad_attended,
):
    tokens, head_count, head_dim = query_rot.shape
    group_size = head_count // key_heads
    key_block = min(keyval_all.shape[0], 1024)
    query_groups = query_rot.reshape(tokens, key_heads, group_size, head_dim)
    grad_groups = grad_attended.reshape(tokens, key_heads, group_size, head_dim)
    block_count = keyval_all.shape[0] // key_block
    row_dot = jnp.sum(
        (grad_attended.astype(jnp.float32) * attended).reshape(
            tokens, key_heads, group_size, head_dim
        ),
        -1,
    ).transpose(1, 2, 0)
    score_scale = head_dim ** (-0.5)

    def step_back(number, state_pair):
        grad_query, grad_keyval = state_pair
        key_rows, value_rows, seg_keys, key_index = key_window(
            keyval_all, seg_all, index_all, number, key_block, key_heads
        )
        masked = score_block(query_groups, key_rows, seg_keys, key_index, seg_own, query_index)
        chances = jnp.exp(masked - log_total[..., None])
        chances_low = chances.astype(jnp.bfloat16)
        grad_chances = jnp.einsum(
            "qgjd,kgd->gjqk", grad_groups, value_rows, preferred_element_type=jnp.float32
        )
        grad_logits = (chances * (grad_chances - row_dot[..., None])).astype(jnp.bfloat16)
        grad_query = (
            grad_query
            + jnp.einsum(
                "gjqk,kgd->gjqd", grad_logits, key_rows, preferred_element_type=jnp.float32
            )
            * score_scale
        )
        grad_keys = (
            jnp.einsum(
                "gjqk,qgjd->kgd", grad_logits, query_groups, preferred_element_type=jnp.float32
            )
            * score_scale
        )
        grad_values = jnp.einsum(
            "gjqk,qgjd->kgd", chances_low, grad_groups, preferred_element_type=jnp.float32
        )
        grad_piece = jnp.concatenate(
            [
                grad_keys.reshape(key_block, key_heads * head_dim),
                grad_values.reshape(key_block, key_heads * head_dim),
            ],
            axis=-1,
        ).astype(jnp.bfloat16)
        grad_keyval = lax.dynamic_update_slice_in_dim(
            grad_keyval, grad_piece, number * key_block, 0
        )
        return (grad_query, grad_keyval)

    start_state = (
        jnp.zeros((key_heads, group_size, tokens, head_dim), jnp.float32),
        jnp.zeros(keyval_all.shape, jnp.bfloat16),
    )
    grad_query, grad_keyval = repeat(block_count, step_back, start_state)
    return (grad_query.transpose(2, 0, 1, 3).reshape(tokens, head_count, head_dim), grad_keyval)


def body(
    layer_input,
    segments,
    positions,
    attn_gain,
    w_q,
    b_q,
    w_k,
    b_k,
    w_v,
    b_v,
    w_o,
    mlp_gain,
    w_gate,
    w_up,
    w_down,
    cotangent,
):
    key_heads = w_k.shape[1] // HEAD_DIM
    head_count = w_q.shape[1] // HEAD_DIM
    width_q, width_k = w_q.shape[1], w_k.shape[1]
    tokens = layer_input.shape[1]
    ctx_size, fsdp_size = lax.axis_size("ctx"), lax.axis_size("fsdp")
    ctx_own = lax.axis_index("ctx")
    rows, hidden_count = w_gate.shape
    features = layer_input.shape[2]
    chunk = -(-hidden_count // (ctx_size * LANES)) * LANES
    tail = ((0, 0), (0, chunk * ctx_size - hidden_count))

    def whole_rows(shard):
        lined = chain_gather(shard)
        pieces = untangle(spread(lined))
        return pieces.transpose(1, 0, 2, 3).reshape(features, shard.shape[1])

    full_qkv = whole_rows(jnp.concatenate([w_q, w_k, w_v], axis=1))
    full_o_turned = whole_rows(w_o.T)

    gate_cut = jnp.pad(w_gate, tail).reshape(rows, ctx_size, chunk)
    up_cut = jnp.pad(w_up, tail).reshape(rows, ctx_size, chunk)
    down_cut = jnp.pad(w_down.T, tail).reshape(rows, ctx_size, chunk)
    gate_up_cut = jnp.concatenate([gate_cut, up_cut], axis=-1).transpose(1, 0, 2)
    down_cut = down_cut.transpose(1, 0, 2)

    def chunk_rows(cut):
        recut = untangle(trade(choose(cut)))
        return chain_gather(recut).reshape(features, cut.shape[-1])

    gate_up = chunk_rows(gate_up_cut)
    down_turned = chunk_rows(down_cut)

    inputs = layer_input[0].astype(jnp.float32)
    seg_own = segments[0]
    place = jnp.arange(tokens, dtype=jnp.int32)
    query_index = ctx_own * tokens + place
    index_all = jnp.concatenate([peer * tokens + place for peer in peers()])
    seg_all = jnp.concatenate(spread(seg_own))
    grad_top = cotangent[0]
    grad_top_all = gather_tokens(grad_top)
    cosines, sines = angles(positions[0], HEAD_DIM)
    scale_one = lax.rsqrt(jnp.mean(inputs * inputs, -1, keepdims=True) + EPS)
    unit_one = inputs * scale_one
    normed = (unit_one * attn_gain).astype(jnp.bfloat16)
    projected = jnp.dot(normed, full_qkv, preferred_element_type=jnp.float32) + jnp.concatenate(
        [b_q, b_k, b_v]
    )
    queries = projected[:, :width_q]
    keyproj = projected[:, width_q : width_q + width_k]
    valproj = projected[:, width_q + width_k :]
    query_rot = rotate(queries.reshape(tokens, head_count, HEAD_DIM), cosines, sines).astype(
        jnp.bfloat16
    )
    key_rot = rotate(keyproj.reshape(tokens, key_heads, HEAD_DIM), cosines, sines).astype(
        jnp.bfloat16
    )
    keyval = jnp.concatenate(
        [key_rot.reshape(tokens, key_heads * HEAD_DIM), valproj.astype(jnp.bfloat16)], axis=-1
    )
    keyval_all = jnp.concatenate(spread(keyval))
    attended, log_total = attend(
        query_rot, keyval_all, seg_all, index_all, seg_own, query_index, key_heads
    )
    attended_low = attended.astype(jnp.bfloat16)
    branch_part = lax.dot_general(
        attended_low, full_o_turned, (((1,), (1,)), ((), ())), preferred_element_type=jnp.float32
    ).astype(jnp.bfloat16)
    middle = inputs + (
        branch_part.astype(jnp.float32) + swap_cores(branch_part).astype(jnp.float32)
    )
    scale_two = lax.rsqrt(jnp.mean(middle * middle, -1, keepdims=True) + EPS)
    unit_two = middle * scale_two
    normed_two = (unit_two * mlp_gain).astype(jnp.bfloat16)

    normed_all = gather_tokens(normed_two)
    gate_upward = jnp.dot(normed_all, gate_up, preferred_element_type=jnp.float32)
    grad_hidden = jnp.dot(grad_top_all, down_turned, preferred_element_type=jnp.float32)
    gate_values, upward = gate_upward[:, :chunk], gate_upward[:, chunk:]
    sigmoid_gate = jax.nn.sigmoid(gate_values)
    swish_gate = gate_values * sigmoid_gate
    hidden = (swish_gate * upward).astype(jnp.bfloat16)
    grad_gate = (
        grad_hidden * upward * sigmoid_gate * (1.0 + gate_values * (1.0 - sigmoid_gate))
    ).astype(jnp.bfloat16)
    grad_upward = (grad_hidden * swish_gate).astype(jnp.bfloat16)
    grad_both = jnp.concatenate([grad_gate, grad_upward], axis=-1)
    grad_normed_two = scatter_tokens(
        lax.dot_general(
            grad_both, gate_up, (((1,), (1,)), ((), ())), preferred_element_type=jnp.float32
        ).astype(jnp.bfloat16)
    )
    branch_two = scatter_tokens(
        lax.dot_general(
            hidden, down_turned, (((1,), (1,)), ((), ())), preferred_element_type=jnp.float32
        ).astype(jnp.bfloat16)
    )
    result = (middle + branch_two).astype(jnp.bfloat16)

    def owners_chunks(grad_chunk):
        width = grad_chunk.shape[-1]
        summed = chain_scatter(
            grad_chunk.astype(jnp.bfloat16).reshape(fsdp_size, ctx_size * rows, width)
        ).astype(jnp.bfloat16)
        pieces = untangle(trade(choose(summed.reshape(ctx_size, rows, width))))
        return pieces.transpose(1, 0, 2)

    def drop_tail(pieces):
        return pieces.reshape(rows, chunk * ctx_size)[:, :hidden_count].astype(jnp.float32)

    def turned_dot(left, right):
        return lax.dot_general(
            left, right, (((0,), (0,)), ((), ())), preferred_element_type=jnp.float32
        )

    grad_down_turned = drop_tail(owners_chunks(turned_dot(grad_top_all, hidden)))
    grad_gate_up = owners_chunks(turned_dot(normed_all, grad_both))
    grad_gate_w = drop_tail(grad_gate_up[..., :chunk])
    grad_up_w = drop_tail(grad_gate_up[..., chunk:])

    grad_mlp_gain = jnp.sum(grad_normed_two * unit_two, 0)
    grad_unit_two = grad_normed_two * mlp_gain
    grad_middle = grad_top.astype(jnp.float32) + scale_two * (
        grad_unit_two - unit_two * jnp.mean(grad_unit_two * unit_two, -1, keepdims=True)
    )
    grad_branch = grad_middle.astype(jnp.bfloat16)

    def owners_rows(grad_rows):
        width = grad_rows.shape[-1]
        cut = grad_rows.astype(jnp.bfloat16).reshape(fsdp_size, ctx_size, rows, width)
        mine = trade(choose(cut.transpose(1, 0, 2, 3)))
        summed = sum(part.astype(jnp.float32) for part in mine).astype(jnp.bfloat16)
        return chain_scatter(summed)

    grad_o_turned = owners_rows(turned_dot(grad_branch, attended_low))
    grad_attended = jnp.dot(
        grad_branch, full_o_turned, preferred_element_type=jnp.float32
    ).astype(jnp.bfloat16)
    grad_query_rot, grad_keyval_all = attend_back(
        query_rot,
        keyval_all,
        seg_all,
        index_all,
        seg_own,
        query_index,
        key_heads,
        log_total,
        attended,
        grad_attended,
    )
    grad_keyval = sum(
        part.astype(jnp.float32) for part in trade(jnp.split(grad_keyval_all, ctx_size))
    )
    grad_query = (
        rotate(grad_query_rot, cosines, -sines)
        .reshape(tokens, head_count * HEAD_DIM)
        .astype(jnp.bfloat16)
    )
    grad_key = (
        rotate(
            grad_keyval[:, : key_heads * HEAD_DIM].reshape(tokens, key_heads, HEAD_DIM),
            cosines,
            -sines,
        )
        .reshape(tokens, key_heads * HEAD_DIM)
        .astype(jnp.bfloat16)
    )
    grad_value = grad_keyval[:, key_heads * HEAD_DIM :].astype(jnp.bfloat16)
    grad_qkv = jnp.concatenate([grad_query, grad_key, grad_value], axis=-1)
    grad_normed_part = lax.dot_general(
        grad_qkv, full_qkv, (((1,), (1,)), ((), ())), preferred_element_type=jnp.float32
    ).astype(jnp.bfloat16)
    grad_normed = grad_normed_part.astype(jnp.float32) + swap_cores(grad_normed_part).astype(
        jnp.float32
    )
    grad_attn_gain = jnp.sum(grad_normed * unit_one, 0)
    grad_unit_one = grad_normed * attn_gain
    grad_inputs = grad_middle + scale_one * (
        grad_unit_one - unit_one * jnp.mean(grad_unit_one * unit_one, -1, keepdims=True)
    )
    grad_qkv_w = owners_rows(turned_dot(normed, grad_qkv))
    small = total_small(
        jnp.concatenate(
            [jnp.sum(grad_qkv.astype(jnp.float32), 0), grad_attn_gain, grad_mlp_gain]
        )
    )
    edges = [width_q, width_q + width_k, width_q + 2 * width_k, width_q + 2 * width_k + features]
    grad_b_q, grad_b_k, grad_b_v, grad_attn_gain, grad_mlp_gain = jnp.split(small, edges)
    return (
        result[None],
        grad_inputs.astype(jnp.bfloat16)[None],
        grad_attn_gain,
        grad_qkv_w[:, :width_q],
        grad_b_q,
        grad_qkv_w[:, width_q : width_q + width_k],
        grad_b_k,
        grad_qkv_w[:, width_q + width_k :],
        grad_b_v,
        grad_o_turned.T,
        grad_mlp_gain,
        grad_gate_w,
        grad_up_w,
        grad_down_turned.T,
    )


def solution(mesh):
    placed = (
        P("fsdp", "ctx", None),
        P("fsdp", "ctx"),
        P("fsdp", "ctx"),
        P(),
        P(("fsdp", "ctx"), "tp"),
        P("tp"),
        P(("fsdp", "ctx"), "tp"),
        P("tp"),
        P(("fsdp", "ctx"), "tp"),
        P("tp"),
        P("tp", ("fsdp", "ctx")),
        P(),
        P(("fsdp", "ctx"), "tp"),
        P(("fsdp", "ctx"), "tp"),
        P("tp", ("fsdp", "ctx")),
        P("fsdp", "ctx", None),
    )
    return jax.shard_map(
        body,
        mesh=mesh,
        in_specs=placed,
        out_specs=(
            P("fsdp", "ctx", None),
            P("fsdp", "ctx", None),
            P(),
            P(("fsdp", "ctx"), "tp"),
            P("tp"),
            P(("fsdp", "ctx"), "tp"),
            P("tp"),
            P(("fsdp", "ctx"), "tp"),
            P("tp"),
            P("tp", ("fsdp", "ctx")),
            P(),
            P(("fsdp", "ctx"), "tp"),
            P(("fsdp", "ctx"), "tp"),
            P("tp", ("fsdp", "ctx")),
        ),
        check_vma=False,
    )
```

```python
import functools
import math

import jax
import jax.numpy as jnp
from jax import lax
from jax.experimental import pallas as pl
from jax.experimental.pallas import tpu as pltpu
from jax.sharding import PartitionSpec as P

HEAD_DIM = 64


EPS = 1e-06
THETA = 1000000.0
NEG = -1e30

LANES = 128
SPLIT = 512
SMALL_ROWS = 16
VMEM_BYTES = 48 * 2**20
FREE = pl.CostEstimate(flops=0, bytes_accessed=0, transcendentals=0)
IN_VMEM = pl.BlockSpec(memory_space=pltpu.VMEM)
IN_SMEM = pl.BlockSpec(memory_space=pltpu.SMEM)
F32 = jnp.float32
BF = jnp.bfloat16


def dot(left, right):
    return jnp.dot(left, right, preferred_element_type=F32)


def dot_rows(left, right):
    return lax.dot_general(left, right, (((1,), (1,)), ((), ())), preferred_element_type=F32)


def turned_dot(left, right):
    return lax.dot_general(left, right, (((0,), (0,)), ((), ())), preferred_element_type=F32)


def rotate(values, cosines, sines):
    halfway = values.shape[-1] // 2
    turned = jnp.concatenate([-values[..., halfway:], values[..., :halfway]], axis=-1)
    return values * cosines + turned * sines


def angles(positions, head_dim):
    even_steps = jnp.arange(0, head_dim, 2).astype(jnp.float32)
    inverse = jnp.exp(-math.log(THETA) * even_steps / head_dim)
    phases = positions.astype(jnp.float32)[..., None] * inverse
    phases = jnp.concatenate([phases, phases], axis=-1)
    return (jnp.cos(phases)[..., None, :], jnp.sin(phases)[..., None, :])


def flips(size, step):
    return [(index, index ^ step) for index in range(size)]


def swap_cores(values):
    return lax.ppermute(values, "tp", flips(lax.axis_size("tp"), 1))


def few():
    return lax.axis_size("ctx") <= 8


def peers():
    size = lax.axis_size("ctx")
    if few():
        return [lax.axis_index("ctx") ^ step for step in range(size)]
    return list(range(size))


def spread(values):
    size = lax.axis_size("ctx")
    if not few():
        return list(lax.all_gather(values, "ctx"))
    return [values] + [lax.ppermute(values, "ctx", flips(size, step)) for step in range(1, size)]


def trade(parts):
    size = lax.axis_size("ctx")
    if not few():
        return list(lax.all_to_all(jnp.stack(parts), "ctx", 0, 0))
    return [parts[0]] + [
        lax.ppermute(parts[step], "ctx", flips(size, step)) for step in range(1, size)
    ]


def untangle(parts):
    if not few():
        return jnp.stack(parts)
    own = lax.axis_index("ctx")
    whole = jnp.stack(parts)
    return jnp.stack(
        [lax.dynamic_index_in_dim(whole, own ^ place, 0, keepdims=False) for place in range(len(parts))]
    )


def choose(whole):
    if not few():
        return list(whole)
    return [lax.dynamic_index_in_dim(whole, peer, 0, keepdims=False) for peer in peers()]


def after(values, *earlier):
    return lax.optimization_barrier((values,) + earlier)[0]


def direct_gather(values):
    size = lax.axis_size("fsdp")
    own = lax.axis_index("fsdp")
    pieces = [values] + [
        lax.ppermute(values, "fsdp", [(index, (index + step) % size) for index in range(size)])
        for step in range(1, size)
    ]
    pieces = pieces[::-1]
    line = jnp.stack(pieces + pieces[:-1])
    return lax.dynamic_slice_in_dim(line, size - 1 - own, size, 0)


def send_up(values, step):
    size = lax.axis_size("fsdp")
    return lax.ppermute(values, "fsdp", [(index, (index + step) % size) for index in range(size)])


def line_steps():
    size = lax.axis_size("fsdp")
    ups = [(index, index + 1) for index in range(size - 1)]
    downs = [(index + 1, index) for index in range(size - 1)]
    return ups, downs


def gather_step(line, step):
    ups, downs = line_steps()
    return (
        [lax.ppermute(line[0], "fsdp", ups[step:])]
        + line
        + [lax.ppermute(line[-1], "fsdp", downs[: len(downs) - step])]
    )


def gather_end(line):
    size = lax.axis_size("fsdp")
    return lax.dynamic_slice_in_dim(
        jnp.stack(line), size - 1 - lax.axis_index("fsdp"), size, 0
    )


def scatter_step(whole, sums, step):
    size = lax.axis_size("fsdp")
    own = lax.axis_index("fsdp")
    ups, downs = line_steps()
    pieces = [
        lax.dynamic_index_in_dim(whole, place, 0, keepdims=False)
        for place in (own + size - step, own - size + step)
    ]
    if sums:
        pieces = [piece + part for piece, part in zip(pieces, sums)]
    return [
        lax.ppermute(pieces[0], "fsdp", ups[:step]),
        lax.ppermute(pieces[1], "fsdp", downs[size - 1 - step :]),
    ]


def scatter_end(whole, sums):
    own = lax.dynamic_index_in_dim(whole, lax.axis_index("fsdp"), 0, keepdims=False)
    return sum(part.astype(F32) for part in [own] + sums)


def gather_half(values):
    half = values.shape[0] // 2
    return jnp.concatenate(
        spread(lax.dynamic_slice_in_dim(values, lax.axis_index("tp") * half, half, 0))
    )


def both_halves(mine):
    return jnp.concatenate([mine, swap_cores(mine)])


def add_cores(partial):
    middle = partial.shape[0] // 2
    return (
        partial[:middle].astype(jnp.float32) + swap_cores(partial[middle:]).astype(jnp.float32)
    ).astype(jnp.bfloat16)


def join_tokens(parts):
    own = sum(part.astype(jnp.float32) for part in parts).astype(jnp.bfloat16)
    other = swap_cores(own)
    first = lax.axis_index("tp") == 0
    return jnp.where(
        first, jnp.concatenate([own, other]), jnp.concatenate([other, own])
    ).astype(jnp.float32)


def turn_back(values, cosines, sines, sign):
    half = cosines.shape[0]
    parts = []
    for begin in range(0, values.shape[0], 2 * half):
        first = values[begin : begin + half]
        second = values[begin + half : begin + 2 * half]
        parts += [first * cosines - second * (sign * sines), second * cosines + first * (sign * sines)]
    return jnp.concatenate(parts)


def project_kernel(width_q, width_k, input_ref, gain_ref, w_ref, b_ref, cos_ref, sin_ref, q_ref, kv_ref):
    inputs = input_ref[...].astype(F32)
    scale = lax.rsqrt(jnp.mean(inputs * inputs, -1, keepdims=True) + EPS)
    normed = (inputs * scale * gain_ref[...]).astype(BF)
    projected = dot(normed, w_ref[...]) + b_ref[...]
    rotated = turn_back(projected[:, : width_q + width_k].T, cos_ref[...], sin_ref[...], 1.0).T
    q_ref[...] = rotated[:, :width_q].astype(BF)
    kv_ref[:, :width_k] = rotated[:, width_q:].astype(BF)
    kv_ref[:, width_k:] = projected[:, width_q + width_k :].astype(BF)


def project(inputs, gain, weights, biases, cosines, sines, width_q, width_k):
    tokens = inputs.shape[0]
    return pl.pallas_call(
        functools.partial(project_kernel, width_q, width_k),
        out_shape=(
            jax.ShapeDtypeStruct((tokens, width_q), BF),
            jax.ShapeDtypeStruct((tokens, 2 * width_k), BF),
        ),
        in_specs=[IN_VMEM] * 6,
        out_specs=(IN_VMEM,) * 2,
        compiler_params=pltpu.CompilerParams(vmem_limit_bytes=VMEM_BYTES),
        cost_estimate=FREE,
        name="project",
    )(inputs, gain, weights, biases, cosines, sines)


def key_grads_kernel(count, q_ref, w_ref, cos_ref, sin_ref, *refs):
    parts, qkv_ref, normed_ref = refs[:count], refs[count], refs[count + 1]
    width_q = q_ref.shape[1]
    total = sum(ref[...].astype(F32) for ref in parts)
    width_k = total.shape[1] // 2
    keys = turn_back(total[:, :width_k].T, cos_ref[...], sin_ref[...], -1.0).T
    qkv_ref[:, :width_q] = q_ref[...]
    qkv_ref[:, width_q : width_q + width_k] = keys.astype(BF)
    qkv_ref[:, width_q + width_k :] = total[:, width_k:].astype(BF)
    normed_ref[...] = dot_rows(qkv_ref[...], w_ref[...]).astype(BF)


def key_grads(grad_query, weights, cosines, sines, parts):
    tokens = grad_query.shape[0]
    features, width = weights.shape
    return pl.pallas_call(
        functools.partial(key_grads_kernel, len(parts)),
        out_shape=(
            jax.ShapeDtypeStruct((tokens, width), BF),
            jax.ShapeDtypeStruct((tokens, features), BF),
        ),
        in_specs=[IN_VMEM] * (4 + len(parts)),
        out_specs=(IN_VMEM,) * 2,
        compiler_params=pltpu.CompilerParams(vmem_limit_bytes=VMEM_BYTES),
        cost_estimate=FREE,
        name="key_grads",
    )(grad_query, weights, cosines, sines, *parts)


def masks(start, tokens, own, step):
    peer = own ^ step
    key = peer*tokens + lax.broadcasted_iota(jnp.int32,(tokens,tokens),0)
    query = own*tokens + lax.broadcasted_iota(jnp.int32,(tokens,tokens),1)
    return jnp.where((key>=start)&(key<=query),0.0,NEG).astype(F32)

def fwd_kernel(count, own_ref, q_ref, seg_ref, counts_ref, other_ref, *refs):
    kv_refs=refs[:count]; att_ref, att_t_ref, lse_ref, start_ref, bias, s_ref = refs[count:]
    own=own_ref[0]
    tokens=q_ref.shape[0]; heads=q_ref.shape[1]//HEAD_DIM
    counts=counts_ref[...]+other_ref[...]
    seg=seg_ref[...]
    start=jnp.where(seg==0,0,jnp.where(seg==1,counts[0:1,0:1],counts[1:2,0:1]))
    start_ref[...]=start
    for step in range(count):
        bias[step*tokens:(step+1)*tokens,:]=masks(start,tokens,own,step)
    q=q_ref[...]*jnp.asarray(HEAD_DIM**-0.5,BF)
    ks=[r[:,:HEAD_DIM] for r in kv_refs]
    vts=[r[:,HEAD_DIM:].astype(F32).T.astype(BF) for r in kv_refs]
    for h in range(heads):
        qh=q[:,h*HEAD_DIM:(h+1)*HEAD_DIM]
        peak=jnp.full((1,tokens),NEG,F32)
        for step in range(count):
            rows=slice(step*tokens,(step+1)*tokens)
            s=dot_rows(ks[step],qh)+bias[rows,:]
            s_ref[h,rows,:]=s
            peak=jnp.maximum(peak,jnp.max(s,0,keepdims=True))
        total=jnp.zeros((1,tokens),F32)
        out=jnp.zeros((HEAD_DIM,tokens),F32)
        for step in range(count):
            rows=slice(step*tokens,(step+1)*tokens)
            p=jnp.exp(s_ref[h,rows,:]-peak)
            total=total+jnp.sum(p,0,keepdims=True)
            out=out+dot(vts[step],p.astype(BF))
        att_t_ref[h*HEAD_DIM:(h+1)*HEAD_DIM,:]=out/total
        lse_ref[h:h+1,:]=peak+jnp.log(total)
    att_ref[...]=att_t_ref[...].T.astype(BF)

def attend_fwd(own, q, segments, counts, other, kvs):
    tokens,width=q.shape; heads=width//HEAD_DIM; n=len(kvs)
    return pl.pallas_call(functools.partial(fwd_kernel,n),
        out_shape=(jax.ShapeDtypeStruct((tokens,width),BF),jax.ShapeDtypeStruct((width,tokens),F32),jax.ShapeDtypeStruct((heads,tokens),F32),jax.ShapeDtypeStruct((1,tokens),jnp.int32)),
        in_specs=[IN_SMEM]+[IN_VMEM]*(4+n), out_specs=(IN_VMEM,)*4,
        scratch_shapes=[pltpu.VMEM((n*tokens,tokens),F32),pltpu.VMEM((heads,n*tokens,tokens),F32)],
        compiler_params=pltpu.CompilerParams(vmem_limit_bytes=VMEM_BYTES),
        cost_estimate=FREE, name="attend_forward")(own,q,segments,counts,other,*kvs)

def bwd_kernel(
    count, own_ref, q_ref, start_ref, att_t_ref, lse_ref, gb_ref, wo_ref, cos_ref, sin_ref, *refs
):
    kv_refs=refs[:count]; gq_ref=refs[count]; gkv_refs=refs[count+1:2*count+1]; bias, gqt, dkv = refs[2*count+1:]
    own=own_ref[0]
    tokens=q_ref.shape[0]; heads=q_ref.shape[1]//HEAD_DIM
    start=start_ref[...]
    do=dot(gb_ref[...],wo_ref[...])
    do_low=do.astype(BF)
    do_t=do_low.astype(F32).T
    prod=do_t*att_t_ref[...]
    q=q_ref[...]
    qs=q*jnp.asarray(HEAD_DIM**-0.5,BF)
    ks=[r[:,:HEAD_DIM] for r in kv_refs]
    vs=[r[:,HEAD_DIM:] for r in kv_refs]
    kts=[k.astype(F32).T.astype(BF) for k in ks]
    dot_low=do_t.astype(BF)
    for step in range(count):
        bias[...]=masks(start,tokens,own,step)
        dk=jnp.zeros((tokens,HEAD_DIM),F32); dv=jnp.zeros((tokens,HEAD_DIM),F32)
        for h in range(heads):
            cols=slice(h*HEAD_DIM,(h+1)*HEAD_DIM)
            qh=qs[:,cols]; doh=do_low[:,cols]
            rowdot=jnp.sum(prod[cols,:],0,keepdims=True)
            p=jnp.exp(dot_rows(ks[step],qh)+(bias[...]-lse_ref[h:h+1,:]))
            dp=dot_rows(vs[step],doh)
            ds=(p*(dp-rowdot)).astype(BF)
            dv=dv+dot(p.astype(BF),doh)
            dk=dk+dot(ds,qh)
            dq=dot(kts[step],ds)
            if step==0: gqt[cols,:]=dq
            else: gqt[cols,:]+=dq
        gkv_refs[step][:,:HEAD_DIM]=dk.astype(BF)
        gkv_refs[step][:,HEAD_DIM:]=dv.astype(BF)
    turned=turn_back(gqt[...]*(HEAD_DIM**-0.5),cos_ref[...],sin_ref[...],-1.0)
    gq_ref[...]=turned.T.astype(BF)

def attend_bwd(own,q,start,att_t,lse,gb,wo,cosines,sines,kvs):
    tokens,width=q.shape; n=len(kvs)
    outs=pl.pallas_call(functools.partial(bwd_kernel,n),
        out_shape=(jax.ShapeDtypeStruct((tokens,width),BF),)+(jax.ShapeDtypeStruct((tokens,2*HEAD_DIM),BF),)*n,
        in_specs=[IN_SMEM]+[IN_VMEM]*(8+n), out_specs=(IN_VMEM,)*(n+1),
        scratch_shapes=[pltpu.VMEM((tokens,tokens),F32),pltpu.VMEM((width,tokens),F32),pltpu.VMEM((8,128),F32)],
        compiler_params=pltpu.CompilerParams(vmem_limit_bytes=VMEM_BYTES),
        cost_estimate=FREE, name="attend_backward")(own,q,start,att_t,lse,gb,wo,cosines,sines,*kvs)
    return outs[0],list(outs[1:])


def prepare_kernel(count, chunk, own_ref, seg_ref, gate_ref, up_ref, down_ref, *refs):
    pieces, counts_ref, wide = refs[:count], refs[count], refs[count + 1]
    counts_ref[...] = jnp.zeros_like(counts_ref)
    for number in range(2):
        below = jnp.sum((seg_ref[...] <= number).astype(jnp.int32), -1, keepdims=True)
        counts_ref[number : number + 1, :] = jnp.broadcast_to(below, (1, LANES))
    rows, hidden = gate_ref.shape
    span = chunk * count
    for number in range(3):
        wide[number, :, :hidden] = (gate_ref, up_ref, down_ref)[number][...]
        if span > hidden:
            wide[number, :, hidden:] = jnp.zeros((rows, span - hidden), BF)
    for step in range(count):
        begin = pl.multiple_of((own_ref[0] ^ step) * chunk, LANES)
        for number in range(3):
            pieces[step][:, number * chunk : (number + 1) * chunk] = wide[
                number, :, pl.ds(begin, chunk)
            ]


def prepare(own, segments, w_gate, w_up, w_down, count, chunk):
    rows = w_gate.shape[0]
    outs = pl.pallas_call(
        functools.partial(prepare_kernel, count, chunk),
        out_shape=(jax.ShapeDtypeStruct((rows, 3 * chunk), BF),) * count
        + (jax.ShapeDtypeStruct((8, LANES), jnp.int32),),
        in_specs=[IN_SMEM] + [IN_VMEM] * 4,
        out_specs=(IN_VMEM,) * (count + 1),
        scratch_shapes=[pltpu.VMEM((3, rows, chunk * count), BF)],
        compiler_params=pltpu.CompilerParams(vmem_limit_bytes=VMEM_BYTES),
        cost_estimate=FREE,
        name="prepare",
    )(own, segments, w_gate, w_up, w_down)
    return list(outs[:count]), outs[count]


def weight_grad_kernel(count, lines, own_ref, left_ref, right_ref, *refs):
    pieces, whole = refs[:count], refs[count]
    whole[...] = turned_dot(left_ref[...], right_ref[...])
    rows = whole.shape[0] // (count * lines)
    for step in range(count):
        peer = own_ref[0] ^ step
        parts = []
        for line in range(lines):
            begin = pl.multiple_of((line * count + peer) * rows, 8)
            parts.append(whole[pl.ds(begin, rows), :])
        pieces[step][...] = jnp.concatenate(parts).astype(BF)


def weight_grad(own, left, right, count, lines):
    height, width = left.shape[1], right.shape[1]
    return list(
        pl.pallas_call(
            functools.partial(weight_grad_kernel, count, lines),
            out_shape=(jax.ShapeDtypeStruct((height // count, width), BF),) * count,
            in_specs=[IN_SMEM] + [IN_VMEM] * 2,
            out_specs=(IN_VMEM,) * count,
            scratch_shapes=[pltpu.VMEM((height, width), F32)],
            compiler_params=pltpu.CompilerParams(vmem_limit_bytes=VMEM_BYTES),
            cost_estimate=FREE,
            name="weight_grad",
        )(own, left, right)
    )


def last_grads_kernel(
    count, lines, own_ref, input_ref, gain_ref, qkv_ref, first_ref, second_ref, middle_ref,
    mlp_ref, out_ref, *refs
):
    pieces, whole, small = refs[:count], refs[count], refs[count + 1]
    features = input_ref.shape[1]
    inputs = input_ref[...].astype(F32)
    scale = lax.rsqrt(jnp.mean(inputs * inputs, -1, keepdims=True) + EPS)
    unit = inputs * scale
    gain = gain_ref[...]
    qkv = qkv_ref[...]
    whole[...] = turned_dot((unit * gain).astype(BF), qkv)
    grad = first_ref[...].astype(F32) + second_ref[...].astype(F32)
    turned = grad * unit
    small[...] = jnp.zeros_like(small)
    small[0:1, :] = jnp.sum(qkv.astype(F32), 0, keepdims=True)
    for row, values in ((1, jnp.sum(turned, 0, keepdims=True)), (3, mlp_ref[...])):
        small[row : row + 1, :SPLIT] = values[:, :SPLIT]
        small[row + 1 : row + 2, : features - SPLIT] = values[:, SPLIT:]
    along = jnp.mean(turned * gain, -1, keepdims=True)
    out_ref[...] = (middle_ref[...] + scale * (grad * gain - unit * along)).astype(BF)
    rows = features // (count * lines)
    for step in range(count):
        peer = own_ref[0] ^ step
        parts = []
        for line in range(lines):
            begin = pl.multiple_of((line * count + peer) * rows, 8)
            parts.append(whole[pl.ds(begin, rows), :])
        pieces[step][...] = jnp.concatenate(parts + [small[...]]).astype(BF)


def last_grads(own, inputs, gain, qkv, first, second, middle, mlp_gain_grad, count, lines):
    tokens, features = inputs.shape
    width = qkv.shape[1]
    outs = pl.pallas_call(
        functools.partial(last_grads_kernel, count, lines),
        out_shape=(jax.ShapeDtypeStruct((tokens, features), BF),)
        + (jax.ShapeDtypeStruct((features // count + SMALL_ROWS, width), BF),) * count,
        in_specs=[IN_SMEM] + [IN_VMEM] * 7,
        out_specs=(IN_VMEM,) * (count + 1),
        scratch_shapes=[pltpu.VMEM((features, width), F32), pltpu.VMEM((SMALL_ROWS, width), F32)],
        compiler_params=pltpu.CompilerParams(vmem_limit_bytes=VMEM_BYTES),
        cost_estimate=FREE,
        name="last_grads",
    )(own, inputs, gain, qkv, first, second, middle, mlp_gain_grad)
    return outs[0], list(outs[1:])


def pack_kernel(count, lines, own_ref, *refs):
    qkv_refs, o_refs = refs[:count], refs[count : 2 * count]
    outs = refs[2 * count : 2 * count + lines]
    qkv_sum, o_sum, block = refs[2 * count + lines :]
    qkv_sum[...] = sum(ref[...].astype(F32) for ref in qkv_refs)
    o_sum[...] = sum(ref[...].astype(F32) for ref in o_refs)
    rows = o_sum.shape[0] // lines
    width = qkv_sum.shape[1]
    block[rows:, :] = jnp.zeros((SMALL_ROWS, block.shape[1]), F32)
    block[rows:, :width] = qkv_sum[lines * rows :, :]
    for step in range(lines):
        begin = pl.multiple_of(lax.rem(own_ref[0] + step, lines) * rows, 8)
        block[:rows, :width] = qkv_sum[pl.ds(begin, rows), :]
        block[:rows, width:] = o_sum[pl.ds(begin, rows), :]
        outs[step][...] = block[...].astype(BF)


def pack(own_line, qkv_parts, o_parts, lines):
    count = len(qkv_parts)
    width, width_o = qkv_parts[0].shape[1], o_parts[0].shape[1]
    rows = o_parts[0].shape[0] // lines
    shape = (rows + SMALL_ROWS, width + width_o)
    return list(
        pl.pallas_call(
            functools.partial(pack_kernel, count, lines),
            out_shape=(jax.ShapeDtypeStruct(shape, BF),) * lines,
            in_specs=[IN_SMEM] + [IN_VMEM] * (2 * count),
            out_specs=(IN_VMEM,) * lines,
            scratch_shapes=[
                pltpu.VMEM(qkv_parts[0].shape, F32),
                pltpu.VMEM(o_parts[0].shape, F32),
                pltpu.VMEM(shape, F32),
            ],
            compiler_params=pltpu.CompilerParams(vmem_limit_bytes=VMEM_BYTES),
            cost_estimate=FREE,
            name="pack",
        )(own_line, *qkv_parts, *o_parts)
    )


def unpack_kernel(lines, widths, *refs):
    parts = refs[:lines]
    q_ref, k_ref, v_ref, o_ref, bq_ref, bk_ref, bv_ref, attn_ref, mlp_ref, total = refs[lines:]
    total[...] = sum(ref[...].astype(F32) for ref in parts)
    rows = q_ref.shape[0]
    first, second = widths[0], widths[0] + widths[1]
    third = second + widths[1]
    q_ref[...] = total[:rows, :first]
    k_ref[...] = total[:rows, first:second]
    v_ref[...] = total[:rows, second:third]
    o_ref[...] = total[:rows, third:]
    bq_ref[...] = total[rows : rows + 1, :first]
    bk_ref[...] = total[rows : rows + 1, first:second]
    bv_ref[...] = total[rows : rows + 1, second:third]
    for row, ref in ((rows + 1, attn_ref), (rows + 3, mlp_ref)):
        ref[:, :SPLIT] = total[row : row + 1, :SPLIT]
        ref[:, SPLIT:] = total[row + 1 : row + 2, : ref.shape[1] - SPLIT]


def unpack(parts, features, width_q, width_k):
    rows, width = parts[0].shape
    rows -= SMALL_ROWS
    width_o = width - width_q - 2 * width_k
    shapes = [
        (rows, width_q), (rows, width_k), (rows, width_k), (rows, width_o),
        (1, width_q), (1, width_k), (1, width_k), (1, features), (1, features),
    ]
    return pl.pallas_call(
        functools.partial(unpack_kernel, len(parts), (width_q, width_k)),
        out_shape=tuple(jax.ShapeDtypeStruct(shape, F32) for shape in shapes),
        in_specs=[IN_VMEM] * len(parts),
        out_specs=(IN_VMEM,) * len(shapes),
        scratch_shapes=[pltpu.VMEM(parts[0].shape, F32)],
        compiler_params=pltpu.CompilerParams(vmem_limit_bytes=VMEM_BYTES),
        cost_estimate=FREE,
        name="unpack",
    )(*parts)


def mlp_out_kernel(count, chunk, own_ref, *refs):
    parts = refs[:count]
    gate_ref, up_ref, down_ref, wide = refs[count:]
    rows, hidden = gate_ref.shape
    for step in range(count):
        begin = pl.multiple_of((own_ref[0] ^ step) * chunk, LANES)
        for number in range(3):
            wide[number, :, pl.ds(begin, chunk)] = parts[step][
                :, number * chunk : (number + 1) * chunk
            ].astype(F32)
    for number, ref in enumerate((gate_ref, up_ref, down_ref)):
        ref[...] = wide[number, :, :hidden]


def mlp_out(own, parts, hidden):
    count = len(parts)
    rows, width = parts[0].shape
    chunk = width // 3
    return pl.pallas_call(
        functools.partial(mlp_out_kernel, count, chunk),
        out_shape=(jax.ShapeDtypeStruct((rows, hidden), F32),) * 3,
        in_specs=[IN_SMEM] + [IN_VMEM] * count,
        out_specs=(IN_VMEM,) * 3,
        scratch_shapes=[pltpu.VMEM((3, rows, chunk * count), F32)],
        compiler_params=pltpu.CompilerParams(vmem_limit_bytes=VMEM_BYTES),
        cost_estimate=FREE,
        name="mlp_out",
    )(own, *parts)


def score_block(query_groups, key_rows, key_index, start, query_index):
    head_dim = query_groups.shape[-1]
    logits = jnp.einsum(
        "qgjd,kgd->gjqk", query_groups, key_rows, preferred_element_type=jnp.float32
    ) * head_dim ** (-0.5)
    allowed = (key_index[None, :] >= start[:, None]) & (key_index[None, :] <= query_index[:, None])
    return jnp.where(allowed, logits, NEG)


def key_window(keyval_all, number, key_block, key_heads):
    window = lax.dynamic_slice_in_dim(keyval_all, number * key_block, key_block, 0)
    width = window.shape[1] // 2
    key_rows = window[:, :width].reshape(key_block, key_heads, width // key_heads)
    value_rows = window[:, width:].reshape(key_block, key_heads, width // key_heads)
    key_index = number * key_block + jnp.arange(key_block, dtype=jnp.int32)
    return key_rows, value_rows, key_index


def repeat(count, step, state):
    if count == 1:
        return step(0, state)
    return lax.fori_loop(0, count, step, state)


def attend(query_rot, keyval_all, start, query_index, key_heads):
    tokens, head_count, head_dim = query_rot.shape
    group_size = head_count // key_heads
    key_block = min(keyval_all.shape[0], 1024)
    query_groups = query_rot.reshape(tokens, key_heads, group_size, head_dim)
    block_count = keyval_all.shape[0] // key_block

    def measure(number, state_pair):
        running_peak, running_total = state_pair
        key_rows, value_rows, key_index = key_window(
            keyval_all, number, key_block, key_heads
        )
        masked = score_block(query_groups, key_rows, key_index, start, query_index)
        fresh = jnp.maximum(running_peak, jnp.max(masked, -1))
        running_total = running_total * jnp.exp(running_peak - fresh) + jnp.sum(
            jnp.exp(masked - fresh[..., None]), -1
        )
        return (fresh, running_total)

    start_state = (
        jnp.full((key_heads, group_size, tokens), NEG, jnp.float32),
        jnp.zeros((key_heads, group_size, tokens), jnp.float32),
    )
    running_peak, running_total = repeat(block_count, measure, start_state)
    log_total = running_peak + jnp.log(running_total)

    def collect(number, summed):
        key_rows, value_rows, key_index = key_window(
            keyval_all, number, key_block, key_heads
        )
        masked = score_block(query_groups, key_rows, key_index, start, query_index)
        chances = jnp.exp(masked - log_total[..., None]).astype(jnp.bfloat16)
        return summed + jnp.einsum(
            "gjqk,kgd->gjqd", chances, value_rows, preferred_element_type=jnp.float32
        )

    summed = repeat(
        block_count, collect, jnp.zeros((key_heads, group_size, tokens, head_dim), jnp.float32)
    )
    return (summed.transpose(2, 0, 1, 3).reshape(tokens, head_count * head_dim), log_total)


def attend_back(
    query_rot,
    keyval_all,
    start,
    query_index,
    key_heads,
    log_total,
    attended,
    grad_attended,
):
    tokens, head_count, head_dim = query_rot.shape
    group_size = head_count // key_heads
    key_block = min(keyval_all.shape[0], 1024)
    query_groups = query_rot.reshape(tokens, key_heads, group_size, head_dim)
    grad_groups = grad_attended.reshape(tokens, key_heads, group_size, head_dim)
    block_count = keyval_all.shape[0] // key_block
    row_dot = jnp.sum(
        (grad_attended.astype(jnp.float32) * attended).reshape(
            tokens, key_heads, group_size, head_dim
        ),
        -1,
    ).transpose(1, 2, 0)
    score_scale = head_dim ** (-0.5)

    def step_back(number, state_pair):
        grad_query, grad_keyval = state_pair
        key_rows, value_rows, key_index = key_window(
            keyval_all, number, key_block, key_heads
        )
        masked = score_block(query_groups, key_rows, key_index, start, query_index)
        chances = jnp.exp(masked - log_total[..., None])
        chances_low = chances.astype(jnp.bfloat16)
        grad_chances = jnp.einsum(
            "qgjd,kgd->gjqk", grad_groups, value_rows, preferred_element_type=jnp.float32
        )
        grad_logits = (chances * (grad_chances - row_dot[..., None])).astype(jnp.bfloat16)
        grad_query = (
            grad_query
            + jnp.einsum(
                "gjqk,kgd->gjqd", grad_logits, key_rows, preferred_element_type=jnp.float32
            )
            * score_scale
        )
        grad_keys = (
            jnp.einsum(
                "gjqk,qgjd->kgd", grad_logits, query_groups, preferred_element_type=jnp.float32
            )
            * score_scale
        )
        grad_values = jnp.einsum(
            "gjqk,qgjd->kgd", chances_low, grad_groups, preferred_element_type=jnp.float32
        )
        grad_piece = jnp.concatenate(
            [
                grad_keys.reshape(key_block, key_heads * head_dim),
                grad_values.reshape(key_block, key_heads * head_dim),
            ],
            axis=-1,
        ).astype(jnp.bfloat16)
        grad_keyval = lax.dynamic_update_slice_in_dim(
            grad_keyval, grad_piece, number * key_block, 0
        )
        return (grad_query, grad_keyval)

    start_state = (
        jnp.zeros((key_heads, group_size, tokens, head_dim), jnp.float32),
        jnp.zeros(keyval_all.shape, jnp.bfloat16),
    )
    grad_query, grad_keyval = repeat(block_count, step_back, start_state)
    return (grad_query.transpose(2, 0, 1, 3).reshape(tokens, head_count, head_dim), grad_keyval)


def body(
    layer_input,
    segments,
    positions,
    attn_gain,
    w_q,
    b_q,
    w_k,
    b_k,
    w_v,
    b_v,
    w_o,
    mlp_gain,
    w_gate,
    w_up,
    w_down,
    cotangent,
):
    key_heads = w_k.shape[1] // HEAD_DIM
    head_count = w_q.shape[1] // HEAD_DIM
    width_q, width_k = w_q.shape[1], w_k.shape[1]
    tokens = layer_input.shape[1]
    ctx_size, fsdp_size = lax.axis_size("ctx"), lax.axis_size("fsdp")
    ctx_own = lax.axis_index("ctx")
    rows, hidden_count = w_gate.shape
    features = layer_input.shape[2]
    chunk = -(-hidden_count // (ctx_size * LANES)) * LANES
    width_qkv = width_q + 2 * width_k
    own = ctx_own.astype(jnp.int32)[None]

    attn_lined = direct_gather(jnp.concatenate([w_q, w_k, w_v, w_o.T], axis=1))

    if few():
        cuts, counts = prepare(own, segments, w_gate, w_up, w_down.T, ctx_size, chunk)
    else:
        tail = ((0, 0), (0, chunk * ctx_size - hidden_count))
        shards = [
            jnp.pad(shard, tail).reshape(rows, ctx_size, chunk) for shard in (w_gate, w_up, w_down.T)
        ]
        cuts = list(jnp.concatenate(shards, axis=-1).transpose(1, 0, 2))
    recut = untangle(trade(cuts))
    mlp_line = gather_step([recut], 0)

    seg_own = segments[0]
    if few():
        counts = after(counts, recut)
    else:
        counts = jnp.stack([jnp.sum((seg_own <= number).astype(jnp.int32)) for number in range(2)])
    step = 1
    while 2 * step < ctx_size:
        counts = counts + lax.ppermute(counts, "ctx", flips(ctx_size, step))
        step *= 2
    counts_other = lax.ppermute(counts, "ctx", flips(ctx_size, step))

    def ordered(parts):
        pieces = untangle(parts)
        return pieces.transpose(1, 0, 2, 3).reshape(features, pieces.shape[-1])

    full_qkv = ordered(spread(attn_lined[..., :width_qkv]))
    o_pieces = spread(attn_lined[..., width_qkv:])

    inputs = layer_input[0].astype(jnp.float32)
    place = jnp.arange(tokens, dtype=jnp.int32)
    query_index = ctx_own * tokens + place
    grad_top = cotangent[0]
    cosines, sines = angles(positions[0], HEAD_DIM)
    scale_one = lax.rsqrt(jnp.mean(inputs * inputs, -1, keepdims=True) + EPS)
    unit_one = inputs * scale_one
    normed = (unit_one * attn_gain).astype(jnp.bfloat16)
    small_heads = few() and key_heads == 1
    if small_heads:
        half = HEAD_DIM // 2
        cos_turned, sin_turned = cosines[:, 0, :half].T, sines[:, 0, :half].T
        query_flat, keyval = project(
            layer_input[0],
            attn_gain[None],
            full_qkv,
            jnp.concatenate([b_q, b_k, b_v])[None],
            cos_turned,
            sin_turned,
            width_q,
            width_k,
        )
    else:
        projected = jnp.dot(normed, full_qkv, preferred_element_type=jnp.float32) + jnp.concatenate(
            [b_q, b_k, b_v]
        )
        queries = projected[:, :width_q]
        keyproj = projected[:, width_q : width_q + width_k]
        valproj = projected[:, width_q + width_k :]
        query_rot = rotate(queries.reshape(tokens, head_count, HEAD_DIM), cosines, sines).astype(
            jnp.bfloat16
        )
        key_rot = rotate(keyproj.reshape(tokens, key_heads, HEAD_DIM), cosines, sines).astype(
            jnp.bfloat16
        )
        keyval = jnp.concatenate(
            [key_rot.reshape(tokens, key_heads * HEAD_DIM), valproj.astype(jnp.bfloat16)], axis=-1
        )
    keyval, o_pieces, mlp_line = lax.optimization_barrier((keyval, o_pieces, mlp_line))
    received = spread(keyval)
    mlp_line = gather_step(mlp_line, 1)
    full_o_turned = ordered(o_pieces)
    grad_top_mine = gather_half(after(grad_top, received[-1]))
    if small_heads:
        attended_low, attended_turned, log_total, start = attend_fwd(
            own, query_flat, segments, counts, counts_other, received
        )
    else:
        counts = counts + counts_other
        start = jnp.where(seg_own == 0, 0, jnp.where(seg_own == 1, counts[0], counts[1]))
        order = untangle(received).reshape(ctx_size * tokens, 2 * width_k)
        attended, log_total = attend(query_rot, order, start, query_index, key_heads)
        attended_low = attended.astype(jnp.bfloat16)
    attended_low, mlp_line, grad_top_mine = lax.optimization_barrier(
        (attended_low, mlp_line, grad_top_mine)
    )
    for step in range(2, fsdp_size - 1):
        mlp_line = gather_step(mlp_line, step)
    branch_part = dot_rows(attended_low, full_o_turned).astype(jnp.bfloat16)
    middle = inputs + (
        branch_part.astype(jnp.float32) + swap_cores(branch_part).astype(jnp.float32)
    )
    scale_two = lax.rsqrt(jnp.mean(middle * middle, -1, keepdims=True) + EPS)
    unit_two = middle * scale_two
    normed_two = (unit_two * mlp_gain).astype(jnp.bfloat16)

    normed_mine = gather_half(normed_two)
    normed_mine, mlp_line = lax.optimization_barrier((normed_mine, mlp_line))
    mlp_rows = gather_end(mlp_line).reshape(features, 3 * chunk)
    gate_up, down_turned = mlp_rows[:, : 2 * chunk], mlp_rows[:, 2 * chunk :]

    normed_all, grad_top_all = both_halves(normed_mine), both_halves(grad_top_mine)
    gate_upward = jnp.dot(normed_all, gate_up, preferred_element_type=jnp.float32)
    grad_hidden = jnp.dot(grad_top_all, down_turned, preferred_element_type=jnp.float32)
    gate_values, upward = gate_upward[:, :chunk], gate_upward[:, chunk:]
    sigmoid_gate = jax.nn.sigmoid(gate_values)
    swish_gate = gate_values * sigmoid_gate
    hidden = (swish_gate * upward).astype(jnp.bfloat16)
    grad_gate = (
        grad_hidden * upward * sigmoid_gate * (1.0 + gate_values * (1.0 - sigmoid_gate))
    ).astype(jnp.bfloat16)
    grad_upward = (grad_hidden * swish_gate).astype(jnp.bfloat16)
    grad_both = jnp.concatenate([grad_gate, grad_upward], axis=-1)
    grad_normed_sum = add_cores(dot_rows(grad_both, gate_up).astype(jnp.bfloat16))
    grad_normed_parts = trade(jnp.split(grad_normed_sum, ctx_size))
    mlp_grad = jnp.concatenate(
        [
            turned_dot(normed_all, grad_both).astype(jnp.bfloat16),
            turned_dot(grad_top_all, hidden).astype(jnp.bfloat16),
        ],
        axis=-1,
    ).reshape(fsdp_size, ctx_size * rows, 3 * chunk)
    mlp_sums = scatter_step(mlp_grad, [], 1)
    branch_two_sum = add_cores(dot_rows(hidden, down_turned).astype(jnp.bfloat16))
    branch_two_sum, *grad_normed_parts = lax.optimization_barrier(
        (branch_two_sum, *grad_normed_parts)
    )
    grad_normed_two = join_tokens(grad_normed_parts)
    branch_two_parts = trade(jnp.split(branch_two_sum, ctx_size))

    grad_mlp_gain = jnp.sum(grad_normed_two * unit_two, 0)
    grad_unit_two = grad_normed_two * mlp_gain
    grad_middle = grad_top.astype(jnp.float32) + scale_two * (
        grad_unit_two - unit_two * jnp.mean(grad_unit_two * unit_two, -1, keepdims=True)
    )
    grad_branch = grad_middle.astype(jnp.bfloat16)
    if small_heads:
        grad_query, grad_keyvals = attend_bwd(
            own,
            query_flat,
            start,
            attended_turned,
            log_total,
            grad_branch,
            full_o_turned,
            cos_turned,
            sin_turned,
            received,
        )
    else:
        grad_attended = dot(grad_branch, full_o_turned).astype(jnp.bfloat16)
        grad_query_rot, grad_keyvals = attend_back(
            query_rot,
            order,
            start,
            query_index,
            key_heads,
            log_total,
            attended,
            grad_attended,
        )
        grad_keyvals = choose(grad_keyvals.reshape(ctx_size, tokens, 2 * width_k))
    grad_keyvals[0], mlp_sums, branch_two_parts = lax.optimization_barrier(
        (grad_keyvals[0], mlp_sums, branch_two_parts)
    )
    if fsdp_size > 2:
        mlp_sums = scatter_step(mlp_grad, mlp_sums, 2)
    keyval_parts = trade(grad_keyvals)
    branch_two = join_tokens(branch_two_parts)
    result = (middle + branch_two).astype(jnp.bfloat16)

    def owners(left, right):
        if few():
            return weight_grad(own, left, right, ctx_size, fsdp_size)
        grad = turned_dot(left, right).astype(jnp.bfloat16)
        cut = grad.reshape(fsdp_size, ctx_size, rows, right.shape[1]).transpose(1, 0, 2, 3)
        return list(cut.reshape(ctx_size, fsdp_size * rows, right.shape[1]))

    o_parts = trade(owners(grad_branch, after(attended_low, grad_keyvals[0])))
    if small_heads:
        grad_qkv, grad_normed_part = key_grads(
            grad_query, full_qkv, cos_turned, sin_turned, keyval_parts
        )
    else:
        grad_keyval = sum(part.astype(F32) for part in keyval_parts)
        grad_query = (
            rotate(grad_query_rot, cosines, -sines)
            .reshape(tokens, head_count * HEAD_DIM)
            .astype(jnp.bfloat16)
        )
        grad_key = (
            rotate(
                grad_keyval[:, : key_heads * HEAD_DIM].reshape(tokens, key_heads, HEAD_DIM),
                cosines,
                -sines,
            )
            .reshape(tokens, key_heads * HEAD_DIM)
            .astype(jnp.bfloat16)
        )
        grad_value = grad_keyval[:, key_heads * HEAD_DIM :].astype(jnp.bfloat16)
        grad_qkv = jnp.concatenate([grad_query, grad_key, grad_value], axis=-1)
        grad_normed_part = dot_rows(grad_qkv, full_qkv).astype(jnp.bfloat16)
    grad_normed_other = swap_cores(grad_normed_part)
    if few():
        grad_inputs, qkv_pieces = last_grads(
            own,
            layer_input[0],
            attn_gain[None],
            grad_qkv,
            grad_normed_part,
            grad_normed_other,
            grad_middle,
            grad_mlp_gain[None],
            ctx_size,
            fsdp_size,
        )
    else:
        grad_normed = grad_normed_part.astype(F32) + grad_normed_other.astype(F32)
        turned = grad_normed * unit_one
        along = jnp.mean(turned * attn_gain, -1, keepdims=True)
        grad_inputs = grad_middle + scale_one * (grad_normed * attn_gain - unit_one * along)
        grad_inputs = grad_inputs.astype(jnp.bfloat16)
        lines = [jnp.sum(grad_qkv.astype(F32), 0)]
        for gains in (jnp.sum(turned, 0), grad_mlp_gain):
            for half in (gains[:SPLIT], gains[SPLIT:]):
                lines.append(jnp.pad(half, (0, width_qkv - half.shape[0])))
        small = jnp.pad(jnp.stack(lines), ((0, SMALL_ROWS - len(lines)), (0, 0)))
        small = small.astype(jnp.bfloat16)
        qkv_pieces = [jnp.concatenate([part, small]) for part in owners(normed, grad_qkv)]
    qkv_pieces[0], mlp_sums = lax.optimization_barrier((qkv_pieces[0], mlp_sums))
    for step in range(3, fsdp_size):
        mlp_sums = scatter_step(mlp_grad, mlp_sums, step)
    qkv_parts = trade(qkv_pieces)
    fsdp_own = lax.axis_index("fsdp").astype(jnp.int32)
    if few():
        packed = pack(fsdp_own[None], qkv_parts, o_parts, fsdp_size)
    else:
        qkv_sum = sum(part.astype(F32) for part in qkv_parts)
        o_sum = sum(part.astype(F32) for part in o_parts)
        small = jnp.pad(qkv_sum[fsdp_size * rows :], ((0, 0), (0, w_o.shape[0])))
        both = jnp.concatenate([qkv_sum[: fsdp_size * rows], o_sum], axis=-1)
        both = both.reshape(fsdp_size, rows, both.shape[-1])
        packed = [
            jnp.concatenate([both[(fsdp_own + step) % fsdp_size], small]).astype(jnp.bfloat16)
            for step in range(fsdp_size)
        ]
    packed[0], mlp_sums = lax.optimization_barrier((packed[0], mlp_sums))
    mlp_mine = scatter_end(mlp_grad, mlp_sums).astype(jnp.bfloat16).reshape(ctx_size, rows, 3 * chunk)
    packed = packed[:1] + [send_up(packed[step], step) for step in range(1, fsdp_size)]
    mlp_pieces = trade(choose(mlp_mine))
    if few():
        w_grads = unpack(packed, features, width_q, width_k)
        mlp_grads = mlp_out(own, mlp_pieces, hidden_count)
    else:
        total = sum(part.astype(F32) for part in packed)
        tops = [0, width_q, width_q + width_k, width_qkv]
        w_grads = [total[:rows, tops[k] : tops[k + 1]] for k in range(3)]
        w_grads.append(total[:rows, width_qkv:])
        w_grads += [total[rows, tops[k] : tops[k + 1]] for k in range(3)]
        for row in (rows + 1, rows + 3):
            w_grads.append(
                jnp.concatenate([total[row, :SPLIT], total[row + 1, : features - SPLIT]])
            )
        mlp_grads = []
        for number in range(3):
            pieces = untangle(mlp_pieces)[..., number * chunk : (number + 1) * chunk]
            wide = pieces.transpose(1, 0, 2).reshape(rows, chunk * ctx_size)
            mlp_grads.append(wide[:, :hidden_count].astype(F32))
    grad_q, grad_k, grad_v, grad_o = w_grads[:4]
    grad_b_q, grad_b_k, grad_b_v, grad_attn_gain, grad_mlp_gain = [
        values.reshape(-1) for values in w_grads[4:]
    ]
    return (
        result[None],
        grad_inputs[None],
        grad_attn_gain,
        grad_q,
        grad_b_q,
        grad_k,
        grad_b_k,
        grad_v,
        grad_b_v,
        grad_o.T,
        grad_mlp_gain,
        mlp_grads[0],
        mlp_grads[1],
        mlp_grads[2].T,
    )


def solution(mesh):
    placed = (
        P("fsdp", "ctx", None),
        P("fsdp", "ctx"),
        P("fsdp", "ctx"),
        P(),
        P(("fsdp", "ctx"), "tp"),
        P("tp"),
        P(("fsdp", "ctx"), "tp"),
        P("tp"),
        P(("fsdp", "ctx"), "tp"),
        P("tp"),
        P("tp", ("fsdp", "ctx")),
        P(),
        P(("fsdp", "ctx"), "tp"),
        P(("fsdp", "ctx"), "tp"),
        P("tp", ("fsdp", "ctx")),
        P("fsdp", "ctx", None),
    )
    return jax.shard_map(
        body,
        mesh=mesh,
        in_specs=placed,
        out_specs=(
            P("fsdp", "ctx", None),
            P("fsdp", "ctx", None),
            P(),
            P(("fsdp", "ctx"), "tp"),
            P("tp"),
            P(("fsdp", "ctx"), "tp"),
            P("tp"),
            P(("fsdp", "ctx"), "tp"),
            P("tp"),
            P("tp", ("fsdp", "ctx")),
            P(),
            P(("fsdp", "ctx"), "tp"),
            P(("fsdp", "ctx"), "tp"),
            P("tp", ("fsdp", "ctx")),
        ),
        check_vma=False,
    )
```

```python
import functools
import math

import jax
import jax.numpy as jnp
from jax import lax
from jax.experimental import pallas as pl
from jax.experimental.pallas import tpu as pltpu
from jax.sharding import PartitionSpec as P

HEAD_DIM = 64


EPS = 1e-06
THETA = 1000000.0
NEG = -1e30

LANES = 128
SPLIT = 512
SMALL_ROWS = 16
VMEM_BYTES = 16 * 2**20
FREE = pl.CostEstimate(flops=0, bytes_accessed=0, transcendentals=0)
IN_VMEM = pl.BlockSpec(memory_space=pltpu.VMEM)
IN_SMEM = pl.BlockSpec(memory_space=pltpu.SMEM)
F32 = jnp.float32
BF = jnp.bfloat16


def dot(left, right):
    return jnp.dot(left, right, preferred_element_type=F32)


def dot_rows(left, right):
    return lax.dot_general(left, right, (((1,), (1,)), ((), ())), preferred_element_type=F32)


def turned_dot(left, right):
    return lax.dot_general(left, right, (((0,), (0,)), ((), ())), preferred_element_type=F32)


def rotate(values, cosines, sines):
    halfway = values.shape[-1] // 2
    turned = jnp.concatenate([-values[..., halfway:], values[..., :halfway]], axis=-1)
    return values * cosines + turned * sines


def angles(positions, head_dim):
    even_steps = jnp.arange(0, head_dim, 2).astype(jnp.float32)
    inverse = jnp.exp(-math.log(THETA) * even_steps / head_dim)
    phases = positions.astype(jnp.float32)[..., None] * inverse
    phases = jnp.concatenate([phases, phases], axis=-1)
    return (jnp.cos(phases)[..., None, :], jnp.sin(phases)[..., None, :])


def flips(size, step):
    return [(index, index ^ step) for index in range(size)]


def swap_cores(values):
    return lax.ppermute(values, "tp", flips(lax.axis_size("tp"), 1))


def few():
    return lax.axis_size("ctx") <= 8


def peers():
    size = lax.axis_size("ctx")
    if few():
        return [lax.axis_index("ctx") ^ step for step in range(size)]
    return list(range(size))


def spread(values):
    size = lax.axis_size("ctx")
    if not few():
        return list(lax.all_gather(values, "ctx"))
    return [values] + [lax.ppermute(values, "ctx", flips(size, step)) for step in range(1, size)]


def trade(parts):
    size = lax.axis_size("ctx")
    if not few():
        return list(lax.all_to_all(jnp.stack(parts), "ctx", 0, 0))
    return [parts[0]] + [
        lax.ppermute(parts[step], "ctx", flips(size, step)) for step in range(1, size)
    ]


def untangle(parts):
    if not few():
        return jnp.stack(parts)
    own = lax.axis_index("ctx")
    whole = jnp.stack(parts)
    return jnp.stack(
        [lax.dynamic_index_in_dim(whole, own ^ place, 0, keepdims=False) for place in range(len(parts))]
    )


def choose(whole):
    if not few():
        return list(whole)
    return [lax.dynamic_index_in_dim(whole, peer, 0, keepdims=False) for peer in peers()]


def after(values, *earlier):
    return lax.optimization_barrier((values,) + earlier)[0]


def direct_gather(values):
    size = lax.axis_size("fsdp")
    own = lax.axis_index("fsdp")
    pieces = [values] + [
        lax.ppermute(values, "fsdp", [(index, (index + step) % size) for index in range(size)])
        for step in range(1, size)
    ]
    pieces = pieces[::-1]
    line = jnp.stack(pieces + pieces[:-1])
    return lax.dynamic_slice_in_dim(line, size - 1 - own, size, 0)


def send_up(values, step):
    size = lax.axis_size("fsdp")
    return lax.ppermute(values, "fsdp", [(index, (index + step) % size) for index in range(size)])


def line_steps():
    size = lax.axis_size("fsdp")
    ups = [(index, index + 1) for index in range(size - 1)]
    downs = [(index + 1, index) for index in range(size - 1)]
    return ups, downs


def gather_step(line, step):
    ups, downs = line_steps()
    return (
        [lax.ppermute(line[0], "fsdp", ups[step:])]
        + line
        + [lax.ppermute(line[-1], "fsdp", downs[: len(downs) - step])]
    )


def gather_end(line):
    size = lax.axis_size("fsdp")
    return lax.dynamic_slice_in_dim(
        jnp.stack(line), size - 1 - lax.axis_index("fsdp"), size, 0
    )


def scatter_step(whole, sums, step):
    size = lax.axis_size("fsdp")
    own = lax.axis_index("fsdp")
    ups, downs = line_steps()
    pieces = [
        lax.dynamic_index_in_dim(whole, place, 0, keepdims=False)
        for place in (own + size - step, own - size + step)
    ]
    if sums:
        pieces = [piece + part for piece, part in zip(pieces, sums)]
    return [
        lax.ppermute(pieces[0], "fsdp", ups[:step]),
        lax.ppermute(pieces[1], "fsdp", downs[size - 1 - step :]),
    ]


def scatter_end(whole, sums):
    own = lax.dynamic_index_in_dim(whole, lax.axis_index("fsdp"), 0, keepdims=False)
    return sum(part.astype(F32) for part in [own] + sums)


def gather_half(values):
    half = values.shape[0] // 2
    return jnp.concatenate(
        spread(lax.dynamic_slice_in_dim(values, lax.axis_index("tp") * half, half, 0))
    )


def add_cores(mine, other):
    return (mine.astype(jnp.float32) + swap_cores(other).astype(jnp.float32)).astype(jnp.bfloat16)


def join_tokens(parts):
    own = sum(part.astype(jnp.float32) for part in parts).astype(jnp.bfloat16)
    other = swap_cores(own)
    first = lax.axis_index("tp") == 0
    return jnp.where(
        first, jnp.concatenate([own, other]), jnp.concatenate([other, own])
    ).astype(jnp.float32)


def turn_back(values, cosines, sines, sign):
    half = cosines.shape[0]
    parts = []
    for begin in range(0, values.shape[0], 2 * half):
        first = values[begin : begin + half]
        second = values[begin + half : begin + 2 * half]
        parts += [first * cosines - second * (sign * sines), second * cosines + first * (sign * sines)]
    return jnp.concatenate(parts)


def project_kernel(
    width_q, width_k, input_ref, gain_ref, w_ref, b_ref, cos_ref, sin_ref, seg_ref, q_ref, kv_ref
):
    inputs = input_ref[...].astype(F32)
    scale = lax.rsqrt(jnp.mean(inputs * inputs, -1, keepdims=True) + EPS)
    normed = (inputs * scale * gain_ref[...]).astype(BF)
    projected = dot(normed, w_ref[...]) + b_ref[...]
    rotated = turn_back(projected[:, : width_q + width_k].T, cos_ref[...], sin_ref[...], 1.0).T
    q_ref[...] = rotated[:, :width_q].astype(BF)
    tokens = q_ref.shape[0]
    kv_ref[:tokens, :width_k] = rotated[:, width_q:].astype(BF)
    kv_ref[:tokens, width_k:] = projected[:, width_q + width_k :].astype(BF)
    number = lax.broadcasted_iota(jnp.int32, (SMALL_ROWS, kv_ref.shape[1]), 0)
    counts = jnp.zeros(number.shape, F32)
    for row in range(2):
        below = jnp.sum((seg_ref[...] <= row).astype(F32), -1, keepdims=True)
        counts = jnp.where(number == row, below, counts)
    kv_ref[tokens:, :] = counts.astype(BF)


def project(inputs, gain, weights, biases, cosines, sines, segments, width_q, width_k):
    tokens = inputs.shape[0]
    return pl.pallas_call(
        functools.partial(project_kernel, width_q, width_k),
        out_shape=(
            jax.ShapeDtypeStruct((tokens, width_q), BF),
            jax.ShapeDtypeStruct((tokens + SMALL_ROWS, 2 * width_k), BF),
        ),
        in_specs=[IN_VMEM] * 7,
        out_specs=(IN_VMEM,) * 2,
        compiler_params=pltpu.CompilerParams(vmem_limit_bytes=VMEM_BYTES),
        cost_estimate=FREE,
        name="project",
    )(inputs, gain, weights, biases, cosines, sines, segments)


def key_grads_kernel(count, q_ref, w_ref, cos_ref, sin_ref, *refs):
    parts, qkv_ref, normed_ref = refs[:count], refs[count], refs[count + 1]
    width_q = q_ref.shape[1]
    total = sum(ref[...].astype(F32) for ref in parts)
    width_k = total.shape[1] // 2
    keys = turn_back(total[:, :width_k].T, cos_ref[...], sin_ref[...], -1.0).T
    qkv_ref[:, :width_q] = q_ref[...]
    qkv_ref[:, width_q : width_q + width_k] = keys.astype(BF)
    qkv_ref[:, width_q + width_k :] = total[:, width_k:].astype(BF)
    normed_ref[...] = dot_rows(qkv_ref[...], w_ref[...]).astype(BF)


def key_grads(grad_query, weights, cosines, sines, parts):
    tokens = grad_query.shape[0]
    features, width = weights.shape
    return pl.pallas_call(
        functools.partial(key_grads_kernel, len(parts)),
        out_shape=(
            jax.ShapeDtypeStruct((tokens, width), BF),
            jax.ShapeDtypeStruct((tokens, features), BF),
        ),
        in_specs=[IN_VMEM] * (4 + len(parts)),
        out_specs=(IN_VMEM,) * 2,
        compiler_params=pltpu.CompilerParams(vmem_limit_bytes=VMEM_BYTES),
        cost_estimate=FREE,
        name="key_grads",
    )(grad_query, weights, cosines, sines, *parts)


def masks(start, tokens, own, step):
    peer = own ^ step
    key = peer*tokens + lax.broadcasted_iota(jnp.int32,(tokens,tokens),0)
    query = own*tokens + lax.broadcasted_iota(jnp.int32,(tokens,tokens),1)
    return jnp.where((key>=start)&(key<=query),0.0,NEG).astype(F32)

def fwd_kernel(count, own_ref, q_ref, seg_ref, *refs):
    kv_refs=refs[:count]; att_ref, att_t_ref, lse_ref, start_ref, bias, s_ref = refs[count:]
    own=own_ref[0]
    tokens=q_ref.shape[0]; heads=q_ref.shape[1]//HEAD_DIM
    counts=sum(r[tokens:,:].astype(F32) for r in kv_refs).astype(jnp.int32)
    seg=seg_ref[...]
    start=jnp.where(seg==0,0,jnp.where(seg==1,counts[0:1,0:1],counts[1:2,0:1]))
    start_ref[...]=start
    for step in range(count):
        bias[step*tokens:(step+1)*tokens,:]=masks(start,tokens,own,step)
    q=q_ref[...]*jnp.asarray(HEAD_DIM**-0.5,BF)
    ks=[r[:tokens,:HEAD_DIM] for r in kv_refs]
    vts=[r[:tokens,HEAD_DIM:].astype(F32).T.astype(BF) for r in kv_refs]
    for h in range(heads):
        qh=q[:,h*HEAD_DIM:(h+1)*HEAD_DIM]
        peak=jnp.full((1,tokens),NEG,F32)
        for step in range(count):
            rows=slice(step*tokens,(step+1)*tokens)
            s=dot_rows(ks[step],qh)+bias[rows,:]
            s_ref[h%2,rows,:]=s
            peak=jnp.maximum(peak,jnp.max(s,0,keepdims=True))
        total=jnp.zeros((1,tokens),F32)
        out=jnp.zeros((HEAD_DIM,tokens),F32)
        for step in range(count):
            rows=slice(step*tokens,(step+1)*tokens)
            p=jnp.exp(s_ref[h%2,rows,:]-peak)
            total=total+jnp.sum(p,0,keepdims=True)
            out=out+dot(vts[step],p.astype(BF))
        att_t_ref[h*HEAD_DIM:(h+1)*HEAD_DIM,:]=out/total
        lse_ref[h:h+1,:]=peak+jnp.log(total)
    att_ref[...]=att_t_ref[...].T.astype(BF)

def attend_fwd(own, q, segments, kvs):
    tokens,width=q.shape; heads=width//HEAD_DIM; n=len(kvs)
    return pl.pallas_call(functools.partial(fwd_kernel,n),
        out_shape=(jax.ShapeDtypeStruct((tokens,width),BF),jax.ShapeDtypeStruct((width,tokens),F32),jax.ShapeDtypeStruct((heads,tokens),F32),jax.ShapeDtypeStruct((1,tokens),jnp.int32)),
        in_specs=[IN_SMEM]+[IN_VMEM]*(2+n), out_specs=(IN_VMEM,)*4,
        scratch_shapes=[pltpu.VMEM((n*tokens,tokens),F32),pltpu.VMEM((2,n*tokens,tokens),F32)],
        compiler_params=pltpu.CompilerParams(vmem_limit_bytes=VMEM_BYTES),
        cost_estimate=FREE, name="attend_forward")(own,q,segments,*kvs)

def bwd_kernel(
    count, own_ref, q_ref, start_ref, att_t_ref, lse_ref, gb_ref, wo_ref, cos_ref, sin_ref, *refs
):
    kv_refs=refs[:count]; gq_ref=refs[count]; gkv_refs=refs[count+1:2*count+1]; bias, gqt, dkv = refs[2*count+1:]
    own=own_ref[0]
    tokens=q_ref.shape[0]; heads=q_ref.shape[1]//HEAD_DIM
    start=start_ref[...]
    do=dot(gb_ref[...],wo_ref[...])
    do_low=do.astype(BF)
    do_t=do_low.astype(F32).T
    prod=do_t*att_t_ref[...]
    q=q_ref[...]
    qs=q*jnp.asarray(HEAD_DIM**-0.5,BF)
    ks=[r[:tokens,:HEAD_DIM] for r in kv_refs]
    vs=[r[:tokens,HEAD_DIM:] for r in kv_refs]
    kts=[k.astype(F32).T.astype(BF) for k in ks]
    dot_low=do_t.astype(BF)
    for step in range(count):
        bias[...]=masks(start,tokens,own,step)
        dk=jnp.zeros((tokens,HEAD_DIM),F32); dv=jnp.zeros((tokens,HEAD_DIM),F32)
        for h in range(heads):
            cols=slice(h*HEAD_DIM,(h+1)*HEAD_DIM)
            qh=qs[:,cols]; doh=do_low[:,cols]
            rowdot=jnp.sum(prod[cols,:],0,keepdims=True)
            p=jnp.exp(dot_rows(ks[step],qh)+(bias[...]-lse_ref[h:h+1,:]))
            dp=dot_rows(vs[step],doh)
            ds=(p*(dp-rowdot)).astype(BF)
            dv=dv+dot(p.astype(BF),doh)
            dk=dk+dot(ds,qh)
            dq=dot(kts[step],ds)
            if step==0: gqt[cols,:]=dq
            else: gqt[cols,:]+=dq
        gkv_refs[step][:,:HEAD_DIM]=dk.astype(BF)
        gkv_refs[step][:,HEAD_DIM:]=dv.astype(BF)
    turned=turn_back(gqt[...]*(HEAD_DIM**-0.5),cos_ref[...],sin_ref[...],-1.0)
    gq_ref[...]=turned.T.astype(BF)

def attend_bwd(own,q,start,att_t,lse,gb,wo,cosines,sines,kvs):
    tokens,width=q.shape; n=len(kvs)
    outs=pl.pallas_call(functools.partial(bwd_kernel,n),
        out_shape=(jax.ShapeDtypeStruct((tokens,width),BF),)+(jax.ShapeDtypeStruct((tokens,2*HEAD_DIM),BF),)*n,
        in_specs=[IN_SMEM]+[IN_VMEM]*(8+n), out_specs=(IN_VMEM,)*(n+1),
        scratch_shapes=[pltpu.VMEM((tokens,tokens),F32),pltpu.VMEM((width,tokens),F32),pltpu.VMEM((8,128),F32)],
        compiler_params=pltpu.CompilerParams(vmem_limit_bytes=VMEM_BYTES),
        cost_estimate=FREE, name="attend_backward")(own,q,start,att_t,lse,gb,wo,cosines,sines,*kvs)
    return outs[0],list(outs[1:])


def prepare_kernel(count, chunk, own_ref, gate_ref, up_ref, down_ref, *refs):
    pieces, wide = refs[:count], refs[count]
    rows, hidden = gate_ref.shape
    span = chunk * count
    for number in range(3):
        wide[number, :, :hidden] = (gate_ref, up_ref, down_ref)[number][...]
        if span > hidden:
            wide[number, :, hidden:] = jnp.zeros((rows, span - hidden), BF)
    for step in range(count):
        begin = pl.multiple_of((own_ref[0] ^ step) * chunk, LANES)
        for number in range(3):
            pieces[step][:, number * chunk : (number + 1) * chunk] = wide[
                number, :, pl.ds(begin, chunk)
            ]


def prepare(own, w_gate, w_up, w_down, count, chunk):
    rows = w_gate.shape[0]
    outs = pl.pallas_call(
        functools.partial(prepare_kernel, count, chunk),
        out_shape=(jax.ShapeDtypeStruct((rows, 3 * chunk), BF),) * count,
        in_specs=[IN_SMEM] + [IN_VMEM] * 3,
        out_specs=(IN_VMEM,) * count,
        scratch_shapes=[pltpu.VMEM((3, rows, chunk * count), BF)],
        compiler_params=pltpu.CompilerParams(vmem_limit_bytes=VMEM_BYTES),
        cost_estimate=FREE,
        name="prepare",
    )(own, w_gate, w_up, w_down)
    return list(outs)


def weight_grad_kernel(count, lines, own_ref, left_ref, right_ref, *refs):
    pieces, whole = refs[:count], refs[count]
    whole[...] = turned_dot(left_ref[...], right_ref[...])
    rows = whole.shape[0] // (count * lines)
    for step in range(count):
        peer = own_ref[0] ^ step
        parts = []
        for line in range(lines):
            begin = pl.multiple_of((line * count + peer) * rows, 8)
            parts.append(whole[pl.ds(begin, rows), :])
        pieces[step][...] = jnp.concatenate(parts).astype(BF)


def weight_grad(own, left, right, count, lines):
    height, width = left.shape[1], right.shape[1]
    return list(
        pl.pallas_call(
            functools.partial(weight_grad_kernel, count, lines),
            out_shape=(jax.ShapeDtypeStruct((height // count, width), BF),) * count,
            in_specs=[IN_SMEM] + [IN_VMEM] * 2,
            out_specs=(IN_VMEM,) * count,
            scratch_shapes=[pltpu.VMEM((height, width), F32)],
            compiler_params=pltpu.CompilerParams(vmem_limit_bytes=VMEM_BYTES),
            cost_estimate=FREE,
            name="weight_grad",
        )(own, left, right)
    )


def last_grads_kernel(
    count, lines, own_ref, input_ref, gain_ref, qkv_ref, first_ref, second_ref, middle_ref,
    mlp_ref, out_ref, *refs
):
    pieces, whole, small = refs[:count], refs[count], refs[count + 1]
    features = input_ref.shape[1]
    inputs = input_ref[...].astype(F32)
    scale = lax.rsqrt(jnp.mean(inputs * inputs, -1, keepdims=True) + EPS)
    unit = inputs * scale
    gain = gain_ref[...]
    qkv = qkv_ref[...]
    whole[...] = turned_dot((unit * gain).astype(BF), qkv)
    grad = first_ref[...].astype(F32) + second_ref[...].astype(F32)
    turned = grad * unit
    small[...] = jnp.zeros_like(small)
    small[0:1, :] = jnp.sum(qkv.astype(F32), 0, keepdims=True)
    for row, values in ((1, jnp.sum(turned, 0, keepdims=True)), (3, mlp_ref[...])):
        small[row : row + 1, :SPLIT] = values[:, :SPLIT]
        small[row + 1 : row + 2, : features - SPLIT] = values[:, SPLIT:]
    along = jnp.mean(turned * gain, -1, keepdims=True)
    out_ref[...] = (middle_ref[...] + scale * (grad * gain - unit * along)).astype(BF)
    rows = features // (count * lines)
    for step in range(count):
        peer = own_ref[0] ^ step
        parts = []
        for line in range(lines):
            begin = pl.multiple_of((line * count + peer) * rows, 8)
            parts.append(whole[pl.ds(begin, rows), :])
        pieces[step][...] = jnp.concatenate(parts + [small[...]]).astype(BF)


def last_grads(own, inputs, gain, qkv, first, second, middle, mlp_gain_grad, count, lines):
    tokens, features = inputs.shape
    width = qkv.shape[1]
    outs = pl.pallas_call(
        functools.partial(last_grads_kernel, count, lines),
        out_shape=(jax.ShapeDtypeStruct((tokens, features), BF),)
        + (jax.ShapeDtypeStruct((features // count + SMALL_ROWS, width), BF),) * count,
        in_specs=[IN_SMEM] + [IN_VMEM] * 7,
        out_specs=(IN_VMEM,) * (count + 1),
        scratch_shapes=[pltpu.VMEM((features, width), F32), pltpu.VMEM((SMALL_ROWS, width), F32)],
        compiler_params=pltpu.CompilerParams(vmem_limit_bytes=VMEM_BYTES),
        cost_estimate=FREE,
        name="last_grads",
    )(own, inputs, gain, qkv, first, second, middle, mlp_gain_grad)
    return outs[0], list(outs[1:])


def pack_kernel(count, lines, own_ref, *refs):
    qkv_refs, o_refs = refs[:count], refs[count : 2 * count]
    outs = refs[2 * count : 2 * count + lines]
    qkv_sum, o_sum, block = refs[2 * count + lines :]
    qkv_sum[...] = sum(ref[...].astype(F32) for ref in qkv_refs)
    o_sum[...] = sum(ref[...].astype(F32) for ref in o_refs)
    rows = o_sum.shape[0] // lines
    width = qkv_sum.shape[1]
    block[rows:, :] = jnp.zeros((SMALL_ROWS, block.shape[1]), F32)
    block[rows:, :width] = qkv_sum[lines * rows :, :]
    for step in range(lines):
        begin = pl.multiple_of(lax.rem(own_ref[0] + step, lines) * rows, 8)
        block[:rows, :width] = qkv_sum[pl.ds(begin, rows), :]
        block[:rows, width:] = o_sum[pl.ds(begin, rows), :]
        outs[step][...] = block[...].astype(BF)


def pack(own_line, qkv_parts, o_parts, lines):
    count = len(qkv_parts)
    width, width_o = qkv_parts[0].shape[1], o_parts[0].shape[1]
    rows = o_parts[0].shape[0] // lines
    shape = (rows + SMALL_ROWS, width + width_o)
    return list(
        pl.pallas_call(
            functools.partial(pack_kernel, count, lines),
            out_shape=(jax.ShapeDtypeStruct(shape, BF),) * lines,
            in_specs=[IN_SMEM] + [IN_VMEM] * (2 * count),
            out_specs=(IN_VMEM,) * lines,
            scratch_shapes=[
                pltpu.VMEM(qkv_parts[0].shape, F32),
                pltpu.VMEM(o_parts[0].shape, F32),
                pltpu.VMEM(shape, F32),
            ],
            compiler_params=pltpu.CompilerParams(vmem_limit_bytes=VMEM_BYTES),
            cost_estimate=FREE,
            name="pack",
        )(own_line, *qkv_parts, *o_parts)
    )


def unpack_kernel(lines, widths, *refs):
    parts = refs[:lines]
    q_ref, k_ref, v_ref, o_ref, bq_ref, bk_ref, bv_ref, attn_ref, mlp_ref, total = refs[lines:]
    total[...] = sum(ref[...].astype(F32) for ref in parts)
    rows = q_ref.shape[0]
    first, second = widths[0], widths[0] + widths[1]
    third = second + widths[1]
    q_ref[...] = total[:rows, :first]
    k_ref[...] = total[:rows, first:second]
    v_ref[...] = total[:rows, second:third]
    o_ref[...] = total[:rows, third:]
    bq_ref[...] = total[rows : rows + 1, :first]
    bk_ref[...] = total[rows : rows + 1, first:second]
    bv_ref[...] = total[rows : rows + 1, second:third]
    for row, ref in ((rows + 1, attn_ref), (rows + 3, mlp_ref)):
        ref[:, :SPLIT] = total[row : row + 1, :SPLIT]
        ref[:, SPLIT:] = total[row + 1 : row + 2, : ref.shape[1] - SPLIT]


def unpack(parts, features, width_q, width_k):
    rows, width = parts[0].shape
    rows -= SMALL_ROWS
    width_o = width - width_q - 2 * width_k
    shapes = [
        (rows, width_q), (rows, width_k), (rows, width_k), (rows, width_o),
        (1, width_q), (1, width_k), (1, width_k), (1, features), (1, features),
    ]
    return pl.pallas_call(
        functools.partial(unpack_kernel, len(parts), (width_q, width_k)),
        out_shape=tuple(jax.ShapeDtypeStruct(shape, F32) for shape in shapes),
        in_specs=[IN_VMEM] * len(parts),
        out_specs=(IN_VMEM,) * len(shapes),
        scratch_shapes=[pltpu.VMEM(parts[0].shape, F32)],
        compiler_params=pltpu.CompilerParams(vmem_limit_bytes=VMEM_BYTES),
        cost_estimate=FREE,
        name="unpack",
    )(*parts)


def mlp_out_kernel(count, chunk, own_ref, *refs):
    parts = refs[:count]
    gate_ref, up_ref, down_ref, wide = refs[count:]
    rows, hidden = gate_ref.shape
    for step in range(count):
        begin = pl.multiple_of((own_ref[0] ^ step) * chunk, LANES)
        for number in range(3):
            wide[number, :, pl.ds(begin, chunk)] = parts[step][
                :, number * chunk : (number + 1) * chunk
            ].astype(F32)
    for number, ref in enumerate((gate_ref, up_ref, down_ref)):
        ref[...] = wide[number, :, :hidden]


def mlp_out(own, parts, hidden):
    count = len(parts)
    rows, width = parts[0].shape
    chunk = width // 3
    return pl.pallas_call(
        functools.partial(mlp_out_kernel, count, chunk),
        out_shape=(jax.ShapeDtypeStruct((rows, hidden), F32),) * 3,
        in_specs=[IN_SMEM] + [IN_VMEM] * count,
        out_specs=(IN_VMEM,) * 3,
        scratch_shapes=[pltpu.VMEM((3, rows, chunk * count), F32)],
        compiler_params=pltpu.CompilerParams(vmem_limit_bytes=VMEM_BYTES),
        cost_estimate=FREE,
        name="mlp_out",
    )(own, *parts)


def score_block(query_groups, key_rows, key_index, start, query_index):
    head_dim = query_groups.shape[-1]
    logits = jnp.einsum(
        "qgjd,kgd->gjqk", query_groups, key_rows, preferred_element_type=jnp.float32
    ) * head_dim ** (-0.5)
    allowed = (key_index[None, :] >= start[:, None]) & (key_index[None, :] <= query_index[:, None])
    return jnp.where(allowed, logits, NEG)


def key_window(keyval_all, number, key_block, key_heads):
    window = lax.dynamic_slice_in_dim(keyval_all, number * key_block, key_block, 0)
    width = window.shape[1] // 2
    key_rows = window[:, :width].reshape(key_block, key_heads, width // key_heads)
    value_rows = window[:, width:].reshape(key_block, key_heads, width // key_heads)
    key_index = number * key_block + jnp.arange(key_block, dtype=jnp.int32)
    return key_rows, value_rows, key_index


def repeat(count, step, state):
    if count == 1:
        return step(0, state)
    return lax.fori_loop(0, count, step, state)


def attend(query_rot, keyval_all, start, query_index, key_heads):
    tokens, head_count, head_dim = query_rot.shape
    group_size = head_count // key_heads
    key_block = min(keyval_all.shape[0], 1024)
    query_groups = query_rot.reshape(tokens, key_heads, group_size, head_dim)
    block_count = keyval_all.shape[0] // key_block

    def measure(number, state_pair):
        running_peak, running_total = state_pair
        key_rows, value_rows, key_index = key_window(
            keyval_all, number, key_block, key_heads
        )
        masked = score_block(query_groups, key_rows, key_index, start, query_index)
        fresh = jnp.maximum(running_peak, jnp.max(masked, -1))
        running_total = running_total * jnp.exp(running_peak - fresh) + jnp.sum(
            jnp.exp(masked - fresh[..., None]), -1
        )
        return (fresh, running_total)

    start_state = (
        jnp.full((key_heads, group_size, tokens), NEG, jnp.float32),
        jnp.zeros((key_heads, group_size, tokens), jnp.float32),
    )
    running_peak, running_total = repeat(block_count, measure, start_state)
    log_total = running_peak + jnp.log(running_total)

    def collect(number, summed):
        key_rows, value_rows, key_index = key_window(
            keyval_all, number, key_block, key_heads
        )
        masked = score_block(query_groups, key_rows, key_index, start, query_index)
        chances = jnp.exp(masked - log_total[..., None]).astype(jnp.bfloat16)
        return summed + jnp.einsum(
            "gjqk,kgd->gjqd", chances, value_rows, preferred_element_type=jnp.float32
        )

    summed = repeat(
        block_count, collect, jnp.zeros((key_heads, group_size, tokens, head_dim), jnp.float32)
    )
    return (summed.transpose(2, 0, 1, 3).reshape(tokens, head_count * head_dim), log_total)


def attend_back(
    query_rot,
    keyval_all,
    start,
    query_index,
    key_heads,
    log_total,
    attended,
    grad_attended,
):
    tokens, head_count, head_dim = query_rot.shape
    group_size = head_count // key_heads
    key_block = min(keyval_all.shape[0], 1024)
    query_groups = query_rot.reshape(tokens, key_heads, group_size, head_dim)
    grad_groups = grad_attended.reshape(tokens, key_heads, group_size, head_dim)
    block_count = keyval_all.shape[0] // key_block
    row_dot = jnp.sum(
        (grad_attended.astype(jnp.float32) * attended).reshape(
            tokens, key_heads, group_size, head_dim
        ),
        -1,
    ).transpose(1, 2, 0)
    score_scale = head_dim ** (-0.5)

    def step_back(number, state_pair):
        grad_query, grad_keyval = state_pair
        key_rows, value_rows, key_index = key_window(
            keyval_all, number, key_block, key_heads
        )
        masked = score_block(query_groups, key_rows, key_index, start, query_index)
        chances = jnp.exp(masked - log_total[..., None])
        chances_low = chances.astype(jnp.bfloat16)
        grad_chances = jnp.einsum(
            "qgjd,kgd->gjqk", grad_groups, value_rows, preferred_element_type=jnp.float32
        )
        grad_logits = (chances * (grad_chances - row_dot[..., None])).astype(jnp.bfloat16)
        grad_query = (
            grad_query
            + jnp.einsum(
                "gjqk,kgd->gjqd", grad_logits, key_rows, preferred_element_type=jnp.float32
            )
            * score_scale
        )
        grad_keys = (
            jnp.einsum(
                "gjqk,qgjd->kgd", grad_logits, query_groups, preferred_element_type=jnp.float32
            )
            * score_scale
        )
        grad_values = jnp.einsum(
            "gjqk,qgjd->kgd", chances_low, grad_groups, preferred_element_type=jnp.float32
        )
        grad_piece = jnp.concatenate(
            [
                grad_keys.reshape(key_block, key_heads * head_dim),
                grad_values.reshape(key_block, key_heads * head_dim),
            ],
            axis=-1,
        ).astype(jnp.bfloat16)
        grad_keyval = lax.dynamic_update_slice_in_dim(
            grad_keyval, grad_piece, number * key_block, 0
        )
        return (grad_query, grad_keyval)

    start_state = (
        jnp.zeros((key_heads, group_size, tokens, head_dim), jnp.float32),
        jnp.zeros(keyval_all.shape, jnp.bfloat16),
    )
    grad_query, grad_keyval = repeat(block_count, step_back, start_state)
    return (grad_query.transpose(2, 0, 1, 3).reshape(tokens, head_count, head_dim), grad_keyval)


def body(
    layer_input,
    segments,
    positions,
    attn_gain,
    w_q,
    b_q,
    w_k,
    b_k,
    w_v,
    b_v,
    w_o,
    mlp_gain,
    w_gate,
    w_up,
    w_down,
    cotangent,
):
    key_heads = w_k.shape[1] // HEAD_DIM
    head_count = w_q.shape[1] // HEAD_DIM
    width_q, width_k = w_q.shape[1], w_k.shape[1]
    tokens = layer_input.shape[1]
    ctx_size, fsdp_size = lax.axis_size("ctx"), lax.axis_size("fsdp")
    ctx_own = lax.axis_index("ctx")
    rows, hidden_count = w_gate.shape
    features = layer_input.shape[2]
    chunk = -(-hidden_count // (ctx_size * LANES)) * LANES
    width_qkv = width_q + 2 * width_k
    own = ctx_own.astype(jnp.int32)[None]

    attn_lined = direct_gather(jnp.concatenate([w_q, w_k, w_v, w_o.T], axis=1))

    if few():
        cuts = prepare(own, w_gate, w_up, w_down.T, ctx_size, chunk)
    else:
        tail = ((0, 0), (0, chunk * ctx_size - hidden_count))
        shards = [
            jnp.pad(shard, tail).reshape(rows, ctx_size, chunk) for shard in (w_gate, w_up, w_down.T)
        ]
        cuts = list(jnp.concatenate(shards, axis=-1).transpose(1, 0, 2))
    recut = untangle(trade(cuts)).reshape(ctx_size * rows, 3 * chunk)
    mlp_rows = lax.all_gather(recut, "fsdp", axis=0, tiled=True)

    def ordered(parts):
        pieces = untangle(parts)
        return pieces.transpose(1, 0, 2, 3).reshape(features, pieces.shape[-1])

    full_qkv = ordered(spread(attn_lined[..., :width_qkv]))
    o_pieces = spread(attn_lined[..., width_qkv:])

    inputs = layer_input[0].astype(jnp.float32)
    place = jnp.arange(tokens, dtype=jnp.int32)
    query_index = ctx_own * tokens + place
    grad_top = cotangent[0]
    cosines, sines = angles(positions[0], HEAD_DIM)
    scale_one = lax.rsqrt(jnp.mean(inputs * inputs, -1, keepdims=True) + EPS)
    unit_one = inputs * scale_one
    normed = (unit_one * attn_gain).astype(jnp.bfloat16)
    small_heads = few() and key_heads == 1 and tokens <= 256
    if small_heads:
        half = HEAD_DIM // 2
        cos_turned, sin_turned = cosines[:, 0, :half].T, sines[:, 0, :half].T
        query_flat, keyval = project(
            layer_input[0],
            attn_gain[None],
            full_qkv,
            jnp.concatenate([b_q, b_k, b_v])[None],
            cos_turned,
            sin_turned,
            segments,
            width_q,
            width_k,
        )
    else:
        projected = jnp.dot(normed, full_qkv, preferred_element_type=jnp.float32) + jnp.concatenate(
            [b_q, b_k, b_v]
        )
        queries = projected[:, :width_q]
        keyproj = projected[:, width_q : width_q + width_k]
        valproj = projected[:, width_q + width_k :]
        query_rot = rotate(queries.reshape(tokens, head_count, HEAD_DIM), cosines, sines).astype(
            jnp.bfloat16
        )
        key_rot = rotate(keyproj.reshape(tokens, key_heads, HEAD_DIM), cosines, sines).astype(
            jnp.bfloat16
        )
        keyval = jnp.concatenate(
            [key_rot.reshape(tokens, key_heads * HEAD_DIM), valproj.astype(jnp.bfloat16)], axis=-1
        )
    received = spread(keyval)
    full_o_turned = ordered(o_pieces)
    if small_heads:
        attended_low, attended_turned, log_total, start = attend_fwd(
            own, query_flat, segments, received
        )
    else:
        seg_own = segments[0]
        counts = jnp.stack([jnp.sum((seg_own <= number).astype(jnp.int32)) for number in range(2)])
        counts = lax.psum(counts, "ctx")
        start = jnp.where(seg_own == 0, 0, jnp.where(seg_own == 1, counts[0], counts[1]))
        order = untangle(received).reshape(ctx_size * tokens, 2 * width_k)
        attended, log_total = attend(query_rot, order, start, query_index, key_heads)
        attended_low = attended.astype(jnp.bfloat16)
    attended_low, grad_top_mine = lax.optimization_barrier(
        (attended_low, gather_half(after(grad_top, *received)))
    )
    branch_part = dot_rows(attended_low, full_o_turned).astype(jnp.bfloat16)
    middle = inputs + (
        branch_part.astype(jnp.float32) + swap_cores(branch_part).astype(jnp.float32)
    )
    scale_two = lax.rsqrt(jnp.mean(middle * middle, -1, keepdims=True) + EPS)
    unit_two = middle * scale_two
    normed_two = (unit_two * mlp_gain).astype(jnp.bfloat16)

    normed_mine = gather_half(normed_two)
    halves = [normed_mine, swap_cores(normed_mine)]
    tops = [grad_top_mine, swap_cores(grad_top_mine)]
    fsdp_own = lax.axis_index("fsdp").astype(jnp.int32)[None]

    gate_up, down_turned = mlp_rows[:, : 2 * chunk], mlp_rows[:, 2 * chunk :]
    normed_all, grad_top_all = jnp.concatenate(halves), jnp.concatenate(tops)
    gate_upward = dot(normed_all, gate_up)
    grad_hidden = dot(grad_top_all, down_turned)
    gate_values, upward = gate_upward[:, :chunk], gate_upward[:, chunk:]
    sigmoid_gate = jax.nn.sigmoid(gate_values)
    swish_gate = gate_values * sigmoid_gate
    hidden = (swish_gate * upward).astype(jnp.bfloat16)
    slope = sigmoid_gate + swish_gate * (1.0 - sigmoid_gate)
    grad_both = jnp.concatenate(
        [grad_hidden * upward * slope, grad_hidden * swish_gate], axis=-1
    ).astype(jnp.bfloat16)
    grad_one, grad_two = jnp.split(dot_rows(grad_both, gate_up).astype(jnp.bfloat16), 2)
    grad_normed_sum = add_cores(grad_one, grad_two)
    grad_normed_parts = trade(jnp.split(grad_normed_sum, ctx_size))
    mlp_grad = jnp.concatenate(
        [
            turned_dot(normed_all, grad_both).astype(jnp.bfloat16),
            turned_dot(grad_top_all, hidden).astype(jnp.bfloat16),
        ],
        axis=-1,
    ).reshape(fsdp_size, ctx_size * rows, 3 * chunk)
    mlp_mine = lax.psum_scatter(mlp_grad, "fsdp", scatter_dimension=0, tiled=False)
    branch_two_sum = add_cores(
        *jnp.split(dot_rows(hidden, down_turned).astype(jnp.bfloat16), 2)
    )
    branch_two_sum, *grad_normed_parts = lax.optimization_barrier(
        (branch_two_sum, *grad_normed_parts)
    )
    grad_normed_two = join_tokens(grad_normed_parts)
    branch_two_parts = trade(jnp.split(branch_two_sum, ctx_size))

    grad_mlp_gain = jnp.sum(grad_normed_two * unit_two, 0)
    grad_unit_two = grad_normed_two * mlp_gain
    grad_middle = grad_top.astype(jnp.float32) + scale_two * (
        grad_unit_two - unit_two * jnp.mean(grad_unit_two * unit_two, -1, keepdims=True)
    )
    grad_branch = grad_middle.astype(jnp.bfloat16)
    def owners(left, right):
        if few():
            return weight_grad(own, left, right, ctx_size, fsdp_size)
        grad = turned_dot(left, right).astype(jnp.bfloat16)
        cut = grad.reshape(fsdp_size, ctx_size, rows, right.shape[1]).transpose(1, 0, 2, 3)
        return list(cut.reshape(ctx_size, fsdp_size * rows, right.shape[1]))

    o_parts = trade(owners(grad_branch, attended_low))
    if small_heads:
        grad_query, grad_keyvals = attend_bwd(
            own,
            query_flat,
            start,
            attended_turned,
            log_total,
            grad_branch,
            full_o_turned,
            cos_turned,
            sin_turned,
            received,
        )
    else:
        grad_attended = dot(grad_branch, full_o_turned).astype(jnp.bfloat16)
        grad_query_rot, grad_keyvals = attend_back(
            query_rot,
            order,
            start,
            query_index,
            key_heads,
            log_total,
            attended,
            grad_attended,
        )
        grad_keyvals = choose(grad_keyvals.reshape(ctx_size, tokens, 2 * width_k))
    grad_keyvals[0], branch_two_parts = lax.optimization_barrier(
        (grad_keyvals[0], branch_two_parts)
    )
    grad_keyvals[0], o_parts[1] = lax.optimization_barrier((grad_keyvals[0], o_parts[1]))
    keyval_parts = trade(grad_keyvals)
    keyval_parts[0], o_parts = lax.optimization_barrier((keyval_parts[0], o_parts))
    branch_two = join_tokens(branch_two_parts)
    result = (middle + branch_two).astype(jnp.bfloat16)

    if small_heads:
        grad_qkv, grad_normed_part = key_grads(
            grad_query, full_qkv, cos_turned, sin_turned, keyval_parts
        )
    else:
        grad_keyval = sum(part.astype(F32) for part in keyval_parts)
        grad_query = (
            rotate(grad_query_rot, cosines, -sines)
            .reshape(tokens, head_count * HEAD_DIM)
            .astype(jnp.bfloat16)
        )
        grad_key = (
            rotate(
                grad_keyval[:, : key_heads * HEAD_DIM].reshape(tokens, key_heads, HEAD_DIM),
                cosines,
                -sines,
            )
            .reshape(tokens, key_heads * HEAD_DIM)
            .astype(jnp.bfloat16)
        )
        grad_value = grad_keyval[:, key_heads * HEAD_DIM :].astype(jnp.bfloat16)
        grad_qkv = jnp.concatenate([grad_query, grad_key, grad_value], axis=-1)
        grad_normed_part = dot_rows(grad_qkv, full_qkv).astype(jnp.bfloat16)
    grad_normed_other = swap_cores(grad_normed_part)
    if few():
        grad_inputs, qkv_pieces = last_grads(
            own,
            layer_input[0],
            attn_gain[None],
            grad_qkv,
            grad_normed_part,
            grad_normed_other,
            grad_middle,
            grad_mlp_gain[None],
            ctx_size,
            fsdp_size,
        )
    else:
        grad_normed = grad_normed_part.astype(F32) + grad_normed_other.astype(F32)
        turned = grad_normed * unit_one
        along = jnp.mean(turned * attn_gain, -1, keepdims=True)
        grad_inputs = grad_middle + scale_one * (grad_normed * attn_gain - unit_one * along)
        grad_inputs = grad_inputs.astype(jnp.bfloat16)
        lines = [jnp.sum(grad_qkv.astype(F32), 0)]
        for gains in (jnp.sum(turned, 0), grad_mlp_gain):
            for half in (gains[:SPLIT], gains[SPLIT:]):
                lines.append(jnp.pad(half, (0, width_qkv - half.shape[0])))
        small = jnp.pad(jnp.stack(lines), ((0, SMALL_ROWS - len(lines)), (0, 0)))
        small = small.astype(jnp.bfloat16)
        qkv_pieces = [jnp.concatenate([part, small]) for part in owners(normed, grad_qkv)]
    qkv_parts = trade(qkv_pieces)
    if few():
        packed = pack(fsdp_own, qkv_parts, o_parts, fsdp_size)
    else:
        qkv_sum = sum(part.astype(F32) for part in qkv_parts)
        o_sum = sum(part.astype(F32) for part in o_parts)
        small = jnp.pad(qkv_sum[fsdp_size * rows :], ((0, 0), (0, w_o.shape[0])))
        both = jnp.concatenate([qkv_sum[: fsdp_size * rows], o_sum], axis=-1)
        both = both.reshape(fsdp_size, rows, both.shape[-1])
        packed = [
            jnp.concatenate([both[(fsdp_own[0] + step) % fsdp_size], small]).astype(jnp.bfloat16)
            for step in range(fsdp_size)
        ]
    mlp_mine = mlp_mine.reshape(ctx_size, rows, 3 * chunk)
    packed = packed[:1] + [send_up(packed[step], step) for step in range(1, fsdp_size)]
    mlp_pieces = trade(choose(mlp_mine))
    if few():
        w_grads = unpack(packed, features, width_q, width_k)
        mlp_grads = mlp_out(own, mlp_pieces, hidden_count)
    else:
        total = sum(part.astype(F32) for part in packed)
        tops = [0, width_q, width_q + width_k, width_qkv]
        w_grads = [total[:rows, tops[k] : tops[k + 1]] for k in range(3)]
        w_grads.append(total[:rows, width_qkv:])
        w_grads += [total[rows, tops[k] : tops[k + 1]] for k in range(3)]
        for row in (rows + 1, rows + 3):
            w_grads.append(
                jnp.concatenate([total[row, :SPLIT], total[row + 1, : features - SPLIT]])
            )
        mlp_grads = []
        for number in range(3):
            pieces = untangle(mlp_pieces)[..., number * chunk : (number + 1) * chunk]
            wide = pieces.transpose(1, 0, 2).reshape(rows, chunk * ctx_size)
            mlp_grads.append(wide[:, :hidden_count].astype(F32))
    grad_q, grad_k, grad_v, grad_o = w_grads[:4]
    grad_b_q, grad_b_k, grad_b_v, grad_attn_gain, grad_mlp_gain = [
        values.reshape(-1) for values in w_grads[4:]
    ]
    return (
        result[None],
        grad_inputs[None],
        grad_attn_gain,
        grad_q,
        grad_b_q,
        grad_k,
        grad_b_k,
        grad_v,
        grad_b_v,
        grad_o.T,
        grad_mlp_gain,
        mlp_grads[0],
        mlp_grads[1],
        mlp_grads[2].T,
    )


def solution(mesh):
    placed = (
        P("fsdp", "ctx", None),
        P("fsdp", "ctx"),
        P("fsdp", "ctx"),
        P(),
        P(("fsdp", "ctx"), "tp"),
        P("tp"),
        P(("fsdp", "ctx"), "tp"),
        P("tp"),
        P(("fsdp", "ctx"), "tp"),
        P("tp"),
        P("tp", ("fsdp", "ctx")),
        P(),
        P(("fsdp", "ctx"), "tp"),
        P(("fsdp", "ctx"), "tp"),
        P("tp", ("fsdp", "ctx")),
        P("fsdp", "ctx", None),
    )
    return jax.shard_map(
        body,
        mesh=mesh,
        in_specs=placed,
        out_specs=(
            P("fsdp", "ctx", None),
            P("fsdp", "ctx", None),
            P(),
            P(("fsdp", "ctx"), "tp"),
            P("tp"),
            P(("fsdp", "ctx"), "tp"),
            P("tp"),
            P(("fsdp", "ctx"), "tp"),
            P("tp"),
            P("tp", ("fsdp", "ctx")),
            P(),
            P(("fsdp", "ctx"), "tp"),
            P(("fsdp", "ctx"), "tp"),
            P("tp", ("fsdp", "ctx")),
        ),
        check_vma=False,
    )
```

```python
import functools
import math

import jax
import jax.numpy as jnp
from jax import lax
from jax.experimental import pallas as pl
from jax.experimental.pallas import tpu as pltpu
from jax.sharding import PartitionSpec as P

HEAD_DIM = 64


EPS = 1e-06
THETA = 1000000.0
NEG = -1e30

LANES = 128
SPLIT = 512
SMALL_ROWS = 16
BLOCK = 512
MLP_VMEM = 32 * 2**20
VMEM_BYTES = 16 * 2**20
FREE = pl.CostEstimate(flops=0, bytes_accessed=0, transcendentals=0)
IN_VMEM = pl.BlockSpec(memory_space=pltpu.VMEM)
IN_SMEM = pl.BlockSpec(memory_space=pltpu.SMEM)
F32 = jnp.float32
BF = jnp.bfloat16


def dot(left, right):
    return jnp.dot(left, right, preferred_element_type=F32)


def dot_rows(left, right):
    return lax.dot_general(left, right, (((1,), (1,)), ((), ())), preferred_element_type=F32)


def turned_dot(left, right):
    return lax.dot_general(left, right, (((0,), (0,)), ((), ())), preferred_element_type=F32)


def rotate(values, cosines, sines):
    halfway = values.shape[-1] // 2
    turned = jnp.concatenate([-values[..., halfway:], values[..., :halfway]], axis=-1)
    return values * cosines + turned * sines


def angles(positions, head_dim):
    even_steps = jnp.arange(0, head_dim, 2).astype(jnp.float32)
    inverse = jnp.exp(-math.log(THETA) * even_steps / head_dim)
    phases = positions.astype(jnp.float32)[..., None] * inverse
    phases = jnp.concatenate([phases, phases], axis=-1)
    return (jnp.cos(phases)[..., None, :], jnp.sin(phases)[..., None, :])


def flips(size, step):
    return [(index, index ^ step) for index in range(size)]


def swap_cores(values):
    return lax.ppermute(values, "tp", flips(lax.axis_size("tp"), 1))


def few():
    return lax.axis_size("ctx") <= 8


def peers():
    size = lax.axis_size("ctx")
    if few():
        return [lax.axis_index("ctx") ^ step for step in range(size)]
    return list(range(size))


def spread(values):
    size = lax.axis_size("ctx")
    if not few():
        return list(lax.all_gather(values, "ctx"))
    return [values] + [lax.ppermute(values, "ctx", flips(size, step)) for step in range(1, size)]


def trade(parts):
    size = lax.axis_size("ctx")
    if not few():
        return list(lax.all_to_all(jnp.stack(parts), "ctx", 0, 0))
    return [parts[0]] + [
        lax.ppermute(parts[step], "ctx", flips(size, step)) for step in range(1, size)
    ]


def untangle(parts):
    if not few():
        return jnp.stack(parts)
    own = lax.axis_index("ctx")
    whole = jnp.stack(parts)
    return jnp.stack(
        [lax.dynamic_index_in_dim(whole, own ^ place, 0, keepdims=False) for place in range(len(parts))]
    )


def choose(whole):
    if not few():
        return list(whole)
    return [lax.dynamic_index_in_dim(whole, peer, 0, keepdims=False) for peer in peers()]


def after(values, *earlier):
    return lax.optimization_barrier((values,) + earlier)[0]


def direct_gather(values):
    size = lax.axis_size("fsdp")
    own = lax.axis_index("fsdp")
    pieces = [values] + [
        lax.ppermute(values, "fsdp", [(index, (index + step) % size) for index in range(size)])
        for step in range(1, size)
    ]
    pieces = pieces[::-1]
    line = jnp.stack(pieces + pieces[:-1])
    return lax.dynamic_slice_in_dim(line, size - 1 - own, size, 0)


def send_up(values, step):
    size = lax.axis_size("fsdp")
    return lax.ppermute(values, "fsdp", [(index, (index + step) % size) for index in range(size)])


def line_steps():
    size = lax.axis_size("fsdp")
    ups = [(index, index + 1) for index in range(size - 1)]
    downs = [(index + 1, index) for index in range(size - 1)]
    return ups, downs


def gather_step(line, step):
    ups, downs = line_steps()
    return (
        [lax.ppermute(line[0], "fsdp", ups[step:])]
        + line
        + [lax.ppermute(line[-1], "fsdp", downs[: len(downs) - step])]
    )


def gather_end(line):
    size = lax.axis_size("fsdp")
    return lax.dynamic_slice_in_dim(
        jnp.stack(line), size - 1 - lax.axis_index("fsdp"), size, 0
    )


def scatter_step(whole, sums, step):
    size = lax.axis_size("fsdp")
    own = lax.axis_index("fsdp")
    ups, downs = line_steps()
    pieces = [
        lax.dynamic_index_in_dim(whole, place, 0, keepdims=False)
        for place in (own + size - step, own - size + step)
    ]
    if sums:
        pieces = [piece + part for piece, part in zip(pieces, sums)]
    return [
        lax.ppermute(pieces[0], "fsdp", ups[:step]),
        lax.ppermute(pieces[1], "fsdp", downs[size - 1 - step :]),
    ]


def scatter_end(whole, sums):
    own = lax.dynamic_index_in_dim(whole, lax.axis_index("fsdp"), 0, keepdims=False)
    return sum(part.astype(F32) for part in [own] + sums)


def gather_half(values):
    half = values.shape[0] // 2
    return jnp.concatenate(
        spread(lax.dynamic_slice_in_dim(values, lax.axis_index("tp") * half, half, 0))
    )


def add_cores(mine, other):
    return (mine.astype(jnp.float32) + swap_cores(other).astype(jnp.float32)).astype(jnp.bfloat16)


def join_tokens(parts):
    own = sum(part.astype(jnp.float32) for part in parts).astype(jnp.bfloat16)
    other = swap_cores(own)
    first = lax.axis_index("tp") == 0
    return jnp.where(
        first, jnp.concatenate([own, other]), jnp.concatenate([other, own])
    ).astype(jnp.float32)


def turn_back(values, cosines, sines, sign):
    half = cosines.shape[0]
    parts = []
    for begin in range(0, values.shape[0], 2 * half):
        first = values[begin : begin + half]
        second = values[begin + half : begin + 2 * half]
        parts += [first * cosines - second * (sign * sines), second * cosines + first * (sign * sines)]
    return jnp.concatenate(parts)


def project_kernel(
    width_q, width_k, input_ref, gain_ref, w_ref, b_ref, cos_ref, sin_ref, seg_ref, q_ref, kv_ref
):
    inputs = input_ref[...].astype(F32)
    scale = lax.rsqrt(jnp.mean(inputs * inputs, -1, keepdims=True) + EPS)
    normed = (inputs * scale * gain_ref[...]).astype(BF)
    projected = dot(normed, w_ref[...]) + b_ref[...]
    rotated = turn_back(projected[:, : width_q + width_k].T, cos_ref[...], sin_ref[...], 1.0).T
    q_ref[...] = rotated[:, :width_q].astype(BF)
    tokens = q_ref.shape[0]
    kv_ref[:tokens, :width_k] = rotated[:, width_q:].astype(BF)
    kv_ref[:tokens, width_k:] = projected[:, width_q + width_k :].astype(BF)
    number = lax.broadcasted_iota(jnp.int32, (SMALL_ROWS, kv_ref.shape[1]), 0)
    counts = jnp.zeros(number.shape, F32)
    for row in range(2):
        below = jnp.sum((seg_ref[...] <= row).astype(F32), -1, keepdims=True)
        counts = jnp.where(number == row, below, counts)
    kv_ref[tokens:, :] = counts.astype(BF)


def project(inputs, gain, weights, biases, cosines, sines, segments, width_q, width_k):
    tokens = inputs.shape[0]
    return pl.pallas_call(
        functools.partial(project_kernel, width_q, width_k),
        out_shape=(
            jax.ShapeDtypeStruct((tokens, width_q), BF),
            jax.ShapeDtypeStruct((tokens + SMALL_ROWS, 2 * width_k), BF),
        ),
        in_specs=[IN_VMEM] * 7,
        out_specs=(IN_VMEM,) * 2,
        compiler_params=pltpu.CompilerParams(vmem_limit_bytes=VMEM_BYTES),
        cost_estimate=FREE,
        name="project",
    )(inputs, gain, weights, biases, cosines, sines, segments)


def key_grads_kernel(count, q_ref, w_ref, cos_ref, sin_ref, *refs):
    parts, qkv_ref, normed_ref = refs[:count], refs[count], refs[count + 1]
    width_q = q_ref.shape[1]
    total = sum(ref[...].astype(F32) for ref in parts)
    width_k = total.shape[1] // 2
    keys = turn_back(total[:, :width_k].T, cos_ref[...], sin_ref[...], -1.0).T
    qkv_ref[:, :width_q] = q_ref[...]
    qkv_ref[:, width_q : width_q + width_k] = keys.astype(BF)
    qkv_ref[:, width_q + width_k :] = total[:, width_k:].astype(BF)
    normed_ref[...] = dot_rows(qkv_ref[...], w_ref[...]).astype(BF)


def key_grads(grad_query, weights, cosines, sines, parts):
    tokens = grad_query.shape[0]
    features, width = weights.shape
    return pl.pallas_call(
        functools.partial(key_grads_kernel, len(parts)),
        out_shape=(
            jax.ShapeDtypeStruct((tokens, width), BF),
            jax.ShapeDtypeStruct((tokens, features), BF),
        ),
        in_specs=[IN_VMEM] * (4 + len(parts)),
        out_specs=(IN_VMEM,) * 2,
        compiler_params=pltpu.CompilerParams(vmem_limit_bytes=VMEM_BYTES),
        cost_estimate=FREE,
        name="key_grads",
    )(grad_query, weights, cosines, sines, *parts)


def masks(start, tokens, own, step):
    peer = own ^ step
    key = peer*tokens + lax.broadcasted_iota(jnp.int32,(tokens,tokens),0)
    query = own*tokens + lax.broadcasted_iota(jnp.int32,(tokens,tokens),1)
    return jnp.where((key>=start)&(key<=query),0.0,NEG).astype(F32)

def fwd_kernel(count, own_ref, q_ref, seg_ref, *refs):
    kv_refs=refs[:count]; att_ref, att_t_ref, lse_ref, start_ref, bias, s_ref = refs[count:]
    own=own_ref[0]
    tokens=q_ref.shape[0]; heads=q_ref.shape[1]//HEAD_DIM
    counts=sum(r[tokens:,:].astype(F32) for r in kv_refs).astype(jnp.int32)
    seg=seg_ref[...]
    start=jnp.where(seg==0,0,jnp.where(seg==1,counts[0:1,0:1],counts[1:2,0:1]))
    start_ref[...]=start
    for step in range(count):
        bias[step*tokens:(step+1)*tokens,:]=masks(start,tokens,own,step)
    q=q_ref[...]*jnp.asarray(HEAD_DIM**-0.5,BF)
    ks=[r[:tokens,:HEAD_DIM] for r in kv_refs]
    vts=[r[:tokens,HEAD_DIM:].astype(F32).T.astype(BF) for r in kv_refs]
    for h in range(heads):
        qh=q[:,h*HEAD_DIM:(h+1)*HEAD_DIM]
        peak=jnp.full((1,tokens),NEG,F32)
        for step in range(count):
            rows=slice(step*tokens,(step+1)*tokens)
            s=dot_rows(ks[step],qh)+bias[rows,:]
            s_ref[h%2,rows,:]=s
            peak=jnp.maximum(peak,jnp.max(s,0,keepdims=True))
        total=jnp.zeros((1,tokens),F32)
        out=jnp.zeros((HEAD_DIM,tokens),F32)
        for step in range(count):
            rows=slice(step*tokens,(step+1)*tokens)
            p=jnp.exp(s_ref[h%2,rows,:]-peak)
            total=total+jnp.sum(p,0,keepdims=True)
            out=out+dot(vts[step],p.astype(BF))
        att_t_ref[h*HEAD_DIM:(h+1)*HEAD_DIM,:]=out/total
        lse_ref[h:h+1,:]=peak+jnp.log(total)
    att_ref[...]=att_t_ref[...].T.astype(BF)

def attend_fwd(own, q, segments, kvs):
    tokens,width=q.shape; heads=width//HEAD_DIM; n=len(kvs)
    return pl.pallas_call(functools.partial(fwd_kernel,n),
        out_shape=(jax.ShapeDtypeStruct((tokens,width),BF),jax.ShapeDtypeStruct((width,tokens),F32),jax.ShapeDtypeStruct((heads,tokens),F32),jax.ShapeDtypeStruct((1,tokens),jnp.int32)),
        in_specs=[IN_SMEM]+[IN_VMEM]*(2+n), out_specs=(IN_VMEM,)*4,
        scratch_shapes=[pltpu.VMEM((n*tokens,tokens),F32),pltpu.VMEM((2,n*tokens,tokens),F32)],
        compiler_params=pltpu.CompilerParams(vmem_limit_bytes=VMEM_BYTES),
        cost_estimate=FREE, name="attend_forward")(own,q,segments,*kvs)

def bwd_kernel(
    count, own_ref, q_ref, start_ref, att_t_ref, lse_ref, gb_ref, wo_ref, cos_ref, sin_ref, *refs
):
    kv_refs=refs[:count]; gq_ref=refs[count]; gkv_refs=refs[count+1:2*count+1]; bias, gqt, dkv = refs[2*count+1:]
    own=own_ref[0]
    tokens=q_ref.shape[0]; heads=q_ref.shape[1]//HEAD_DIM
    start=start_ref[...]
    do=dot(gb_ref[...],wo_ref[...])
    do_low=do.astype(BF)
    do_t=do_low.astype(F32).T
    prod=do_t*att_t_ref[...]
    q=q_ref[...]
    qs=q*jnp.asarray(HEAD_DIM**-0.5,BF)
    ks=[r[:tokens,:HEAD_DIM] for r in kv_refs]
    vs=[r[:tokens,HEAD_DIM:] for r in kv_refs]
    kts=[k.astype(F32).T.astype(BF) for k in ks]
    dot_low=do_t.astype(BF)
    for step in range(count):
        bias[...]=masks(start,tokens,own,step)
        dk=jnp.zeros((tokens,HEAD_DIM),F32); dv=jnp.zeros((tokens,HEAD_DIM),F32)
        for h in range(heads):
            cols=slice(h*HEAD_DIM,(h+1)*HEAD_DIM)
            qh=qs[:,cols]; doh=do_low[:,cols]
            rowdot=jnp.sum(prod[cols,:],0,keepdims=True)
            p=jnp.exp(dot_rows(ks[step],qh)+(bias[...]-lse_ref[h:h+1,:]))
            dp=dot_rows(vs[step],doh)
            ds=(p*(dp-rowdot)).astype(BF)
            dv=dv+dot(p.astype(BF),doh)
            dk=dk+dot(ds,qh)
            dq=dot(kts[step],ds)
            if step==0: gqt[cols,:]=dq
            else: gqt[cols,:]+=dq
        gkv_refs[step][:,:HEAD_DIM]=dk.astype(BF)
        gkv_refs[step][:,HEAD_DIM:]=dv.astype(BF)
    turned=turn_back(gqt[...]*(HEAD_DIM**-0.5),cos_ref[...],sin_ref[...],-1.0)
    gq_ref[...]=turned.T.astype(BF)

def attend_bwd(own,q,start,att_t,lse,gb,wo,cosines,sines,kvs):
    tokens,width=q.shape; n=len(kvs)
    outs=pl.pallas_call(functools.partial(bwd_kernel,n),
        out_shape=(jax.ShapeDtypeStruct((tokens,width),BF),)+(jax.ShapeDtypeStruct((tokens,2*HEAD_DIM),BF),)*n,
        in_specs=[IN_SMEM]+[IN_VMEM]*(8+n), out_specs=(IN_VMEM,)*(n+1),
        scratch_shapes=[pltpu.VMEM((tokens,tokens),F32),pltpu.VMEM((width,tokens),F32),pltpu.VMEM((8,128),F32)],
        compiler_params=pltpu.CompilerParams(vmem_limit_bytes=VMEM_BYTES),
        cost_estimate=FREE, name="attend_backward")(own,q,start,att_t,lse,gb,wo,cosines,sines,*kvs)
    return outs[0],list(outs[1:])


def prepare_kernel(count, chunk, own_ref, gate_ref, up_ref, down_ref, *refs):
    pieces, wide = refs[:count], refs[count]
    rows, hidden = gate_ref.shape
    span = chunk * count
    for number in range(3):
        wide[number, :, :hidden] = (gate_ref, up_ref, down_ref)[number][...]
        if span > hidden:
            wide[number, :, hidden:] = jnp.zeros((rows, span - hidden), BF)
    for step in range(count):
        begin = pl.multiple_of((own_ref[0] ^ step) * chunk, LANES)
        for number in range(3):
            pieces[step][:, number * chunk : (number + 1) * chunk] = wide[
                number, :, pl.ds(begin, chunk)
            ]


def prepare(own, w_gate, w_up, w_down, count, chunk):
    rows = w_gate.shape[0]
    outs = pl.pallas_call(
        functools.partial(prepare_kernel, count, chunk),
        out_shape=(jax.ShapeDtypeStruct((rows, 3 * chunk), BF),) * count,
        in_specs=[IN_SMEM] + [IN_VMEM] * 3,
        out_specs=(IN_VMEM,) * count,
        scratch_shapes=[pltpu.VMEM((3, rows, chunk * count), BF)],
        compiler_params=pltpu.CompilerParams(vmem_limit_bytes=VMEM_BYTES),
        cost_estimate=FREE,
        name="prepare",
    )(own, w_gate, w_up, w_down)
    return list(outs)


def mlp_kernel(chunk, first_ref, second_ref, top_one_ref, top_two_ref, weights, *refs):
    grad_one_ref, grad_two_ref, hidden_ref, both_ref = refs
    rows = first_ref.shape[0]
    block = min(rows, BLOCK)
    for half, (tokens_ref, top_ref, grad_ref) in enumerate(
        ((first_ref, top_one_ref, grad_one_ref), (second_ref, top_two_ref, grad_two_ref))
    ):
        for begin in range(0, rows, block):
            here = slice(begin, begin + block)
            there = slice(half * rows + begin, half * rows + begin + block)
            gate_up = dot(tokens_ref[here, :], weights[:, : 2 * chunk])
            grad_hidden = dot(top_ref[here, :], weights[:, 2 * chunk :])
            gate, upward = gate_up[:, :chunk], gate_up[:, chunk:]
            sigmoid = jax.nn.sigmoid(gate)
            swish = gate * sigmoid
            hidden_ref[there, :] = (swish * upward).astype(BF)
            slope = sigmoid + swish * (1.0 - sigmoid)
            both_ref[there, :chunk] = (grad_hidden * upward * slope).astype(BF)
            both_ref[there, chunk:] = (grad_hidden * swish).astype(BF)
            grad_ref[here, :] = dot_rows(both_ref[there, :], weights[:, : 2 * chunk]).astype(BF)


def mlp(halves, tops, weights, chunk):
    rows, features = halves[0].shape
    return pl.pallas_call(
        functools.partial(mlp_kernel, chunk),
        out_shape=(jax.ShapeDtypeStruct((rows, features), BF),) * 2
        + (
            jax.ShapeDtypeStruct((2 * rows, chunk), BF),
            jax.ShapeDtypeStruct((2 * rows, 2 * chunk), BF),
        ),
        in_specs=[IN_VMEM] * 5,
        out_specs=(IN_VMEM,) * 4,
        compiler_params=pltpu.CompilerParams(vmem_limit_bytes=MLP_VMEM),
        cost_estimate=FREE,
        name="mlp",
    )(*halves, *tops, weights)


def weight_grad_kernel(count, lines, own_ref, left_ref, right_ref, *refs):
    pieces, whole = refs[:count], refs[count]
    whole[...] = turned_dot(left_ref[...], right_ref[...])
    rows = whole.shape[0] // (count * lines)
    for step in range(count):
        peer = own_ref[0] ^ step
        parts = []
        for line in range(lines):
            begin = pl.multiple_of((line * count + peer) * rows, 8)
            parts.append(whole[pl.ds(begin, rows), :])
        pieces[step][...] = jnp.concatenate(parts).astype(BF)


def weight_grad(own, left, right, count, lines):
    height, width = left.shape[1], right.shape[1]
    return list(
        pl.pallas_call(
            functools.partial(weight_grad_kernel, count, lines),
            out_shape=(jax.ShapeDtypeStruct((height // count, width), BF),) * count,
            in_specs=[IN_SMEM] + [IN_VMEM] * 2,
            out_specs=(IN_VMEM,) * count,
            scratch_shapes=[pltpu.VMEM((height, width), F32)],
            compiler_params=pltpu.CompilerParams(vmem_limit_bytes=VMEM_BYTES),
            cost_estimate=FREE,
            name="weight_grad",
        )(own, left, right)
    )


def last_grads_kernel(
    count, lines, own_ref, input_ref, gain_ref, qkv_ref, first_ref, second_ref, middle_ref,
    mlp_ref, out_ref, *refs
):
    pieces, whole, small = refs[:count], refs[count], refs[count + 1]
    features = input_ref.shape[1]
    inputs = input_ref[...].astype(F32)
    scale = lax.rsqrt(jnp.mean(inputs * inputs, -1, keepdims=True) + EPS)
    unit = inputs * scale
    gain = gain_ref[...]
    qkv = qkv_ref[...]
    whole[...] = turned_dot((unit * gain).astype(BF), qkv)
    grad = first_ref[...].astype(F32) + second_ref[...].astype(F32)
    turned = grad * unit
    small[...] = jnp.zeros_like(small)
    small[0:1, :] = jnp.sum(qkv.astype(F32), 0, keepdims=True)
    for row, values in ((1, jnp.sum(turned, 0, keepdims=True)), (3, mlp_ref[...])):
        small[row : row + 1, :SPLIT] = values[:, :SPLIT]
        small[row + 1 : row + 2, : features - SPLIT] = values[:, SPLIT:]
    along = jnp.mean(turned * gain, -1, keepdims=True)
    out_ref[...] = (middle_ref[...] + scale * (grad * gain - unit * along)).astype(BF)
    rows = features // (count * lines)
    for step in range(count):
        peer = own_ref[0] ^ step
        parts = []
        for line in range(lines):
            begin = pl.multiple_of((line * count + peer) * rows, 8)
            parts.append(whole[pl.ds(begin, rows), :])
        pieces[step][...] = jnp.concatenate(parts + [small[...]]).astype(BF)


def last_grads(own, inputs, gain, qkv, first, second, middle, mlp_gain_grad, count, lines):
    tokens, features = inputs.shape
    width = qkv.shape[1]
    outs = pl.pallas_call(
        functools.partial(last_grads_kernel, count, lines),
        out_shape=(jax.ShapeDtypeStruct((tokens, features), BF),)
        + (jax.ShapeDtypeStruct((features // count + SMALL_ROWS, width), BF),) * count,
        in_specs=[IN_SMEM] + [IN_VMEM] * 7,
        out_specs=(IN_VMEM,) * (count + 1),
        scratch_shapes=[pltpu.VMEM((features, width), F32), pltpu.VMEM((SMALL_ROWS, width), F32)],
        compiler_params=pltpu.CompilerParams(vmem_limit_bytes=VMEM_BYTES),
        cost_estimate=FREE,
        name="last_grads",
    )(own, inputs, gain, qkv, first, second, middle, mlp_gain_grad)
    return outs[0], list(outs[1:])


def pack_kernel(count, lines, own_ref, *refs):
    qkv_refs, o_refs = refs[:count], refs[count : 2 * count]
    outs = refs[2 * count : 2 * count + lines]
    qkv_sum, o_sum, block = refs[2 * count + lines :]
    qkv_sum[...] = sum(ref[...].astype(F32) for ref in qkv_refs)
    o_sum[...] = sum(ref[...].astype(F32) for ref in o_refs)
    rows = o_sum.shape[0] // lines
    width = qkv_sum.shape[1]
    block[rows:, :] = jnp.zeros((SMALL_ROWS, block.shape[1]), F32)
    block[rows:, :width] = qkv_sum[lines * rows :, :]
    for step in range(lines):
        begin = pl.multiple_of(lax.rem(own_ref[0] + step, lines) * rows, 8)
        block[:rows, :width] = qkv_sum[pl.ds(begin, rows), :]
        block[:rows, width:] = o_sum[pl.ds(begin, rows), :]
        outs[step][...] = block[...].astype(BF)


def pack(own_line, qkv_parts, o_parts, lines):
    count = len(qkv_parts)
    width, width_o = qkv_parts[0].shape[1], o_parts[0].shape[1]
    rows = o_parts[0].shape[0] // lines
    shape = (rows + SMALL_ROWS, width + width_o)
    return list(
        pl.pallas_call(
            functools.partial(pack_kernel, count, lines),
            out_shape=(jax.ShapeDtypeStruct(shape, BF),) * lines,
            in_specs=[IN_SMEM] + [IN_VMEM] * (2 * count),
            out_specs=(IN_VMEM,) * lines,
            scratch_shapes=[
                pltpu.VMEM(qkv_parts[0].shape, F32),
                pltpu.VMEM(o_parts[0].shape, F32),
                pltpu.VMEM(shape, F32),
            ],
            compiler_params=pltpu.CompilerParams(vmem_limit_bytes=VMEM_BYTES),
            cost_estimate=FREE,
            name="pack",
        )(own_line, *qkv_parts, *o_parts)
    )


def unpack_kernel(lines, widths, *refs):
    parts = refs[:lines]
    q_ref, k_ref, v_ref, o_ref, bq_ref, bk_ref, bv_ref, attn_ref, mlp_ref, total = refs[lines:]
    total[...] = sum(ref[...].astype(F32) for ref in parts)
    rows = q_ref.shape[0]
    first, second = widths[0], widths[0] + widths[1]
    third = second + widths[1]
    q_ref[...] = total[:rows, :first]
    k_ref[...] = total[:rows, first:second]
    v_ref[...] = total[:rows, second:third]
    o_ref[...] = total[:rows, third:]
    bq_ref[...] = total[rows : rows + 1, :first]
    bk_ref[...] = total[rows : rows + 1, first:second]
    bv_ref[...] = total[rows : rows + 1, second:third]
    for row, ref in ((rows + 1, attn_ref), (rows + 3, mlp_ref)):
        ref[:, :SPLIT] = total[row : row + 1, :SPLIT]
        ref[:, SPLIT:] = total[row + 1 : row + 2, : ref.shape[1] - SPLIT]


def unpack(parts, features, width_q, width_k):
    rows, width = parts[0].shape
    rows -= SMALL_ROWS
    width_o = width - width_q - 2 * width_k
    shapes = [
        (rows, width_q), (rows, width_k), (rows, width_k), (rows, width_o),
        (1, width_q), (1, width_k), (1, width_k), (1, features), (1, features),
    ]
    return pl.pallas_call(
        functools.partial(unpack_kernel, len(parts), (width_q, width_k)),
        out_shape=tuple(jax.ShapeDtypeStruct(shape, F32) for shape in shapes),
        in_specs=[IN_VMEM] * len(parts),
        out_specs=(IN_VMEM,) * len(shapes),
        scratch_shapes=[pltpu.VMEM(parts[0].shape, F32)],
        compiler_params=pltpu.CompilerParams(vmem_limit_bytes=VMEM_BYTES),
        cost_estimate=FREE,
        name="unpack",
    )(*parts)


def mlp_out_kernel(count, chunk, own_ref, *refs):
    parts = refs[:count]
    gate_ref, up_ref, down_ref, wide = refs[count:]
    rows, hidden = gate_ref.shape
    for step in range(count):
        begin = pl.multiple_of((own_ref[0] ^ step) * chunk, LANES)
        for number in range(3):
            wide[number, :, pl.ds(begin, chunk)] = parts[step][
                :, number * chunk : (number + 1) * chunk
            ].astype(F32)
    for number, ref in enumerate((gate_ref, up_ref, down_ref)):
        ref[...] = wide[number, :, :hidden]


def mlp_out(own, parts, hidden):
    count = len(parts)
    rows, width = parts[0].shape
    chunk = width // 3
    return pl.pallas_call(
        functools.partial(mlp_out_kernel, count, chunk),
        out_shape=(jax.ShapeDtypeStruct((rows, hidden), F32),) * 3,
        in_specs=[IN_SMEM] + [IN_VMEM] * count,
        out_specs=(IN_VMEM,) * 3,
        scratch_shapes=[pltpu.VMEM((3, rows, chunk * count), F32)],
        compiler_params=pltpu.CompilerParams(vmem_limit_bytes=VMEM_BYTES),
        cost_estimate=FREE,
        name="mlp_out",
    )(own, *parts)


def score_block(query_groups, key_rows, key_index, start, query_index):
    head_dim = query_groups.shape[-1]
    logits = jnp.einsum(
        "qgjd,kgd->gjqk", query_groups, key_rows, preferred_element_type=jnp.float32
    ) * head_dim ** (-0.5)
    allowed = (key_index[None, :] >= start[:, None]) & (key_index[None, :] <= query_index[:, None])
    return jnp.where(allowed, logits, NEG)


def key_window(keyval_all, number, key_block, key_heads):
    window = lax.dynamic_slice_in_dim(keyval_all, number * key_block, key_block, 0)
    width = window.shape[1] // 2
    key_rows = window[:, :width].reshape(key_block, key_heads, width // key_heads)
    value_rows = window[:, width:].reshape(key_block, key_heads, width // key_heads)
    key_index = number * key_block + jnp.arange(key_block, dtype=jnp.int32)
    return key_rows, value_rows, key_index


def repeat(count, step, state):
    if count == 1:
        return step(0, state)
    return lax.fori_loop(0, count, step, state)


def attend(query_rot, keyval_all, start, query_index, key_heads):
    tokens, head_count, head_dim = query_rot.shape
    group_size = head_count // key_heads
    key_block = min(keyval_all.shape[0], 1024)
    query_groups = query_rot.reshape(tokens, key_heads, group_size, head_dim)
    block_count = keyval_all.shape[0] // key_block

    def measure(number, state_pair):
        running_peak, running_total = state_pair
        key_rows, value_rows, key_index = key_window(
            keyval_all, number, key_block, key_heads
        )
        masked = score_block(query_groups, key_rows, key_index, start, query_index)
        fresh = jnp.maximum(running_peak, jnp.max(masked, -1))
        running_total = running_total * jnp.exp(running_peak - fresh) + jnp.sum(
            jnp.exp(masked - fresh[..., None]), -1
        )
        return (fresh, running_total)

    start_state = (
        jnp.full((key_heads, group_size, tokens), NEG, jnp.float32),
        jnp.zeros((key_heads, group_size, tokens), jnp.float32),
    )
    running_peak, running_total = repeat(block_count, measure, start_state)
    log_total = running_peak + jnp.log(running_total)

    def collect(number, summed):
        key_rows, value_rows, key_index = key_window(
            keyval_all, number, key_block, key_heads
        )
        masked = score_block(query_groups, key_rows, key_index, start, query_index)
        chances = jnp.exp(masked - log_total[..., None]).astype(jnp.bfloat16)
        return summed + jnp.einsum(
            "gjqk,kgd->gjqd", chances, value_rows, preferred_element_type=jnp.float32
        )

    summed = repeat(
        block_count, collect, jnp.zeros((key_heads, group_size, tokens, head_dim), jnp.float32)
    )
    return (summed.transpose(2, 0, 1, 3).reshape(tokens, head_count * head_dim), log_total)


def attend_back(
    query_rot,
    keyval_all,
    start,
    query_index,
    key_heads,
    log_total,
    attended,
    grad_attended,
):
    tokens, head_count, head_dim = query_rot.shape
    group_size = head_count // key_heads
    key_block = min(keyval_all.shape[0], 1024)
    query_groups = query_rot.reshape(tokens, key_heads, group_size, head_dim)
    grad_groups = grad_attended.reshape(tokens, key_heads, group_size, head_dim)
    block_count = keyval_all.shape[0] // key_block
    row_dot = jnp.sum(
        (grad_attended.astype(jnp.float32) * attended).reshape(
            tokens, key_heads, group_size, head_dim
        ),
        -1,
    ).transpose(1, 2, 0)
    score_scale = head_dim ** (-0.5)

    def step_back(number, state_pair):
        grad_query, grad_keyval = state_pair
        key_rows, value_rows, key_index = key_window(
            keyval_all, number, key_block, key_heads
        )
        masked = score_block(query_groups, key_rows, key_index, start, query_index)
        chances = jnp.exp(masked - log_total[..., None])
        chances_low = chances.astype(jnp.bfloat16)
        grad_chances = jnp.einsum(
            "qgjd,kgd->gjqk", grad_groups, value_rows, preferred_element_type=jnp.float32
        )
        grad_logits = (chances * (grad_chances - row_dot[..., None])).astype(jnp.bfloat16)
        grad_query = (
            grad_query
            + jnp.einsum(
                "gjqk,kgd->gjqd", grad_logits, key_rows, preferred_element_type=jnp.float32
            )
            * score_scale
        )
        grad_keys = (
            jnp.einsum(
                "gjqk,qgjd->kgd", grad_logits, query_groups, preferred_element_type=jnp.float32
            )
            * score_scale
        )
        grad_values = jnp.einsum(
            "gjqk,qgjd->kgd", chances_low, grad_groups, preferred_element_type=jnp.float32
        )
        grad_piece = jnp.concatenate(
            [
                grad_keys.reshape(key_block, key_heads * head_dim),
                grad_values.reshape(key_block, key_heads * head_dim),
            ],
            axis=-1,
        ).astype(jnp.bfloat16)
        grad_keyval = lax.dynamic_update_slice_in_dim(
            grad_keyval, grad_piece, number * key_block, 0
        )
        return (grad_query, grad_keyval)

    start_state = (
        jnp.zeros((key_heads, group_size, tokens, head_dim), jnp.float32),
        jnp.zeros(keyval_all.shape, jnp.bfloat16),
    )
    grad_query, grad_keyval = repeat(block_count, step_back, start_state)
    return (grad_query.transpose(2, 0, 1, 3).reshape(tokens, head_count, head_dim), grad_keyval)


def body(
    layer_input,
    segments,
    positions,
    attn_gain,
    w_q,
    b_q,
    w_k,
    b_k,
    w_v,
    b_v,
    w_o,
    mlp_gain,
    w_gate,
    w_up,
    w_down,
    cotangent,
):
    key_heads = w_k.shape[1] // HEAD_DIM
    head_count = w_q.shape[1] // HEAD_DIM
    width_q, width_k = w_q.shape[1], w_k.shape[1]
    tokens = layer_input.shape[1]
    ctx_size, fsdp_size = lax.axis_size("ctx"), lax.axis_size("fsdp")
    ctx_own = lax.axis_index("ctx")
    rows, hidden_count = w_gate.shape
    features = layer_input.shape[2]
    chunk = -(-hidden_count // (ctx_size * LANES)) * LANES
    width_qkv = width_q + 2 * width_k
    own = ctx_own.astype(jnp.int32)[None]

    attn_lined = direct_gather(jnp.concatenate([w_q, w_k, w_v, w_o.T], axis=1))

    if few():
        cuts = prepare(own, w_gate, w_up, w_down.T, ctx_size, chunk)
    else:
        tail = ((0, 0), (0, chunk * ctx_size - hidden_count))
        shards = [
            jnp.pad(shard, tail).reshape(rows, ctx_size, chunk) for shard in (w_gate, w_up, w_down.T)
        ]
        cuts = list(jnp.concatenate(shards, axis=-1).transpose(1, 0, 2))
    recut = untangle(trade(cuts)).reshape(ctx_size * rows, 3 * chunk)
    mlp_rows = lax.all_gather(recut, "fsdp", axis=0, tiled=True)

    def ordered(parts):
        pieces = untangle(parts)
        return pieces.transpose(1, 0, 2, 3).reshape(features, pieces.shape[-1])

    full_qkv = ordered(spread(attn_lined[..., :width_qkv]))
    o_pieces = spread(attn_lined[..., width_qkv:])

    inputs = layer_input[0].astype(jnp.float32)
    place = jnp.arange(tokens, dtype=jnp.int32)
    query_index = ctx_own * tokens + place
    grad_top = cotangent[0]
    cosines, sines = angles(positions[0], HEAD_DIM)
    scale_one = lax.rsqrt(jnp.mean(inputs * inputs, -1, keepdims=True) + EPS)
    unit_one = inputs * scale_one
    normed = (unit_one * attn_gain).astype(jnp.bfloat16)
    small_heads = few() and key_heads == 1 and tokens <= 256
    if small_heads:
        half = HEAD_DIM // 2
        cos_turned, sin_turned = cosines[:, 0, :half].T, sines[:, 0, :half].T
        query_flat, keyval = project(
            layer_input[0],
            attn_gain[None],
            full_qkv,
            jnp.concatenate([b_q, b_k, b_v])[None],
            cos_turned,
            sin_turned,
            segments,
            width_q,
            width_k,
        )
    else:
        projected = jnp.dot(normed, full_qkv, preferred_element_type=jnp.float32) + jnp.concatenate(
            [b_q, b_k, b_v]
        )
        queries = projected[:, :width_q]
        keyproj = projected[:, width_q : width_q + width_k]
        valproj = projected[:, width_q + width_k :]
        query_rot = rotate(queries.reshape(tokens, head_count, HEAD_DIM), cosines, sines).astype(
            jnp.bfloat16
        )
        key_rot = rotate(keyproj.reshape(tokens, key_heads, HEAD_DIM), cosines, sines).astype(
            jnp.bfloat16
        )
        keyval = jnp.concatenate(
            [key_rot.reshape(tokens, key_heads * HEAD_DIM), valproj.astype(jnp.bfloat16)], axis=-1
        )
    received = spread(keyval)
    full_o_turned = ordered(o_pieces)
    if small_heads:
        attended_low, attended_turned, log_total, start = attend_fwd(
            own, query_flat, segments, received
        )
    else:
        seg_own = segments[0]
        counts = jnp.stack([jnp.sum((seg_own <= number).astype(jnp.int32)) for number in range(2)])
        counts = lax.psum(counts, "ctx")
        start = jnp.where(seg_own == 0, 0, jnp.where(seg_own == 1, counts[0], counts[1]))
        order = untangle(received).reshape(ctx_size * tokens, 2 * width_k)
        attended, log_total = attend(query_rot, order, start, query_index, key_heads)
        attended_low = attended.astype(jnp.bfloat16)
    attended_low, grad_top_mine = lax.optimization_barrier(
        (attended_low, gather_half(after(grad_top, *received)))
    )
    branch_part = dot_rows(attended_low, full_o_turned).astype(jnp.bfloat16)
    middle = inputs + (
        branch_part.astype(jnp.float32) + swap_cores(branch_part).astype(jnp.float32)
    )
    scale_two = lax.rsqrt(jnp.mean(middle * middle, -1, keepdims=True) + EPS)
    unit_two = middle * scale_two
    normed_two = (unit_two * mlp_gain).astype(jnp.bfloat16)

    normed_mine = gather_half(normed_two)
    halves = [normed_mine, swap_cores(normed_mine)]
    tops = [grad_top_mine, swap_cores(grad_top_mine)]
    fsdp_own = lax.axis_index("fsdp").astype(jnp.int32)[None]

    gate_up, down_turned = mlp_rows[:, : 2 * chunk], mlp_rows[:, 2 * chunk :]
    normed_all, grad_top_all = jnp.concatenate(halves), jnp.concatenate(tops)
    if few():
        grad_one, grad_two, hidden, grad_both = mlp(halves, tops, mlp_rows, chunk)
    else:
        gate_upward = dot(normed_all, gate_up)
        grad_hidden = dot(grad_top_all, down_turned)
        gate_values, upward = gate_upward[:, :chunk], gate_upward[:, chunk:]
        sigmoid_gate = jax.nn.sigmoid(gate_values)
        swish_gate = gate_values * sigmoid_gate
        hidden = (swish_gate * upward).astype(jnp.bfloat16)
        slope = sigmoid_gate + swish_gate * (1.0 - sigmoid_gate)
        grad_both = jnp.concatenate(
            [grad_hidden * upward * slope, grad_hidden * swish_gate], axis=-1
        ).astype(jnp.bfloat16)
        grad_one, grad_two = jnp.split(dot_rows(grad_both, gate_up).astype(jnp.bfloat16), 2)
    grad_normed_sum = add_cores(grad_one, grad_two)
    grad_normed_parts = trade(jnp.split(grad_normed_sum, ctx_size))
    grad_both, grad_normed_sum = lax.optimization_barrier((grad_both, grad_normed_sum))
    mlp_grad = jnp.concatenate(
        [
            turned_dot(normed_all, grad_both).astype(jnp.bfloat16),
            turned_dot(grad_top_all, hidden).astype(jnp.bfloat16),
        ],
        axis=-1,
    ).reshape(fsdp_size, ctx_size * rows, 3 * chunk)
    mlp_mine = lax.psum_scatter(mlp_grad, "fsdp", scatter_dimension=0, tiled=False)
    branch_two_sum = add_cores(
        *jnp.split(dot_rows(after(hidden, grad_normed_sum), down_turned).astype(jnp.bfloat16), 2)
    )
    branch_two_sum, *grad_normed_parts = lax.optimization_barrier(
        (branch_two_sum, *grad_normed_parts)
    )
    grad_normed_two = join_tokens(grad_normed_parts)
    branch_two_parts = trade(jnp.split(branch_two_sum, ctx_size))

    grad_mlp_gain = jnp.sum(grad_normed_two * unit_two, 0)
    grad_unit_two = grad_normed_two * mlp_gain
    grad_middle = grad_top.astype(jnp.float32) + scale_two * (
        grad_unit_two - unit_two * jnp.mean(grad_unit_two * unit_two, -1, keepdims=True)
    )
    grad_branch = grad_middle.astype(jnp.bfloat16)
    def owners(left, right):
        if few():
            return weight_grad(own, left, right, ctx_size, fsdp_size)
        grad = turned_dot(left, right).astype(jnp.bfloat16)
        cut = grad.reshape(fsdp_size, ctx_size, rows, right.shape[1]).transpose(1, 0, 2, 3)
        return list(cut.reshape(ctx_size, fsdp_size * rows, right.shape[1]))

    o_parts = trade(owners(grad_branch, attended_low))
    if small_heads:
        grad_query, grad_keyvals = attend_bwd(
            own,
            query_flat,
            start,
            attended_turned,
            log_total,
            grad_branch,
            full_o_turned,
            cos_turned,
            sin_turned,
            received,
        )
    else:
        grad_attended = dot(grad_branch, full_o_turned).astype(jnp.bfloat16)
        grad_query_rot, grad_keyvals = attend_back(
            query_rot,
            order,
            start,
            query_index,
            key_heads,
            log_total,
            attended,
            grad_attended,
        )
        grad_keyvals = choose(grad_keyvals.reshape(ctx_size, tokens, 2 * width_k))
    grad_keyvals[0], branch_two_parts = lax.optimization_barrier(
        (grad_keyvals[0], branch_two_parts)
    )
    grad_keyvals[0], o_parts[1] = lax.optimization_barrier((grad_keyvals[0], o_parts[1]))
    keyval_parts = trade(grad_keyvals)
    keyval_parts[0], o_parts = lax.optimization_barrier((keyval_parts[0], o_parts))
    branch_two = join_tokens(branch_two_parts)
    result = (middle + branch_two).astype(jnp.bfloat16)

    if small_heads:
        grad_qkv, grad_normed_part = key_grads(
            grad_query, full_qkv, cos_turned, sin_turned, keyval_parts
        )
    else:
        grad_keyval = sum(part.astype(F32) for part in keyval_parts)
        grad_query = (
            rotate(grad_query_rot, cosines, -sines)
            .reshape(tokens, head_count * HEAD_DIM)
            .astype(jnp.bfloat16)
        )
        grad_key = (
            rotate(
                grad_keyval[:, : key_heads * HEAD_DIM].reshape(tokens, key_heads, HEAD_DIM),
                cosines,
                -sines,
            )
            .reshape(tokens, key_heads * HEAD_DIM)
            .astype(jnp.bfloat16)
        )
        grad_value = grad_keyval[:, key_heads * HEAD_DIM :].astype(jnp.bfloat16)
        grad_qkv = jnp.concatenate([grad_query, grad_key, grad_value], axis=-1)
        grad_normed_part = dot_rows(grad_qkv, full_qkv).astype(jnp.bfloat16)
    grad_normed_other = swap_cores(grad_normed_part)
    if few():
        grad_inputs, qkv_pieces = last_grads(
            own,
            layer_input[0],
            attn_gain[None],
            grad_qkv,
            grad_normed_part,
            grad_normed_other,
            grad_middle,
            grad_mlp_gain[None],
            ctx_size,
            fsdp_size,
        )
    else:
        grad_normed = grad_normed_part.astype(F32) + grad_normed_other.astype(F32)
        turned = grad_normed * unit_one
        along = jnp.mean(turned * attn_gain, -1, keepdims=True)
        grad_inputs = grad_middle + scale_one * (grad_normed * attn_gain - unit_one * along)
        grad_inputs = grad_inputs.astype(jnp.bfloat16)
        lines = [jnp.sum(grad_qkv.astype(F32), 0)]
        for gains in (jnp.sum(turned, 0), grad_mlp_gain):
            for half in (gains[:SPLIT], gains[SPLIT:]):
                lines.append(jnp.pad(half, (0, width_qkv - half.shape[0])))
        small = jnp.pad(jnp.stack(lines), ((0, SMALL_ROWS - len(lines)), (0, 0)))
        small = small.astype(jnp.bfloat16)
        qkv_pieces = [jnp.concatenate([part, small]) for part in owners(normed, grad_qkv)]
    qkv_parts = trade(qkv_pieces)
    if few():
        packed = pack(fsdp_own, qkv_parts, o_parts, fsdp_size)
    else:
        qkv_sum = sum(part.astype(F32) for part in qkv_parts)
        o_sum = sum(part.astype(F32) for part in o_parts)
        small = jnp.pad(qkv_sum[fsdp_size * rows :], ((0, 0), (0, w_o.shape[0])))
        both = jnp.concatenate([qkv_sum[: fsdp_size * rows], o_sum], axis=-1)
        both = both.reshape(fsdp_size, rows, both.shape[-1])
        packed = [
            jnp.concatenate([both[(fsdp_own[0] + step) % fsdp_size], small]).astype(jnp.bfloat16)
            for step in range(fsdp_size)
        ]
    mlp_mine = mlp_mine.reshape(ctx_size, rows, 3 * chunk)
    packed = packed[:1] + [send_up(packed[step], step) for step in range(1, fsdp_size)]
    mlp_pieces = trade(choose(mlp_mine))
    if few():
        w_grads = unpack(packed, features, width_q, width_k)
        mlp_grads = mlp_out(own, mlp_pieces, hidden_count)
    else:
        total = sum(part.astype(F32) for part in packed)
        tops = [0, width_q, width_q + width_k, width_qkv]
        w_grads = [total[:rows, tops[k] : tops[k + 1]] for k in range(3)]
        w_grads.append(total[:rows, width_qkv:])
        w_grads += [total[rows, tops[k] : tops[k + 1]] for k in range(3)]
        for row in (rows + 1, rows + 3):
            w_grads.append(
                jnp.concatenate([total[row, :SPLIT], total[row + 1, : features - SPLIT]])
            )
        mlp_grads = []
        for number in range(3):
            pieces = untangle(mlp_pieces)[..., number * chunk : (number + 1) * chunk]
            wide = pieces.transpose(1, 0, 2).reshape(rows, chunk * ctx_size)
            mlp_grads.append(wide[:, :hidden_count].astype(F32))
    grad_q, grad_k, grad_v, grad_o = w_grads[:4]
    grad_b_q, grad_b_k, grad_b_v, grad_attn_gain, grad_mlp_gain = [
        values.reshape(-1) for values in w_grads[4:]
    ]
    return (
        result[None],
        grad_inputs[None],
        grad_attn_gain,
        grad_q,
        grad_b_q,
        grad_k,
        grad_b_k,
        grad_v,
        grad_b_v,
        grad_o.T,
        grad_mlp_gain,
        mlp_grads[0],
        mlp_grads[1],
        mlp_grads[2].T,
    )


def solution(mesh):
    placed = (
        P("fsdp", "ctx", None),
        P("fsdp", "ctx"),
        P("fsdp", "ctx"),
        P(),
        P(("fsdp", "ctx"), "tp"),
        P("tp"),
        P(("fsdp", "ctx"), "tp"),
        P("tp"),
        P(("fsdp", "ctx"), "tp"),
        P("tp"),
        P("tp", ("fsdp", "ctx")),
        P(),
        P(("fsdp", "ctx"), "tp"),
        P(("fsdp", "ctx"), "tp"),
        P("tp", ("fsdp", "ctx")),
        P("fsdp", "ctx", None),
    )
    return jax.shard_map(
        body,
        mesh=mesh,
        in_specs=placed,
        out_specs=(
            P("fsdp", "ctx", None),
            P("fsdp", "ctx", None),
            P(),
            P(("fsdp", "ctx"), "tp"),
            P("tp"),
            P(("fsdp", "ctx"), "tp"),
            P("tp"),
            P(("fsdp", "ctx"), "tp"),
            P("tp"),
            P("tp", ("fsdp", "ctx")),
            P(),
            P(("fsdp", "ctx"), "tp"),
            P(("fsdp", "ctx"), "tp"),
            P("tp", ("fsdp", "ctx")),
        ),
        check_vma=False,
    )
```

```python
import functools
import math

import jax
import jax.numpy as jnp
from jax import lax
from jax.experimental import pallas as pl
from jax.experimental.pallas import tpu as pltpu
from jax.sharding import PartitionSpec as P

HEAD_DIM = 64


EPS = 1e-06
THETA = 1000000.0
NEG = -1e30

LANES = 128
SPLIT = 512
SMALL_ROWS = 16
BLOCK = 512
MLP_VMEM = 32 * 2**20
VMEM_BYTES = 16 * 2**20
FREE = pl.CostEstimate(flops=0, bytes_accessed=0, transcendentals=0)
IN_VMEM = pl.BlockSpec(memory_space=pltpu.VMEM)
IN_SMEM = pl.BlockSpec(memory_space=pltpu.SMEM)
F32 = jnp.float32
BF = jnp.bfloat16


def dot(left, right):
    return jnp.dot(left, right, preferred_element_type=F32)


def dot_rows(left, right):
    return lax.dot_general(left, right, (((1,), (1,)), ((), ())), preferred_element_type=F32)


def turned_dot(left, right):
    return lax.dot_general(left, right, (((0,), (0,)), ((), ())), preferred_element_type=F32)


def rotate(values, cosines, sines):
    halfway = values.shape[-1] // 2
    turned = jnp.concatenate([-values[..., halfway:], values[..., :halfway]], axis=-1)
    return values * cosines + turned * sines


def angles(positions, head_dim):
    even_steps = jnp.arange(0, head_dim, 2).astype(jnp.float32)
    inverse = jnp.exp(-math.log(THETA) * even_steps / head_dim)
    phases = positions.astype(jnp.float32)[..., None] * inverse
    phases = jnp.concatenate([phases, phases], axis=-1)
    return (jnp.cos(phases)[..., None, :], jnp.sin(phases)[..., None, :])


def flips(size, step):
    return [(index, index ^ step) for index in range(size)]


def swap_cores(values):
    return lax.ppermute(values, "tp", flips(lax.axis_size("tp"), 1))


def few():
    return lax.axis_size("ctx") <= 8


def peers():
    size = lax.axis_size("ctx")
    if few():
        return [lax.axis_index("ctx") ^ step for step in range(size)]
    return list(range(size))


def spread(values):
    size = lax.axis_size("ctx")
    if not few():
        return list(lax.all_gather(values, "ctx"))
    return [values] + [lax.ppermute(values, "ctx", flips(size, step)) for step in range(1, size)]


def trade(parts):
    size = lax.axis_size("ctx")
    if not few():
        return list(lax.all_to_all(jnp.stack(parts), "ctx", 0, 0))
    return [parts[0]] + [
        lax.ppermute(parts[step], "ctx", flips(size, step)) for step in range(1, size)
    ]


def untangle(parts):
    if not few():
        return jnp.stack(parts)
    own = lax.axis_index("ctx")
    whole = jnp.stack(parts)
    return jnp.stack(
        [lax.dynamic_index_in_dim(whole, own ^ place, 0, keepdims=False) for place in range(len(parts))]
    )


def choose(whole):
    if not few():
        return list(whole)
    return [lax.dynamic_index_in_dim(whole, peer, 0, keepdims=False) for peer in peers()]


def after(values, *earlier):
    return lax.optimization_barrier((values,) + earlier)[0]


def direct_gather(values):
    size = lax.axis_size("fsdp")
    own = lax.axis_index("fsdp")
    pieces = [values] + [
        lax.ppermute(values, "fsdp", [(index, (index + step) % size) for index in range(size)])
        for step in range(1, size)
    ]
    pieces = pieces[::-1]
    line = jnp.stack(pieces + pieces[:-1])
    return lax.dynamic_slice_in_dim(line, size - 1 - own, size, 0)


def send_up(values, step):
    size = lax.axis_size("fsdp")
    return lax.ppermute(values, "fsdp", [(index, (index + step) % size) for index in range(size)])


def line_steps():
    size = lax.axis_size("fsdp")
    ups = [(index, index + 1) for index in range(size - 1)]
    downs = [(index + 1, index) for index in range(size - 1)]
    return ups, downs


def gather_step(line, step):
    ups, downs = line_steps()
    return (
        [lax.ppermute(line[0], "fsdp", ups[step:])]
        + line
        + [lax.ppermute(line[-1], "fsdp", downs[: len(downs) - step])]
    )


def gather_end(line):
    size = lax.axis_size("fsdp")
    return lax.dynamic_slice_in_dim(
        jnp.stack(line), size - 1 - lax.axis_index("fsdp"), size, 0
    )


def scatter_step(whole, sums, step):
    size = lax.axis_size("fsdp")
    own = lax.axis_index("fsdp")
    ups, downs = line_steps()
    pieces = [
        lax.dynamic_index_in_dim(whole, place, 0, keepdims=False)
        for place in (own + size - step, own - size + step)
    ]
    if sums:
        pieces = [piece + part for piece, part in zip(pieces, sums)]
    return [
        lax.ppermute(pieces[0], "fsdp", ups[:step]),
        lax.ppermute(pieces[1], "fsdp", downs[size - 1 - step :]),
    ]


def scatter_end(whole, sums):
    own = lax.dynamic_index_in_dim(whole, lax.axis_index("fsdp"), 0, keepdims=False)
    return sum(part.astype(F32) for part in [own] + sums)


def gather_half(values):
    half = values.shape[0] // 2
    return jnp.concatenate(
        spread(lax.dynamic_slice_in_dim(values, lax.axis_index("tp") * half, half, 0))
    )


def add_cores(mine, other):
    return (mine.astype(jnp.float32) + swap_cores(other).astype(jnp.float32)).astype(jnp.bfloat16)


def join_tokens(parts):
    own = sum(part.astype(jnp.float32) for part in parts).astype(jnp.bfloat16)
    other = swap_cores(own)
    first = lax.axis_index("tp") == 0
    return jnp.where(
        first, jnp.concatenate([own, other]), jnp.concatenate([other, own])
    ).astype(jnp.float32)


def turn_back(values, cosines, sines, sign):
    half = cosines.shape[0]
    parts = []
    for begin in range(0, values.shape[0], 2 * half):
        first = values[begin : begin + half]
        second = values[begin + half : begin + 2 * half]
        parts += [first * cosines - second * (sign * sines), second * cosines + first * (sign * sines)]
    return jnp.concatenate(parts)


def project_kernel(
    width_q, width_k, input_ref, gain_ref, w_ref, b_ref, cos_ref, sin_ref, seg_ref, q_ref, kv_ref
):
    inputs = input_ref[...].astype(F32)
    scale = lax.rsqrt(jnp.mean(inputs * inputs, -1, keepdims=True) + EPS)
    normed = (inputs * scale * gain_ref[...]).astype(BF)
    projected = dot(normed, w_ref[...]) + b_ref[...]
    rotated = turn_back(projected[:, : width_q + width_k].T, cos_ref[...], sin_ref[...], 1.0).T
    q_ref[...] = rotated[:, :width_q].astype(BF)
    tokens = q_ref.shape[0]
    kv_ref[:tokens, :width_k] = rotated[:, width_q:].astype(BF)
    kv_ref[:tokens, width_k:] = projected[:, width_q + width_k :].astype(BF)
    number = lax.broadcasted_iota(jnp.int32, (SMALL_ROWS, kv_ref.shape[1]), 0)
    counts = jnp.zeros(number.shape, F32)
    for row in range(2):
        below = jnp.sum((seg_ref[...] <= row).astype(F32), -1, keepdims=True)
        counts = jnp.where(number == row, below, counts)
    kv_ref[tokens:, :] = counts.astype(BF)


def project(inputs, gain, weights, biases, cosines, sines, segments, width_q, width_k):
    tokens = inputs.shape[0]
    return pl.pallas_call(
        functools.partial(project_kernel, width_q, width_k),
        out_shape=(
            jax.ShapeDtypeStruct((tokens, width_q), BF),
            jax.ShapeDtypeStruct((tokens + SMALL_ROWS, 2 * width_k), BF),
        ),
        in_specs=[IN_VMEM] * 7,
        out_specs=(IN_VMEM,) * 2,
        compiler_params=pltpu.CompilerParams(vmem_limit_bytes=VMEM_BYTES),
        cost_estimate=FREE,
        name="project",
    )(inputs, gain, weights, biases, cosines, sines, segments)


def key_grads_kernel(count, q_ref, w_ref, cos_ref, sin_ref, *refs):
    parts, qkv_ref, normed_ref = refs[:count], refs[count], refs[count + 1]
    width_q = q_ref.shape[1]
    total = sum(ref[...].astype(F32) for ref in parts)
    width_k = total.shape[1] // 2
    keys = turn_back(total[:, :width_k].T, cos_ref[...], sin_ref[...], -1.0).T
    qkv_ref[:, :width_q] = q_ref[...]
    qkv_ref[:, width_q : width_q + width_k] = keys.astype(BF)
    qkv_ref[:, width_q + width_k :] = total[:, width_k:].astype(BF)
    normed_ref[...] = dot_rows(qkv_ref[...], w_ref[...]).astype(BF)


def key_grads(grad_query, weights, cosines, sines, parts):
    tokens = grad_query.shape[0]
    features, width = weights.shape
    return pl.pallas_call(
        functools.partial(key_grads_kernel, len(parts)),
        out_shape=(
            jax.ShapeDtypeStruct((tokens, width), BF),
            jax.ShapeDtypeStruct((tokens, features), BF),
        ),
        in_specs=[IN_VMEM] * (4 + len(parts)),
        out_specs=(IN_VMEM,) * 2,
        compiler_params=pltpu.CompilerParams(vmem_limit_bytes=VMEM_BYTES),
        cost_estimate=FREE,
        name="key_grads",
    )(grad_query, weights, cosines, sines, *parts)


def masks(start, tokens, own, step):
    peer = own ^ step
    key = peer*tokens + lax.broadcasted_iota(jnp.int32,(tokens,tokens),0)
    query = own*tokens + lax.broadcasted_iota(jnp.int32,(tokens,tokens),1)
    return jnp.where((key>=start)&(key<=query),0.0,NEG).astype(F32)

def fwd_kernel(count, own_ref, q_ref, seg_ref, *refs):
    kv_refs=refs[:count]; att_ref, att_t_ref, lse_ref, start_ref, bias, s_ref = refs[count:]
    own=own_ref[0]
    tokens=q_ref.shape[0]; heads=q_ref.shape[1]//HEAD_DIM
    counts=sum(r[tokens:,:].astype(F32) for r in kv_refs).astype(jnp.int32)
    seg=seg_ref[...]
    start=jnp.where(seg==0,0,jnp.where(seg==1,counts[0:1,0:1],counts[1:2,0:1]))
    start_ref[...]=start
    for step in range(count):
        bias[step*tokens:(step+1)*tokens,:]=masks(start,tokens,own,step)
    q=q_ref[...]*jnp.asarray(HEAD_DIM**-0.5,BF)
    ks=[r[:tokens,:HEAD_DIM] for r in kv_refs]
    vts=[r[:tokens,HEAD_DIM:].astype(F32).T.astype(BF) for r in kv_refs]
    for h in range(heads):
        qh=q[:,h*HEAD_DIM:(h+1)*HEAD_DIM]
        peak=jnp.full((1,tokens),NEG,F32)
        for step in range(count):
            rows=slice(step*tokens,(step+1)*tokens)
            s=dot_rows(ks[step],qh)+bias[rows,:]
            s_ref[h%2,rows,:]=s
            peak=jnp.maximum(peak,jnp.max(s,0,keepdims=True))
        total=jnp.zeros((1,tokens),F32)
        out=jnp.zeros((HEAD_DIM,tokens),F32)
        for step in range(count):
            rows=slice(step*tokens,(step+1)*tokens)
            p=jnp.exp(s_ref[h%2,rows,:]-peak)
            total=total+jnp.sum(p,0,keepdims=True)
            out=out+dot(vts[step],p.astype(BF))
        att_t_ref[h*HEAD_DIM:(h+1)*HEAD_DIM,:]=out/total
        lse_ref[h:h+1,:]=peak+jnp.log(total)
    att_ref[...]=att_t_ref[...].T.astype(BF)

def attend_fwd(own, q, segments, kvs):
    tokens,width=q.shape; heads=width//HEAD_DIM; n=len(kvs)
    return pl.pallas_call(functools.partial(fwd_kernel,n),
        out_shape=(jax.ShapeDtypeStruct((tokens,width),BF),jax.ShapeDtypeStruct((width,tokens),F32),jax.ShapeDtypeStruct((heads,tokens),F32),jax.ShapeDtypeStruct((1,tokens),jnp.int32)),
        in_specs=[IN_SMEM]+[IN_VMEM]*(2+n), out_specs=(IN_VMEM,)*4,
        scratch_shapes=[pltpu.VMEM((n*tokens,tokens),F32),pltpu.VMEM((2,n*tokens,tokens),F32)],
        compiler_params=pltpu.CompilerParams(vmem_limit_bytes=VMEM_BYTES),
        cost_estimate=FREE, name="attend_forward")(own,q,segments,*kvs)

def bwd_kernel(
    count, own_ref, q_ref, start_ref, att_t_ref, lse_ref, gb_ref, wo_ref, cos_ref, sin_ref, *refs
):
    kv_refs=refs[:count]; gq_ref=refs[count]; gkv_refs=refs[count+1:2*count+1]; bias, gqt, dkv = refs[2*count+1:]
    own=own_ref[0]
    tokens=q_ref.shape[0]; heads=q_ref.shape[1]//HEAD_DIM
    start=start_ref[...]
    do=dot(gb_ref[...],wo_ref[...])
    do_low=do.astype(BF)
    do_t=do_low.astype(F32).T
    prod=do_t*att_t_ref[...]
    q=q_ref[...]
    qs=q*jnp.asarray(HEAD_DIM**-0.5,BF)
    ks=[r[:tokens,:HEAD_DIM] for r in kv_refs]
    vs=[r[:tokens,HEAD_DIM:] for r in kv_refs]
    kts=[k.astype(F32).T.astype(BF) for k in ks]
    dot_low=do_t.astype(BF)
    for step in range(count):
        bias[...]=masks(start,tokens,own,step)
        dk=jnp.zeros((tokens,HEAD_DIM),F32); dv=jnp.zeros((tokens,HEAD_DIM),F32)
        for h in range(heads):
            cols=slice(h*HEAD_DIM,(h+1)*HEAD_DIM)
            qh=qs[:,cols]; doh=do_low[:,cols]
            rowdot=jnp.sum(prod[cols,:],0,keepdims=True)
            p=jnp.exp(dot_rows(ks[step],qh)+(bias[...]-lse_ref[h:h+1,:]))
            dp=dot_rows(vs[step],doh)
            ds=(p*(dp-rowdot)).astype(BF)
            dv=dv+dot(p.astype(BF),doh)
            dk=dk+dot(ds,qh)
            dq=dot(kts[step],ds)
            if step==0: gqt[cols,:]=dq
            else: gqt[cols,:]+=dq
        gkv_refs[step][:,:HEAD_DIM]=dk.astype(BF)
        gkv_refs[step][:,HEAD_DIM:]=dv.astype(BF)
    turned=turn_back(gqt[...]*(HEAD_DIM**-0.5),cos_ref[...],sin_ref[...],-1.0)
    gq_ref[...]=turned.T.astype(BF)

def attend_bwd(own,q,start,att_t,lse,gb,wo,cosines,sines,kvs):
    tokens,width=q.shape; n=len(kvs)
    outs=pl.pallas_call(functools.partial(bwd_kernel,n),
        out_shape=(jax.ShapeDtypeStruct((tokens,width),BF),)+(jax.ShapeDtypeStruct((tokens,2*HEAD_DIM),BF),)*n,
        in_specs=[IN_SMEM]+[IN_VMEM]*(8+n), out_specs=(IN_VMEM,)*(n+1),
        scratch_shapes=[pltpu.VMEM((tokens,tokens),F32),pltpu.VMEM((width,tokens),F32),pltpu.VMEM((8,128),F32)],
        compiler_params=pltpu.CompilerParams(vmem_limit_bytes=VMEM_BYTES),
        cost_estimate=FREE, name="attend_backward")(own,q,start,att_t,lse,gb,wo,cosines,sines,*kvs)
    return outs[0],list(outs[1:])


def prepare_kernel(count, chunk, own_ref, gate_ref, up_ref, down_ref, *refs):
    pieces, wide = refs[:count], refs[count]
    rows, hidden = gate_ref.shape
    span = chunk * count
    for number in range(3):
        wide[number, :, :hidden] = (gate_ref, up_ref, down_ref)[number][...]
        if span > hidden:
            wide[number, :, hidden:] = jnp.zeros((rows, span - hidden), BF)
    for step in range(count):
        begin = pl.multiple_of((own_ref[0] ^ step) * chunk, LANES)
        for number in range(3):
            pieces[step][:, number * chunk : (number + 1) * chunk] = wide[
                number, :, pl.ds(begin, chunk)
            ]


def prepare(own, w_gate, w_up, w_down, count, chunk):
    rows = w_gate.shape[0]
    outs = pl.pallas_call(
        functools.partial(prepare_kernel, count, chunk),
        out_shape=(jax.ShapeDtypeStruct((rows, 3 * chunk), BF),) * count,
        in_specs=[IN_SMEM] + [IN_VMEM] * 3,
        out_specs=(IN_VMEM,) * count,
        scratch_shapes=[pltpu.VMEM((3, rows, chunk * count), BF)],
        compiler_params=pltpu.CompilerParams(vmem_limit_bytes=VMEM_BYTES),
        cost_estimate=FREE,
        name="prepare",
    )(own, w_gate, w_up, w_down)
    return list(outs)


def mlp_kernel(chunk, first_ref, second_ref, top_one_ref, top_two_ref, weights, *refs):
    grad_one_ref, grad_two_ref, hidden_ref, both_ref = refs
    rows = first_ref.shape[0]
    block = min(rows, BLOCK)
    for half, (tokens_ref, top_ref, grad_ref) in enumerate(
        ((first_ref, top_one_ref, grad_one_ref), (second_ref, top_two_ref, grad_two_ref))
    ):
        for begin in range(0, rows, block):
            here = slice(begin, begin + block)
            there = slice(half * rows + begin, half * rows + begin + block)
            gate_up = dot(tokens_ref[here, :], weights[:, : 2 * chunk])
            grad_hidden = dot(top_ref[here, :], weights[:, 2 * chunk :])
            gate, upward = gate_up[:, :chunk], gate_up[:, chunk:]
            sigmoid = jax.nn.sigmoid(gate)
            swish = gate * sigmoid
            hidden_ref[there, :] = (swish * upward).astype(BF)
            slope = sigmoid + swish * (1.0 - sigmoid)
            both_ref[there, :chunk] = (grad_hidden * upward * slope).astype(BF)
            both_ref[there, chunk:] = (grad_hidden * swish).astype(BF)
            grad_ref[here, :] = dot_rows(both_ref[there, :], weights[:, : 2 * chunk]).astype(BF)


def mlp(halves, tops, weights, chunk):
    rows, features = halves[0].shape
    return pl.pallas_call(
        functools.partial(mlp_kernel, chunk),
        out_shape=(jax.ShapeDtypeStruct((rows, features), BF),) * 2
        + (
            jax.ShapeDtypeStruct((2 * rows, chunk), BF),
            jax.ShapeDtypeStruct((2 * rows, 2 * chunk), BF),
        ),
        in_specs=[IN_VMEM] * 5,
        out_specs=(IN_VMEM,) * 4,
        compiler_params=pltpu.CompilerParams(vmem_limit_bytes=MLP_VMEM),
        cost_estimate=FREE,
        name="mlp",
    )(*halves, *tops, weights)


def weight_grad_kernel(count, lines, own_ref, left_ref, right_ref, *refs):
    pieces, whole = refs[:count], refs[count]
    whole[...] = turned_dot(left_ref[...], right_ref[...])
    rows = whole.shape[0] // (count * lines)
    for step in range(count):
        peer = own_ref[0] ^ step
        parts = []
        for line in range(lines):
            begin = pl.multiple_of((line * count + peer) * rows, 8)
            parts.append(whole[pl.ds(begin, rows), :])
        pieces[step][...] = jnp.concatenate(parts).astype(BF)


def weight_grad(own, left, right, count, lines):
    height, width = left.shape[1], right.shape[1]
    return list(
        pl.pallas_call(
            functools.partial(weight_grad_kernel, count, lines),
            out_shape=(jax.ShapeDtypeStruct((height // count, width), BF),) * count,
            in_specs=[IN_SMEM] + [IN_VMEM] * 2,
            out_specs=(IN_VMEM,) * count,
            scratch_shapes=[pltpu.VMEM((height, width), F32)],
            compiler_params=pltpu.CompilerParams(vmem_limit_bytes=VMEM_BYTES),
            cost_estimate=FREE,
            name="weight_grad",
        )(own, left, right)
    )


def last_grads_kernel(
    count, lines, own_ref, input_ref, gain_ref, qkv_ref, first_ref, second_ref, middle_ref,
    mlp_ref, out_ref, *refs
):
    pieces, whole, small = refs[:count], refs[count], refs[count + 1]
    features = input_ref.shape[1]
    inputs = input_ref[...].astype(F32)
    scale = lax.rsqrt(jnp.mean(inputs * inputs, -1, keepdims=True) + EPS)
    unit = inputs * scale
    gain = gain_ref[...]
    qkv = qkv_ref[...]
    whole[...] = turned_dot((unit * gain).astype(BF), qkv)
    grad = first_ref[...].astype(F32) + second_ref[...].astype(F32)
    turned = grad * unit
    small[...] = jnp.zeros_like(small)
    small[0:1, :] = jnp.sum(qkv.astype(F32), 0, keepdims=True)
    for row, values in ((1, jnp.sum(turned, 0, keepdims=True)), (3, mlp_ref[...])):
        small[row : row + 1, :SPLIT] = values[:, :SPLIT]
        small[row + 1 : row + 2, : features - SPLIT] = values[:, SPLIT:]
    along = jnp.mean(turned * gain, -1, keepdims=True)
    out_ref[...] = (middle_ref[...] + scale * (grad * gain - unit * along)).astype(BF)
    rows = features // (count * lines)
    for step in range(count):
        peer = own_ref[0] ^ step
        parts = []
        for line in range(lines):
            begin = pl.multiple_of((line * count + peer) * rows, 8)
            parts.append(whole[pl.ds(begin, rows), :])
        pieces[step][...] = jnp.concatenate(parts + [small[...]]).astype(BF)


def last_grads(own, inputs, gain, qkv, first, second, middle, mlp_gain_grad, count, lines):
    tokens, features = inputs.shape
    width = qkv.shape[1]
    outs = pl.pallas_call(
        functools.partial(last_grads_kernel, count, lines),
        out_shape=(jax.ShapeDtypeStruct((tokens, features), BF),)
        + (jax.ShapeDtypeStruct((features // count + SMALL_ROWS, width), BF),) * count,
        in_specs=[IN_SMEM] + [IN_VMEM] * 7,
        out_specs=(IN_VMEM,) * (count + 1),
        scratch_shapes=[pltpu.VMEM((features, width), F32), pltpu.VMEM((SMALL_ROWS, width), F32)],
        compiler_params=pltpu.CompilerParams(vmem_limit_bytes=VMEM_BYTES),
        cost_estimate=FREE,
        name="last_grads",
    )(own, inputs, gain, qkv, first, second, middle, mlp_gain_grad)
    return outs[0], list(outs[1:])


def pack_kernel(count, lines, own_ref, *refs):
    qkv_refs, outs = refs[:count], refs[count : count + lines]
    qkv_sum, block = refs[count + lines :]
    qkv_sum[...] = sum(ref[...].astype(F32) for ref in qkv_refs)
    rows = block.shape[0] - SMALL_ROWS
    block[rows:, :] = qkv_sum[lines * rows :, :]
    for step in range(lines):
        begin = pl.multiple_of(lax.rem(own_ref[0] + step, lines) * rows, 8)
        block[:rows, :] = qkv_sum[pl.ds(begin, rows), :]
        outs[step][...] = block[...].astype(BF)


def pack(own_line, qkv_parts, lines):
    height, width = qkv_parts[0].shape
    shape = ((height - SMALL_ROWS) // lines + SMALL_ROWS, width)
    return list(
        pl.pallas_call(
            functools.partial(pack_kernel, len(qkv_parts), lines),
            out_shape=(jax.ShapeDtypeStruct(shape, BF),) * lines,
            in_specs=[IN_SMEM] + [IN_VMEM] * len(qkv_parts),
            out_specs=(IN_VMEM,) * lines,
            scratch_shapes=[pltpu.VMEM((height, width), F32), pltpu.VMEM(shape, F32)],
            compiler_params=pltpu.CompilerParams(vmem_limit_bytes=VMEM_BYTES),
            cost_estimate=FREE,
            name="pack",
        )(own_line, *qkv_parts)
    )


def unpack_kernel(lines, widths, *refs):
    parts, o_parts = refs[:lines], refs[lines : 2 * lines]
    q_ref, k_ref, v_ref, o_ref, bq_ref, bk_ref, bv_ref, attn_ref, mlp_ref, total = refs[2 * lines :]
    total[...] = sum(ref[...].astype(F32) for ref in parts)
    rows = q_ref.shape[0]
    first, second = widths[0], widths[0] + widths[1]
    third = second + widths[1]
    q_ref[...] = total[:rows, :first]
    k_ref[...] = total[:rows, first:second]
    v_ref[...] = total[:rows, second:third]
    o_ref[...] = sum(ref[...].astype(F32) for ref in o_parts)
    bq_ref[...] = total[rows : rows + 1, :first]
    bk_ref[...] = total[rows : rows + 1, first:second]
    bv_ref[...] = total[rows : rows + 1, second:third]
    for row, ref in ((rows + 1, attn_ref), (rows + 3, mlp_ref)):
        ref[:, :SPLIT] = total[row : row + 1, :SPLIT]
        ref[:, SPLIT:] = total[row + 1 : row + 2, : ref.shape[1] - SPLIT]


def unpack(parts, o_parts, features, width_q, width_k):
    rows, width = parts[0].shape
    rows -= SMALL_ROWS
    width_o = o_parts[0].shape[1]
    shapes = [
        (rows, width_q), (rows, width_k), (rows, width_k), (rows, width_o),
        (1, width_q), (1, width_k), (1, width_k), (1, features), (1, features),
    ]
    return pl.pallas_call(
        functools.partial(unpack_kernel, len(parts), (width_q, width_k)),
        out_shape=tuple(jax.ShapeDtypeStruct(shape, F32) for shape in shapes),
        in_specs=[IN_VMEM] * (2 * len(parts)),
        out_specs=(IN_VMEM,) * len(shapes),
        scratch_shapes=[pltpu.VMEM(parts[0].shape, F32)],
        compiler_params=pltpu.CompilerParams(vmem_limit_bytes=VMEM_BYTES),
        cost_estimate=FREE,
        name="unpack",
    )(*parts, *o_parts)


def mlp_out_kernel(count, chunk, own_ref, *refs):
    parts = refs[:count]
    gate_ref, up_ref, down_ref, wide = refs[count:]
    rows, hidden = gate_ref.shape
    for step in range(count):
        begin = pl.multiple_of((own_ref[0] ^ step) * chunk, LANES)
        for number in range(3):
            wide[number, :, pl.ds(begin, chunk)] = parts[step][
                :, number * chunk : (number + 1) * chunk
            ].astype(F32)
    for number, ref in enumerate((gate_ref, up_ref, down_ref)):
        ref[...] = wide[number, :, :hidden]


def mlp_out(own, parts, hidden):
    count = len(parts)
    rows, width = parts[0].shape
    chunk = width // 3
    return pl.pallas_call(
        functools.partial(mlp_out_kernel, count, chunk),
        out_shape=(jax.ShapeDtypeStruct((rows, hidden), F32),) * 3,
        in_specs=[IN_SMEM] + [IN_VMEM] * count,
        out_specs=(IN_VMEM,) * 3,
        scratch_shapes=[pltpu.VMEM((3, rows, chunk * count), F32)],
        compiler_params=pltpu.CompilerParams(vmem_limit_bytes=VMEM_BYTES),
        cost_estimate=FREE,
        name="mlp_out",
    )(own, *parts)


def score_block(query_groups, key_rows, key_index, start, query_index):
    head_dim = query_groups.shape[-1]
    logits = jnp.einsum(
        "qgjd,kgd->gjqk", query_groups, key_rows, preferred_element_type=jnp.float32
    ) * head_dim ** (-0.5)
    allowed = (key_index[None, :] >= start[:, None]) & (key_index[None, :] <= query_index[:, None])
    return jnp.where(allowed, logits, NEG)


def key_window(keyval_all, number, key_block, key_heads):
    window = lax.dynamic_slice_in_dim(keyval_all, number * key_block, key_block, 0)
    width = window.shape[1] // 2
    key_rows = window[:, :width].reshape(key_block, key_heads, width // key_heads)
    value_rows = window[:, width:].reshape(key_block, key_heads, width // key_heads)
    key_index = number * key_block + jnp.arange(key_block, dtype=jnp.int32)
    return key_rows, value_rows, key_index


def repeat(count, step, state):
    if count == 1:
        return step(0, state)
    return lax.fori_loop(0, count, step, state)


def attend(query_rot, keyval_all, start, query_index, key_heads):
    tokens, head_count, head_dim = query_rot.shape
    group_size = head_count // key_heads
    key_block = min(keyval_all.shape[0], 1024)
    query_groups = query_rot.reshape(tokens, key_heads, group_size, head_dim)
    block_count = keyval_all.shape[0] // key_block

    def measure(number, state_pair):
        running_peak, running_total = state_pair
        key_rows, value_rows, key_index = key_window(
            keyval_all, number, key_block, key_heads
        )
        masked = score_block(query_groups, key_rows, key_index, start, query_index)
        fresh = jnp.maximum(running_peak, jnp.max(masked, -1))
        running_total = running_total * jnp.exp(running_peak - fresh) + jnp.sum(
            jnp.exp(masked - fresh[..., None]), -1
        )
        return (fresh, running_total)

    start_state = (
        jnp.full((key_heads, group_size, tokens), NEG, jnp.float32),
        jnp.zeros((key_heads, group_size, tokens), jnp.float32),
    )
    running_peak, running_total = repeat(block_count, measure, start_state)
    log_total = running_peak + jnp.log(running_total)

    def collect(number, summed):
        key_rows, value_rows, key_index = key_window(
            keyval_all, number, key_block, key_heads
        )
        masked = score_block(query_groups, key_rows, key_index, start, query_index)
        chances = jnp.exp(masked - log_total[..., None]).astype(jnp.bfloat16)
        return summed + jnp.einsum(
            "gjqk,kgd->gjqd", chances, value_rows, preferred_element_type=jnp.float32
        )

    summed = repeat(
        block_count, collect, jnp.zeros((key_heads, group_size, tokens, head_dim), jnp.float32)
    )
    return (summed.transpose(2, 0, 1, 3).reshape(tokens, head_count * head_dim), log_total)


def attend_back(
    query_rot,
    keyval_all,
    start,
    query_index,
    key_heads,
    log_total,
    attended,
    grad_attended,
):
    tokens, head_count, head_dim = query_rot.shape
    group_size = head_count // key_heads
    key_block = min(keyval_all.shape[0], 1024)
    query_groups = query_rot.reshape(tokens, key_heads, group_size, head_dim)
    grad_groups = grad_attended.reshape(tokens, key_heads, group_size, head_dim)
    block_count = keyval_all.shape[0] // key_block
    row_dot = jnp.sum(
        (grad_attended.astype(jnp.float32) * attended).reshape(
            tokens, key_heads, group_size, head_dim
        ),
        -1,
    ).transpose(1, 2, 0)
    score_scale = head_dim ** (-0.5)

    def step_back(number, state_pair):
        grad_query, grad_keyval = state_pair
        key_rows, value_rows, key_index = key_window(
            keyval_all, number, key_block, key_heads
        )
        masked = score_block(query_groups, key_rows, key_index, start, query_index)
        chances = jnp.exp(masked - log_total[..., None])
        chances_low = chances.astype(jnp.bfloat16)
        grad_chances = jnp.einsum(
            "qgjd,kgd->gjqk", grad_groups, value_rows, preferred_element_type=jnp.float32
        )
        grad_logits = (chances * (grad_chances - row_dot[..., None])).astype(jnp.bfloat16)
        grad_query = (
            grad_query
            + jnp.einsum(
                "gjqk,kgd->gjqd", grad_logits, key_rows, preferred_element_type=jnp.float32
            )
            * score_scale
        )
        grad_keys = (
            jnp.einsum(
                "gjqk,qgjd->kgd", grad_logits, query_groups, preferred_element_type=jnp.float32
            )
            * score_scale
        )
        grad_values = jnp.einsum(
            "gjqk,qgjd->kgd", chances_low, grad_groups, preferred_element_type=jnp.float32
        )
        grad_piece = jnp.concatenate(
            [
                grad_keys.reshape(key_block, key_heads * head_dim),
                grad_values.reshape(key_block, key_heads * head_dim),
            ],
            axis=-1,
        ).astype(jnp.bfloat16)
        grad_keyval = lax.dynamic_update_slice_in_dim(
            grad_keyval, grad_piece, number * key_block, 0
        )
        return (grad_query, grad_keyval)

    start_state = (
        jnp.zeros((key_heads, group_size, tokens, head_dim), jnp.float32),
        jnp.zeros(keyval_all.shape, jnp.bfloat16),
    )
    grad_query, grad_keyval = repeat(block_count, step_back, start_state)
    return (grad_query.transpose(2, 0, 1, 3).reshape(tokens, head_count, head_dim), grad_keyval)


def body(
    layer_input,
    segments,
    positions,
    attn_gain,
    w_q,
    b_q,
    w_k,
    b_k,
    w_v,
    b_v,
    w_o,
    mlp_gain,
    w_gate,
    w_up,
    w_down,
    cotangent,
):
    key_heads = w_k.shape[1] // HEAD_DIM
    head_count = w_q.shape[1] // HEAD_DIM
    width_q, width_k = w_q.shape[1], w_k.shape[1]
    tokens = layer_input.shape[1]
    ctx_size, fsdp_size = lax.axis_size("ctx"), lax.axis_size("fsdp")
    ctx_own = lax.axis_index("ctx")
    rows, hidden_count = w_gate.shape
    features = layer_input.shape[2]
    chunk = -(-hidden_count // (ctx_size * LANES)) * LANES
    width_qkv = width_q + 2 * width_k
    own = ctx_own.astype(jnp.int32)[None]

    attn_lined = direct_gather(jnp.concatenate([w_q, w_k, w_v, w_o.T], axis=1))

    if few():
        cuts = prepare(own, w_gate, w_up, w_down.T, ctx_size, chunk)
    else:
        tail = ((0, 0), (0, chunk * ctx_size - hidden_count))
        shards = [
            jnp.pad(shard, tail).reshape(rows, ctx_size, chunk) for shard in (w_gate, w_up, w_down.T)
        ]
        cuts = list(jnp.concatenate(shards, axis=-1).transpose(1, 0, 2))
    recut = untangle(trade(cuts)).reshape(ctx_size * rows, 3 * chunk)
    mlp_rows = lax.all_gather(recut, "fsdp", axis=0, tiled=True)

    def ordered(parts):
        pieces = untangle(parts)
        return pieces.transpose(1, 0, 2, 3).reshape(features, pieces.shape[-1])

    full_qkv = ordered(spread(attn_lined[..., :width_qkv]))
    o_pieces = spread(attn_lined[..., width_qkv:])

    inputs = layer_input[0].astype(jnp.float32)
    place = jnp.arange(tokens, dtype=jnp.int32)
    query_index = ctx_own * tokens + place
    grad_top = cotangent[0]
    cosines, sines = angles(positions[0], HEAD_DIM)
    scale_one = lax.rsqrt(jnp.mean(inputs * inputs, -1, keepdims=True) + EPS)
    unit_one = inputs * scale_one
    normed = (unit_one * attn_gain).astype(jnp.bfloat16)
    small_heads = few() and key_heads == 1 and tokens <= 256
    if small_heads:
        half = HEAD_DIM // 2
        cos_turned, sin_turned = cosines[:, 0, :half].T, sines[:, 0, :half].T
        query_flat, keyval = project(
            layer_input[0],
            attn_gain[None],
            full_qkv,
            jnp.concatenate([b_q, b_k, b_v])[None],
            cos_turned,
            sin_turned,
            segments,
            width_q,
            width_k,
        )
    else:
        projected = jnp.dot(normed, full_qkv, preferred_element_type=jnp.float32) + jnp.concatenate(
            [b_q, b_k, b_v]
        )
        queries = projected[:, :width_q]
        keyproj = projected[:, width_q : width_q + width_k]
        valproj = projected[:, width_q + width_k :]
        query_rot = rotate(queries.reshape(tokens, head_count, HEAD_DIM), cosines, sines).astype(
            jnp.bfloat16
        )
        key_rot = rotate(keyproj.reshape(tokens, key_heads, HEAD_DIM), cosines, sines).astype(
            jnp.bfloat16
        )
        keyval = jnp.concatenate(
            [key_rot.reshape(tokens, key_heads * HEAD_DIM), valproj.astype(jnp.bfloat16)], axis=-1
        )
    received = spread(keyval)
    full_o_turned = ordered(o_pieces)
    if small_heads:
        attended_low, attended_turned, log_total, start = attend_fwd(
            own, query_flat, segments, received
        )
    else:
        seg_own = segments[0]
        counts = jnp.stack([jnp.sum((seg_own <= number).astype(jnp.int32)) for number in range(2)])
        counts = lax.psum(counts, "ctx")
        start = jnp.where(seg_own == 0, 0, jnp.where(seg_own == 1, counts[0], counts[1]))
        order = untangle(received).reshape(ctx_size * tokens, 2 * width_k)
        attended, log_total = attend(query_rot, order, start, query_index, key_heads)
        attended_low = attended.astype(jnp.bfloat16)
    attended_low, grad_top_mine = lax.optimization_barrier(
        (attended_low, gather_half(after(grad_top, *received)))
    )
    branch_part = dot_rows(attended_low, full_o_turned).astype(jnp.bfloat16)
    middle = inputs + (
        branch_part.astype(jnp.float32) + swap_cores(branch_part).astype(jnp.float32)
    )
    scale_two = lax.rsqrt(jnp.mean(middle * middle, -1, keepdims=True) + EPS)
    unit_two = middle * scale_two
    normed_two = (unit_two * mlp_gain).astype(jnp.bfloat16)

    normed_mine = gather_half(normed_two)
    halves = [normed_mine, swap_cores(normed_mine)]
    tops = [grad_top_mine, swap_cores(grad_top_mine)]
    fsdp_own = lax.axis_index("fsdp").astype(jnp.int32)[None]

    gate_up, down_turned = mlp_rows[:, : 2 * chunk], mlp_rows[:, 2 * chunk :]
    normed_all, grad_top_all = jnp.concatenate(halves), jnp.concatenate(tops)
    if few():
        grad_one, grad_two, hidden, grad_both = mlp(halves, tops, mlp_rows, chunk)
    else:
        gate_upward = dot(normed_all, gate_up)
        grad_hidden = dot(grad_top_all, down_turned)
        gate_values, upward = gate_upward[:, :chunk], gate_upward[:, chunk:]
        sigmoid_gate = jax.nn.sigmoid(gate_values)
        swish_gate = gate_values * sigmoid_gate
        hidden = (swish_gate * upward).astype(jnp.bfloat16)
        slope = sigmoid_gate + swish_gate * (1.0 - sigmoid_gate)
        grad_both = jnp.concatenate(
            [grad_hidden * upward * slope, grad_hidden * swish_gate], axis=-1
        ).astype(jnp.bfloat16)
        grad_one, grad_two = jnp.split(dot_rows(grad_both, gate_up).astype(jnp.bfloat16), 2)
    grad_normed_sum = add_cores(grad_one, grad_two)
    grad_normed_parts = trade(jnp.split(grad_normed_sum, ctx_size))
    grad_both, grad_normed_sum = lax.optimization_barrier((grad_both, grad_normed_sum))
    mlp_grad = jnp.concatenate(
        [
            turned_dot(normed_all, grad_both).astype(jnp.bfloat16),
            turned_dot(grad_top_all, hidden).astype(jnp.bfloat16),
        ],
        axis=-1,
    ).reshape(fsdp_size, ctx_size * rows, 3 * chunk)
    mlp_mine = lax.psum_scatter(mlp_grad, "fsdp", scatter_dimension=0, tiled=False)
    branch_two_sum = add_cores(
        *jnp.split(dot_rows(after(hidden, grad_normed_sum), down_turned).astype(jnp.bfloat16), 2)
    )
    branch_two_sum, *grad_normed_parts = lax.optimization_barrier(
        (branch_two_sum, *grad_normed_parts)
    )
    grad_normed_two = join_tokens(grad_normed_parts)
    branch_two_parts = trade(jnp.split(branch_two_sum, ctx_size))

    grad_mlp_gain = jnp.sum(grad_normed_two * unit_two, 0)
    grad_unit_two = grad_normed_two * mlp_gain
    grad_middle = grad_top.astype(jnp.float32) + scale_two * (
        grad_unit_two - unit_two * jnp.mean(grad_unit_two * unit_two, -1, keepdims=True)
    )
    grad_branch = grad_middle.astype(jnp.bfloat16)
    def owners(left, right):
        if few():
            return weight_grad(own, left, right, ctx_size, fsdp_size)
        grad = turned_dot(left, right).astype(jnp.bfloat16)
        cut = grad.reshape(fsdp_size, ctx_size, rows, right.shape[1]).transpose(1, 0, 2, 3)
        return list(cut.reshape(ctx_size, fsdp_size * rows, right.shape[1]))

    o_parts = trade(owners(grad_branch, attended_low))
    if small_heads:
        grad_query, grad_keyvals = attend_bwd(
            own,
            query_flat,
            start,
            attended_turned,
            log_total,
            grad_branch,
            full_o_turned,
            cos_turned,
            sin_turned,
            received,
        )
    else:
        grad_attended = dot(grad_branch, full_o_turned).astype(jnp.bfloat16)
        grad_query_rot, grad_keyvals = attend_back(
            query_rot,
            order,
            start,
            query_index,
            key_heads,
            log_total,
            attended,
            grad_attended,
        )
        grad_keyvals = choose(grad_keyvals.reshape(ctx_size, tokens, 2 * width_k))
    grad_keyvals[0], branch_two_parts = lax.optimization_barrier(
        (grad_keyvals[0], branch_two_parts)
    )
    grad_keyvals[0], o_parts[1] = lax.optimization_barrier((grad_keyvals[0], o_parts[1]))
    keyval_parts = trade(grad_keyvals)
    keyval_parts[0], o_parts = lax.optimization_barrier((keyval_parts[0], o_parts))
    branch_two = join_tokens(branch_two_parts)
    result = (middle + branch_two).astype(jnp.bfloat16)

    if small_heads:
        grad_qkv, grad_normed_part = key_grads(
            grad_query, full_qkv, cos_turned, sin_turned, keyval_parts
        )
    else:
        grad_keyval = sum(part.astype(F32) for part in keyval_parts)
        grad_query = (
            rotate(grad_query_rot, cosines, -sines)
            .reshape(tokens, head_count * HEAD_DIM)
            .astype(jnp.bfloat16)
        )
        grad_key = (
            rotate(
                grad_keyval[:, : key_heads * HEAD_DIM].reshape(tokens, key_heads, HEAD_DIM),
                cosines,
                -sines,
            )
            .reshape(tokens, key_heads * HEAD_DIM)
            .astype(jnp.bfloat16)
        )
        grad_value = grad_keyval[:, key_heads * HEAD_DIM :].astype(jnp.bfloat16)
        grad_qkv = jnp.concatenate([grad_query, grad_key, grad_value], axis=-1)
        grad_normed_part = dot_rows(grad_qkv, full_qkv).astype(jnp.bfloat16)
    grad_normed_other = swap_cores(grad_normed_part)
    if few():
        grad_inputs, qkv_pieces = last_grads(
            own,
            layer_input[0],
            attn_gain[None],
            grad_qkv,
            grad_normed_part,
            grad_normed_other,
            grad_middle,
            grad_mlp_gain[None],
            ctx_size,
            fsdp_size,
        )
    else:
        grad_normed = grad_normed_part.astype(F32) + grad_normed_other.astype(F32)
        turned = grad_normed * unit_one
        along = jnp.mean(turned * attn_gain, -1, keepdims=True)
        grad_inputs = grad_middle + scale_one * (grad_normed * attn_gain - unit_one * along)
        grad_inputs = grad_inputs.astype(jnp.bfloat16)
        lines = [jnp.sum(grad_qkv.astype(F32), 0)]
        for gains in (jnp.sum(turned, 0), grad_mlp_gain):
            for half in (gains[:SPLIT], gains[SPLIT:]):
                lines.append(jnp.pad(half, (0, width_qkv - half.shape[0])))
        small = jnp.pad(jnp.stack(lines), ((0, SMALL_ROWS - len(lines)), (0, 0)))
        small = small.astype(jnp.bfloat16)
        qkv_pieces = [jnp.concatenate([part, small]) for part in owners(normed, grad_qkv)]
    qkv_parts = trade(qkv_pieces)
    o_sum = sum(part.astype(F32) for part in o_parts).astype(jnp.bfloat16)
    o_sum = o_sum.reshape(fsdp_size, rows, o_sum.shape[-1])
    o_lines = [
        lax.dynamic_index_in_dim(o_sum, (fsdp_own[0] + step) % fsdp_size, 0, keepdims=False)
        for step in range(fsdp_size)
    ]
    o_lines = o_lines[:1] + [send_up(o_lines[step], step) for step in range(1, fsdp_size)]
    mlp_mine = mlp_mine.reshape(ctx_size, rows, 3 * chunk)
    mlp_chosen = choose(mlp_mine)
    qkv_parts[0], o_lines, mlp_chosen = lax.optimization_barrier(
        (qkv_parts[0], o_lines, mlp_chosen)
    )
    if few():
        packed = pack(fsdp_own, qkv_parts, fsdp_size)
    else:
        qkv_sum = sum(part.astype(F32) for part in qkv_parts)
        small = qkv_sum[fsdp_size * rows :]
        both = qkv_sum[: fsdp_size * rows].reshape(fsdp_size, rows, width_qkv)
        packed = [
            jnp.concatenate([both[(fsdp_own[0] + step) % fsdp_size], small]).astype(jnp.bfloat16)
            for step in range(fsdp_size)
        ]
    packed = packed[:1] + [send_up(packed[step], step) for step in range(1, fsdp_size)]
    mlp_pieces = trade(mlp_chosen)
    if few():
        w_grads = unpack(packed, o_lines, features, width_q, width_k)
        mlp_grads = mlp_out(own, mlp_pieces, hidden_count)
    else:
        total = sum(part.astype(F32) for part in packed)
        tops = [0, width_q, width_q + width_k, width_qkv]
        w_grads = [total[:rows, tops[k] : tops[k + 1]] for k in range(3)]
        w_grads.append(sum(part.astype(F32) for part in o_lines))
        w_grads += [total[rows, tops[k] : tops[k + 1]] for k in range(3)]
        for row in (rows + 1, rows + 3):
            w_grads.append(
                jnp.concatenate([total[row, :SPLIT], total[row + 1, : features - SPLIT]])
            )
        mlp_grads = []
        for number in range(3):
            pieces = untangle(mlp_pieces)[..., number * chunk : (number + 1) * chunk]
            wide = pieces.transpose(1, 0, 2).reshape(rows, chunk * ctx_size)
            mlp_grads.append(wide[:, :hidden_count].astype(F32))
    grad_q, grad_k, grad_v, grad_o = w_grads[:4]
    grad_b_q, grad_b_k, grad_b_v, grad_attn_gain, grad_mlp_gain = [
        values.reshape(-1) for values in w_grads[4:]
    ]
    return (
        result[None],
        grad_inputs[None],
        grad_attn_gain,
        grad_q,
        grad_b_q,
        grad_k,
        grad_b_k,
        grad_v,
        grad_b_v,
        grad_o.T,
        grad_mlp_gain,
        mlp_grads[0],
        mlp_grads[1],
        mlp_grads[2].T,
    )


def solution(mesh):
    placed = (
        P("fsdp", "ctx", None),
        P("fsdp", "ctx"),
        P("fsdp", "ctx"),
        P(),
        P(("fsdp", "ctx"), "tp"),
        P("tp"),
        P(("fsdp", "ctx"), "tp"),
        P("tp"),
        P(("fsdp", "ctx"), "tp"),
        P("tp"),
        P("tp", ("fsdp", "ctx")),
        P(),
        P(("fsdp", "ctx"), "tp"),
        P(("fsdp", "ctx"), "tp"),
        P("tp", ("fsdp", "ctx")),
        P("fsdp", "ctx", None),
    )
    return jax.shard_map(
        body,
        mesh=mesh,
        in_specs=placed,
        out_specs=(
            P("fsdp", "ctx", None),
            P("fsdp", "ctx", None),
            P(),
            P(("fsdp", "ctx"), "tp"),
            P("tp"),
            P(("fsdp", "ctx"), "tp"),
            P("tp"),
            P(("fsdp", "ctx"), "tp"),
            P("tp"),
            P("tp", ("fsdp", "ctx")),
            P(),
            P(("fsdp", "ctx"), "tp"),
            P(("fsdp", "ctx"), "tp"),
            P("tp", ("fsdp", "ctx")),
        ),
        check_vma=False,
    )
```
